32 devices in a mesh: seq: 16 (over z, y, x), head: 2 (over core).
Axes of the slice: x: 2, y: 2, z: 4, core: 2. Of those that a mesh axis runs over, the one named last changes fastest.
Arguments:
- queries: bfloat16 [2048, 2048], P('seq', 'head'), may hold values from -8 to 8
- key_tokens: bfloat16 [2048, 2048], P('seq', 'head'), may hold values from -8 to 8
- value_tokens: bfloat16 [2048, 2048], P('seq', 'head'), may hold values from -6 to 6
- out_weight: bfloat16 [2048, 2048], P(None, 'head'), may hold values from -0.125 to 0.125
- output_grad: bfloat16 [2048, 2048], P('seq', 'head'), may hold values from -6 to 6
Outputs:
- output: bfloat16 [2048, 2048], P('seq', 'head')
- query_grad: bfloat16 [2048, 2048], P('seq', 'head')
- key_grad: bfloat16 [2048, 2048], P('seq', 'head')
- value_grad: bfloat16 [2048, 2048], P('seq', 'head')
The draws below stay inside these ranges and needn't reach their ends.
All inputs are finite; a program needn't handle non-finite values.
Results may differ from the reference program's by a relative error of at most 0.024.
Values may be sent and summed in bfloat16 or wider, within the bound.
No kernel may reach another device: no remote copies, remote signals or barrier semaphores. Data moves between devices by JAX's collectives and lax.ppermute only.
A program may use at most 128 MiB of HBM per device.

```python
import jax
import jax.numpy as jnp
from jax import lax

D = 2048
HEADS = 16
HDIM = 128
BLOCK = 128
TOK_DEV = 128
SLABS = 16
LEVELS = 4
TOKENS = 2048


def base_field(key):
    return jnp.clip(jax.random.normal(key, (TOKENS, D), jnp.float32), -6.0, 6.0)


def draw_queries(key, part):
    field = base_field(jax.random.fold_in(key, 11))
    return field.astype(jnp.bfloat16)


def draw_key_tokens(key, part):
    field = base_field(jax.random.fold_in(key, 23))
    return field.astype(jnp.bfloat16)


def block_scale(own_key, shape, pieces, smallest, high):
    def one(dim, blocks):
        draws = jax.random.uniform(jax.random.fold_in(jax.random.fold_in(own_key, 6), dim), (blocks,), jnp.float32, smallest / len(pieces), high / len(pieces))
        return jnp.repeat(jnp.exp(draws), shape[dim] // blocks).reshape((-1,) + (1,) * (len(shape) - dim - 1))

    loudness = one(*pieces[0])
    for cut in pieces[1:]:
        loudness = loudness * one(*cut)
    return loudness


def scatter_about(own_key, extent, deviation, bound, shards=(), kind=jnp.bfloat16):
    entries = deviation * jax.random.normal(own_key, extent, jnp.float32)
    if shards:
        entries = entries * block_scale(own_key, extent, shards, -0.22, 0.18)
    return jnp.clip(entries, -bound, bound).astype(kind)


def setup_inputs(seed: int = 0) -> dict:
    keys = jax.random.split(jax.random.key(seed), 6)
    queries = draw_queries(jax.random.fold_in(keys[5], 71), 0)
    key_tokens = draw_key_tokens(jax.random.fold_in(keys[5], 71), 0)
    value_tokens = scatter_about(keys[2], (TOKENS, D), 1.0, 6.0, ((0, 16), (1, 2)))
    out_weight = scatter_about(keys[3], (D, D), D ** -0.5, 0.125, ((1, 2),))
    output_grad = scatter_about(keys[4], (TOKENS, D), 1.0, 6.0, ((0, 16), (1, 2)))
    return {"queries": queries, "key_tokens": key_tokens, "value_tokens": value_tokens, "out_weight": out_weight, "output_grad": output_grad}


def coarsen(tokens, run_length, summed):
    grouped = tokens.astype(jnp.float32).reshape(-1, run_length, tokens.shape[1])
    if summed:
        reduced = jnp.sum(grouped, axis=1)
    else:
        reduced = jnp.mean(grouped, axis=1)
    return reduced.astype(jnp.bfloat16)


def reference(queries, key_tokens, value_tokens, out_weight, output_grad):
    run_lengths = [(TOK_DEV << level) // BLOCK for level in range(LEVELS)]
    coarse_keys = [coarsen(key_tokens, run_lengths[level], False) for level in range(LEVELS)]
    coarse_values = [coarsen(value_tokens, run_lengths[level], True) for level in range(LEVELS)]
    grad_attended = jnp.dot(output_grad, out_weight, preferred_element_type=jnp.float32).astype(jnp.bfloat16)
    inv_scale = 1.0 / float(HDIM) ** 0.5
    list_rows = TOK_DEV + LEVELS * BLOCK

    def slab_step(carry, slab):
        key_accum, value_accum = carry
        start = (slab * TOK_DEV).astype(jnp.int32)
        query_slab = lax.dynamic_slice_in_dim(queries, start, TOK_DEV, 0)
        key_parts = [lax.dynamic_slice_in_dim(key_tokens, start, TOK_DEV, 0)]
        value_parts = [lax.dynamic_slice_in_dim(value_tokens, start, TOK_DEV, 0)]
        grad_slab = lax.dynamic_slice_in_dim(grad_attended, start, TOK_DEV, 0)
        offsets = []
        for level in range(LEVELS):
            other = (((slab >> level) ^ 1) * BLOCK).astype(jnp.int32)
            offsets.append(other)
            key_parts.append(lax.dynamic_slice_in_dim(coarse_keys[level], other, BLOCK, 0))
            value_parts.append(lax.dynamic_slice_in_dim(coarse_values[level], other, BLOCK, 0))
        key_list = jnp.concatenate(key_parts, axis=0)
        value_list = jnp.concatenate(value_parts, axis=0)
        query_heads = query_slab.reshape(TOK_DEV, HEADS, HDIM).astype(jnp.float32)
        key_heads = key_list.reshape(list_rows, HEADS, HDIM).astype(jnp.float32)
        value_heads = value_list.reshape(list_rows, HEADS, HDIM).astype(jnp.float32)
        grad_heads = grad_slab.reshape(TOK_DEV, HEADS, HDIM).astype(jnp.float32)
        scores = jnp.einsum("thd,khd->htk", query_heads, key_heads) * inv_scale
        shifted = jnp.exp(scores - jnp.max(scores, axis=2, keepdims=True))
        probs = shifted / jnp.sum(shifted, axis=2, keepdims=True)
        probs_low = probs.astype(jnp.bfloat16).astype(jnp.float32)
        attended = jnp.einsum("htk,khd->thd", probs_low, value_heads).reshape(TOK_DEV, D).astype(jnp.bfloat16)
        prob_grad = jnp.einsum("thd,khd->htk", grad_heads, value_heads)
        centre = jnp.sum(probs * prob_grad, axis=2, keepdims=True)
        score_grad = (probs * (prob_grad - centre) * inv_scale).astype(jnp.bfloat16).astype(jnp.float32)
        query_grad = jnp.einsum("htk,khd->thd", score_grad, key_heads).reshape(TOK_DEV, D).astype(jnp.bfloat16)
        key_terms = jnp.einsum("htk,thd->khd", score_grad, query_heads).reshape(list_rows, D)
        value_terms = jnp.einsum("htk,thd->khd", probs_low, grad_heads).reshape(list_rows, D)
        new_keys = []
        new_values = []
        for level in range(LEVELS):
            first = TOK_DEV + level * BLOCK
            old_key = lax.dynamic_slice_in_dim(key_accum[level], offsets[level], BLOCK, 0)
            old_value = lax.dynamic_slice_in_dim(value_accum[level], offsets[level], BLOCK, 0)
            new_keys.append(lax.dynamic_update_slice_in_dim(key_accum[level], old_key + key_terms[first:first + BLOCK], offsets[level], 0))
            new_values.append(lax.dynamic_update_slice_in_dim(value_accum[level], old_value + value_terms[first:first + BLOCK], offsets[level], 0))
        return (new_keys, new_values), (attended, query_grad, key_terms[:TOK_DEV], value_terms[:TOK_DEV])

    start_keys = [jnp.zeros((TOKENS // run_lengths[level], D), jnp.float32) for level in range(LEVELS)]
    start_values = [jnp.zeros((TOKENS // run_lengths[level], D), jnp.float32) for level in range(LEVELS)]
    (key_accum, value_accum), stacked = lax.scan(slab_step, (start_keys, start_values), jnp.arange(SLABS, dtype=jnp.int32))
    attended = stacked[0].reshape(TOKENS, D)
    query_grad = stacked[1].reshape(TOKENS, D)
    key_sum = stacked[2].reshape(TOKENS, D)
    value_sum = stacked[3].reshape(TOKENS, D)
    for level in range(LEVELS):
        key_sum = key_sum + jnp.repeat(key_accum[level] / run_lengths[level], run_lengths[level], axis=0)
        value_sum = value_sum + jnp.repeat(value_accum[level], run_lengths[level], axis=0)
    output = jnp.dot(attended, out_weight.T, preferred_element_type=jnp.float32).astype(jnp.bfloat16)
    return output, query_grad, key_sum.astype(jnp.bfloat16), value_sum.astype(jnp.bfloat16)
```

```python
import math

import jax
import jax.numpy as jnp
from jax import lax
from jax.experimental import pallas as pl
from jax.experimental.pallas import tpu as pltpu
from jax.sharding import PartitionSpec as P

HDIM = 128
BLOCK = 128
BF16 = jnp.bfloat16
F32 = jnp.float32
VMEM = pl.BlockSpec(memory_space=pltpu.VMEM)
SMEM = pl.BlockSpec(memory_space=pltpu.SMEM)


def swap_seq(array, mask):
    return lax.ppermute(array, "seq", [(i, i ^ mask) for i in range(lax.axis_size("seq"))])


def swap_head(array):
    return lax.ppermute(array, "head", [(0, 1), (1, 0)])


def mm(left, right):
    return jnp.dot(left, right, preferred_element_type=F32)


def mm_cols(left, right):
    return lax.dot_general(left, right, (((1,), (1,)), ((), ())), preferred_element_type=F32)


def mm_rows(left, right):
    return lax.dot_general(left, right, (((0,), (0,)), ((), ())), preferred_element_type=F32)


def pool_matrix(rows, shift):
    shape = (rows, rows << shift)
    row = lax.broadcasted_iota(jnp.int32, shape, 0)
    col = lax.broadcasted_iota(jnp.int32, shape, 1)
    return jnp.where(lax.shift_right_logical(col, shift) == row, 1.0, 0.0).astype(BF16)


def call(kernel, out_shape, operands, scratch=(), flops=0, vmem=24, specs=None):
    moved = sum(x.size * x.dtype.itemsize for x in operands)
    return pl.pallas_call(
        kernel,
        out_shape=out_shape,
        in_specs=specs or [VMEM] * len(operands),
        out_specs=jax.tree.map(lambda _: VMEM, out_shape),
        scratch_shapes=list(scratch),
        compiler_params=pltpu.CompilerParams(vmem_limit_bytes=vmem << 20),
        cost_estimate=pl.CostEstimate(flops=flops, bytes_accessed=moved, transcendentals=0),
    )(*operands)


def coarse_kernel(levels, k_ref, v_ref, out_ref):
    for place, level in enumerate(levels):
        shape = (16, BLOCK)
        row = lax.broadcasted_iota(jnp.int32, shape, 0)
        col = lax.broadcasted_iota(jnp.int32, shape, 1)
        pool = jnp.where(lax.shift_right_logical(col, level) == row, 1.0, 0.0).astype(BF16)
        keys = mm(pool, k_ref[...]) * (1.0 / (1 << level))
        out_ref[32 * place : 32 * place + 16, :] = keys.astype(BF16)
        out_ref[32 * place + 16 : 32 * place + 32, :] = mm(pool, v_ref[...]).astype(BF16)


def pack_kernel(heads, at_ref, q_ref, k_ref, v_ref, mine_ref, other_ref, w_ref, far_ref, *refs):
    out_refs, grad_ref = refs[:heads], refs[heads]
    low, core = at_ref[0], at_ref[1]
    half = mine_ref.shape[1]
    tok = q_ref.shape[0]
    first = pl.multiple_of(core * half, half)
    second = pl.multiple_of((1 - core) * half, half)
    total = mm(mine_ref[...], w_ref[pl.ds(first, half), :])
    total += mm(other_ref[...], w_ref[pl.ds(second, half), :])
    grad_ref[...] = total.astype(BF16)
    for mask in range(heads):
        col = pl.ds(pl.multiple_of((low ^ mask) * HDIM, HDIM), HDIM)
        out = out_refs[mask]
        out[0:tok, :] = q_ref[:, col]
        out[tok : 2 * tok, :] = k_ref[:, col]
        out[2 * tok : 3 * tok, :] = v_ref[:, col]
        out[3 * tok : 4 * tok, :] = grad_ref[:, col]
        out[4 * tok :, :] = far_ref[:, col]


def attend_kernel(heads, local_levels, far_levels, *refs):
    in_refs, out_refs = refs[:heads], refs[heads : 2 * heads]
    kl_ref, vl_ref, q_all, g_all, dk_ref, dv_ref, ck_ref, cv_ref, fk_ref, fv_ref = refs[2 * heads :]
    tok = BLOCK
    pairs = heads // 2
    inv_scale = 1.0 / math.sqrt(HDIM)
    to_exp2 = inv_scale * math.log2(math.e)
    for slab in range(heads):
        pair, row = slab // 2, (slab % 2) * tok
        q_all[pair, row : row + tok, :] = in_refs[slab][0:tok, :]
        kl_ref[pair, row : row + tok, :] = in_refs[slab][tok : 2 * tok, :]
        vl_ref[pair, row : row + tok, :] = in_refs[slab][2 * tok : 3 * tok, :]
        g_all[pair, row : row + tok, :] = in_refs[slab][3 * tok : 4 * tok, :]
        for place in range(far_levels):
            at = 4 * tok + 32 * place
            spot = 2 * tok + (local_levels - 1 + place) * BLOCK + 16 * slab
            fk, fv = in_refs[slab][at : at + 16, :], in_refs[slab][at + 16 : at + 32, :]
            for each in range(pairs):
                kl_ref[each, spot : spot + 16, :] = fk
                vl_ref[each, spot : spot + 16, :] = fv
    for level in range(1, local_levels):
        spot = 2 * tok + (level - 1) * BLOCK
        part = BLOCK >> level
        pool = pool_matrix(2 * part, level)
        for pair in range(pairs):
            keys = (mm(pool, kl_ref[pair, 0 : 2 * tok, :]) * (1.0 / (1 << level))).astype(BF16)
            values = mm(pool, vl_ref[pair, 0 : 2 * tok, :]).astype(BF16)
            group = pair >> (level - 1)
            inside = (pair & ((1 << (level - 1)) - 1)) * 2 * part
            at = spot + inside
            for each in range(pairs):
                if each >> (level - 1) == group ^ 1:
                    kl_ref[each, at : at + 2 * part, :] = keys
                    vl_ref[each, at : at + 2 * part, :] = values
    for pair in range(pairs):
        queries, grads = q_all[pair], g_all[pair]
        keys, values = kl_ref[pair], vl_ref[pair]
        scores = mm_cols(queries, keys)
        prob_grad = mm_cols(grads, values)
        top = jnp.max(scores, axis=1, keepdims=True)
        raised = jnp.exp2((scores - top) * to_exp2)
        inverse = 1.0 / jnp.sum(raised, axis=1, keepdims=True)
        prob = raised * inverse
        centre = jnp.sum(prob * prob_grad, axis=1, keepdims=True)
        prob_low = prob.astype(BF16)
        score_grad = (prob * ((prob_grad - centre) * inv_scale)).astype(BF16)
        attended = mm(prob_low, values).astype(BF16)
        query_grad = mm(score_grad, keys).astype(BF16)
        for side in range(2):
            rows = slice(side * tok, side * tok + tok)
            out_refs[2 * pair + side][0:tok, :] = attended[rows]
            out_refs[2 * pair + side][tok : 2 * tok, :] = query_grad[rows]
        key_terms = mm_rows(score_grad, queries)
        value_terms = mm_rows(prob_low, grads)
        dk_ref[pair] = key_terms[0 : 2 * tok]
        dv_ref[pair] = value_terms[0 : 2 * tok]
        for level in range(1, local_levels):
            group = (pair >> (level - 1)) ^ 1
            rows = slice(2 * tok + (level - 1) * BLOCK, 2 * tok + level * BLOCK)
            slot = (level - 1) * pairs + group
            if pair & ((1 << (level - 1)) - 1) == 0:
                ck_ref[slot] = key_terms[rows]
                cv_ref[slot] = value_terms[rows]
            else:
                ck_ref[slot] += key_terms[rows]
                cv_ref[slot] += value_terms[rows]
        for place in range(far_levels):
            start = 2 * tok + (local_levels - 1 + place) * BLOCK
            rows = slice(start, start + BLOCK)
            if pair == 0:
                fk_ref[place] = key_terms[rows]
                fv_ref[place] = value_terms[rows]
            else:
                fk_ref[place] += key_terms[rows]
                fv_ref[place] += value_terms[rows]
    for pair in range(pairs):
        key_sum, value_sum = dk_ref[pair], dv_ref[pair]
        for level in range(1, local_levels):
            part = BLOCK >> level
            pool = pool_matrix(2 * part, level)
            slot = (level - 1) * pairs + (pair >> (level - 1))
            inside = (pair & ((1 << (level - 1)) - 1)) * 2 * part
            rows = slice(inside, inside + 2 * part)
            key_sum += mm_rows(pool, (ck_ref[slot, rows, :] * (1.0 / (1 << level))).astype(BF16))
            value_sum += mm_rows(pool, cv_ref[slot, rows, :].astype(BF16))
        for side in range(2):
            rows = slice(side * tok, side * tok + tok)
            out_refs[2 * pair + side][2 * tok : 3 * tok, :] = key_sum[rows].astype(BF16)
            out_refs[2 * pair + side][3 * tok : 4 * tok, :] = value_sum[rows].astype(BF16)
    for slab in range(heads):
        for place in range(far_levels):
            at = 4 * tok + 32 * place
            rows = slice(16 * slab, 16 * slab + 16)
            out_refs[slab][at : at + 16, :] = fk_ref[place, rows, :].astype(BF16)
            out_refs[slab][at + 16 : at + 32, :] = fv_ref[place, rows, :].astype(BF16)


def unpack_kernel(heads, at_ref, w_ref, *refs):
    in_refs = refs[:heads]
    keep_ref, send_ref, dq_ref, dk_ref, dv_ref, far_ref, att_ref = refs[heads:]
    low, core = at_ref[0], at_ref[1]
    tok, half = dq_ref.shape
    for mask in range(heads):
        col = pl.ds(pl.multiple_of((low ^ mask) * HDIM, HDIM), HDIM)
        chunk = in_refs[mask]
        att_ref[:, col] = chunk[0:tok, :]
        dq_ref[:, col] = chunk[tok : 2 * tok, :]
        dk_ref[:, col] = chunk[2 * tok : 3 * tok, :]
        dv_ref[:, col] = chunk[3 * tok : 4 * tok, :]
        far_ref[:, col] = chunk[4 * tok :, :]
    first = pl.multiple_of(core * half, half)
    second = pl.multiple_of((1 - core) * half, half)
    send_ref[...] = mm_cols(att_ref[...], w_ref[pl.ds(second, half), :]).astype(BF16)
    keep_ref[...] = mm_cols(att_ref[...], w_ref[pl.ds(first, half), :])


def finish_kernel(levels, keep_ref, got_ref, dk_ref, dv_ref, far_ref, out_ref, key_ref, value_ref):
    out_ref[...] = (keep_ref[...] + got_ref[...].astype(F32)).astype(BF16)
    key_sum, value_sum = dk_ref[...].astype(F32), dv_ref[...].astype(F32)
    for place, level in enumerate(levels):
        shape = (16, BLOCK)
        row = lax.broadcasted_iota(jnp.int32, shape, 0)
        col = lax.broadcasted_iota(jnp.int32, shape, 1)
        pool = jnp.where(lax.shift_right_logical(col, level) == row, 1.0, 0.0).astype(BF16)
        at = 32 * place
        key_sum += mm_rows(pool, far_ref[at : at + 16, :]) * (1.0 / (1 << level))
        value_sum += mm_rows(pool, far_ref[at + 16 : at + 32, :])
    key_ref[...] = key_sum.astype(BF16)
    value_ref[...] = value_sum.astype(BF16)


def gather_far(pieces, levels, columns):
    held = {}
    for place, level in enumerate(levels):
        rows = BLOCK >> level
        block = pieces[32 * place : 32 * place + 32].reshape(2, 16, columns)
        held[level] = block[:, None, :rows]
    found = []
    for step in levels:
        sent = [held[level].reshape(-1, columns) for level in levels if level >= step]
        got = swap_seq(jnp.concatenate(sent, axis=0) if len(sent) > 1 else sent[0], 1 << step)
        first = 0
        for level in levels:
            if level < step:
                continue
            count = held[level].size // columns
            part = got[first : first + count].reshape(held[level].shape)
            first += count
            if level == step:
                found.append(part.reshape(32, columns))
            else:
                held[level] = jnp.concatenate([held[level], part], axis=1)
    return jnp.concatenate(found, axis=0) if len(found) > 1 else found[0]


def scatter_far(packed, levels, columns):
    blocks = {}
    for place, level in enumerate(levels):
        rows = BLOCK >> level
        block = packed[32 * place : 32 * place + 32]
        blocks[level] = block.reshape(2, 16 // rows, rows, columns)
    ready = {}
    for step in reversed(levels):
        sent, kept = [blocks[step].reshape(-1, columns)], {}
        for level in levels:
            if level > step:
                size = ready[level].shape[1] // 2
                kept[level] = ready[level][:, :size]
                sent.append(ready[level][:, size:].astype(BF16).reshape(-1, columns))
        got = swap_seq(jnp.concatenate(sent, axis=0) if len(sent) > 1 else sent[0], 1 << step)
        ready[step] = got[0 : blocks[step].size // columns].reshape(blocks[step].shape)
        first = blocks[step].size // columns
        for level in kept:
            count = kept[level].size // columns
            part = got[first : first + count].reshape(kept[level].shape)
            first += count
            ready[level] = kept[level].astype(F32) + part.astype(F32)
    shares = []
    for level in levels:
        share = ready[level].astype(BF16).reshape(2, -1, columns)
        pad = 16 - share.shape[1]
        if pad:
            share = jnp.pad(share, ((0, 0), (0, pad), (0, 0)))
        shares.append(share.reshape(32, columns))
    return jnp.concatenate(shares, axis=0) if len(shares) > 1 else shares[0]


def on_device(queries, key_tokens, value_tokens, out_weight, output_grad):
    tok, columns = queries.shape
    heads = columns // HDIM
    local_levels = heads.bit_length() - 1
    level_count = lax.axis_size("seq").bit_length() - 1
    far = list(range(local_levels, level_count))
    rows = 4 * tok + 32 * len(far)
    place = jnp.stack([lax.axis_index("seq") & (heads - 1), lax.axis_index("head")])
    place = place.astype(jnp.int32)

    def shape(dims, dtype=BF16):
        return jax.ShapeDtypeStruct(dims, dtype)

    other_grad = swap_head(output_grad)
    pieces = call(
        lambda *refs: coarse_kernel(far, *refs),
        shape((32 * len(far), columns)),
        (key_tokens, value_tokens),
    )
    far_rows = gather_far(pieces, far, columns)
    chunks = call(
        lambda *refs: pack_kernel(heads, *refs),
        [shape((rows, HDIM))] * heads,
        (place, queries, key_tokens, value_tokens, output_grad, other_grad, out_weight, far_rows),
        scratch=[pltpu.VMEM((tok, columns), BF16)],
        flops=4 * tok * columns * columns,
        specs=[SMEM] + [VMEM] * 7,
    )
    mine = [chunks[0]] + [swap_seq(chunks[mask], mask) for mask in range(1, heads)]
    list_rows = 2 * tok + (local_levels - 1 + len(far)) * BLOCK
    pairs = heads // 2
    back = call(
        lambda *refs: attend_kernel(heads, local_levels, len(far), *refs),
        [shape((rows, HDIM))] * heads,
        mine,
        scratch=[
            pltpu.VMEM((pairs, list_rows, HDIM), BF16),
            pltpu.VMEM((pairs, list_rows, HDIM), BF16),
            pltpu.VMEM((pairs, 2 * tok, HDIM), BF16),
            pltpu.VMEM((pairs, 2 * tok, HDIM), BF16),
            pltpu.VMEM((pairs, 2 * tok, HDIM), F32),
            pltpu.VMEM((pairs, 2 * tok, HDIM), F32),
            pltpu.VMEM(((local_levels - 1) * pairs, BLOCK, HDIM), F32),
            pltpu.VMEM(((local_levels - 1) * pairs, BLOCK, HDIM), F32),
            pltpu.VMEM((len(far), BLOCK, HDIM), F32),
            pltpu.VMEM((len(far), BLOCK, HDIM), F32),
        ],
        flops=12 * heads * tok * list_rows * HDIM,
    )
    home = [back[0]] + [swap_seq(back[mask], mask) for mask in range(1, heads)]
    wide = shape((tok, columns))
    keep, send, query_grad, key_part, value_part, far_part = call(
        lambda *refs: unpack_kernel(heads, *refs),
        [shape((tok, columns), F32), wide, wide, wide, wide, shape((32 * len(far), columns))],
        [place, out_weight] + home,
        scratch=[pltpu.VMEM((tok, columns), BF16)],
        flops=4 * tok * columns * columns,
        specs=[SMEM] + [VMEM] * (1 + heads),
    )
    got = swap_head(send)
    far_share = scatter_far(far_part, far, columns)
    output, key_grad, value_grad = call(
        lambda *refs: finish_kernel(far, *refs),
        [wide, wide, wide],
        (keep, got, key_part, value_part, far_share),
    )
    return output, query_grad, key_grad, value_grad


def solution(mesh):
    placed = P("seq", "head")
    return jax.shard_map(
        on_device,
        mesh=mesh,
        in_specs=(placed, placed, placed, P(None, "head"), placed),
        out_specs=(placed, placed, placed, placed),
        check_vma=False,
    )
```

```python
import math

import jax
import jax.numpy as jnp
from jax import lax
from jax.experimental import pallas as pl
from jax.experimental.pallas import tpu as pltpu
from jax.sharding import PartitionSpec as P

HDIM = 128
BLOCK = 128
BF16 = jnp.bfloat16
F32 = jnp.float32
VMEM = pl.BlockSpec(memory_space=pltpu.VMEM)
SMEM = pl.BlockSpec(memory_space=pltpu.SMEM)
HBM = pl.BlockSpec(memory_space=pltpu.HBM)


def swap_seq(array, mask):
    return lax.ppermute(array, "seq", [(i, i ^ mask) for i in range(lax.axis_size("seq"))])


def swap_head(array):
    return lax.ppermute(array, "head", [(0, 1), (1, 0)])


def mm(left, right):
    return jnp.dot(left, right, preferred_element_type=F32)


def mm_cols(left, right):
    return lax.dot_general(left, right, (((1,), (1,)), ((), ())), preferred_element_type=F32)


def mm_rows(left, right):
    return lax.dot_general(left, right, (((0,), (0,)), ((), ())), preferred_element_type=F32)


def pool_matrix(rows, shift):
    shape = (rows, rows << shift)
    row = lax.broadcasted_iota(jnp.int32, shape, 0)
    col = lax.broadcasted_iota(jnp.int32, shape, 1)
    return jnp.where(lax.shift_right_logical(col, shift) == row, 1.0, 0.0).astype(BF16)


def call(kernel, out_shape, operands, scratch=(), flops=0, vmem=24, specs=None, free=False, outs=VMEM):
    specs = specs or [VMEM] * len(operands)
    operands = [
        pltpu.with_memory_space_constraint(x, pltpu.HBM) if spec is HBM else x
        for x, spec in zip(operands, specs)
    ]
    moved = 0 if free else sum(x.size * x.dtype.itemsize for x in operands)
    return pl.pallas_call(
        kernel,
        out_shape=out_shape,
        in_specs=specs,
        out_specs=jax.tree.map(lambda _: outs, out_shape),
        scratch_shapes=list(scratch),
        compiler_params=pltpu.CompilerParams(vmem_limit_bytes=vmem << 20),
        cost_estimate=pl.CostEstimate(flops=flops, bytes_accessed=moved, transcendentals=0),
    )(*operands)


def level_pool(rows, level):
    row = lax.broadcasted_iota(jnp.int32, (rows, BLOCK), 0)
    col = lax.broadcasted_iota(jnp.int32, (rows, BLOCK), 1)
    return jnp.where(lax.shift_right_logical(col, level) == row, 1.0, 0.0).astype(BF16)


def col_block(low, mask, width):
    return pl.ds(pl.multiple_of((low ^ mask) * width, width), width)


def piece_rows(level):
    return max(16, BLOCK >> level)


def split_kernel(slots, at_ref, q_hbm, k_hbm, v_hbm, *refs):
    chunk_refs, sems = refs[:slots], refs[slots]
    low = at_ref[0]
    tok, width = BLOCK, chunk_refs[0].shape[1]
    copies = []
    for place, source in enumerate((q_hbm, k_hbm, v_hbm)):
        for mask in range(slots):
            copy = pltpu.make_async_copy(
                source.at[:, col_block(low, mask, width)],
                chunk_refs[mask].at[pl.ds(place * tok, tok), :],
                sems.at[place * slots + mask],
            )
            copy.start()
            copies.append(copy)
    for copy in copies:
        copy.wait()


def coarse_kernel(levels, k_hbm, v_hbm, *refs):
    piece_refs, (k_ref, v_ref, sems) = refs[: len(levels)], refs[len(levels) :]
    copies = [
        pltpu.make_async_copy(k_hbm, k_ref, sems.at[0]),
        pltpu.make_async_copy(v_hbm, v_ref, sems.at[1]),
    ]
    for copy in copies:
        copy.start()
    for copy in copies:
        copy.wait()
    for level, piece in zip(levels, piece_refs):
        rows = piece_rows(level)
        pool = level_pool(rows, level)
        piece[0:rows, :] = (mm(pool, k_ref[...]) * (1.0 / (1 << level))).astype(BF16)
        piece[rows:, :] = mm(pool, v_ref[...]).astype(BF16)


def grad_kernel(at_ref, mine_ref, w_ref, other_ref, out_ref):
    core = at_ref[1]
    half = mine_ref.shape[1]
    first = pl.multiple_of(core * half, half)
    second = pl.multiple_of((1 - core) * half, half)
    total = mm(mine_ref[...], w_ref[pl.ds(first, half), :])
    total += mm(other_ref[...], w_ref[pl.ds(second, half), :])
    out_ref[...] = total.astype(BF16)


def second_kernel(slots, entries, at_ref, grad_ref, *refs):
    far_refs, out_refs = refs[: len(entries)], refs[len(entries) :]
    low = at_ref[0]
    tok, width = BLOCK, out_refs[0].shape[1]
    for mask in range(slots):
        cols = col_block(low, mask, width)
        out_refs[mask][0:tok, :] = grad_ref[:, cols]
        for (place, part, rows), far_ref in zip(entries, far_refs):
            for kind in range(2):
                at = tok + 64 * place + 32 * kind + part * rows
                source = far_ref[kind * rows : kind * rows + rows, cols]
                out_refs[mask][at : at + rows, :] = source


def attend_kernel(slots, far_levels, entries, *refs):
    first_refs, second_refs = refs[:slots], refs[slots : 2 * slots]
    far_refs, refs = refs[2 * slots : 2 * slots + len(entries)], refs[2 * slots + len(entries) :]
    dk_ref, dv_ref, kl_ref, vl_ref, prob_ref, grad_ref = refs[:6]
    q_all, g_all, ck_ref, cv_ref, fk_ref, fv_ref = refs[6:]
    tok = BLOCK
    pairs = slots // 2
    inv_scale = 1.0 / math.sqrt(HDIM)
    to_exp2 = inv_scale * math.log2(math.e)
    near, far = 2 * tok, 3 * tok
    for slab in range(slots):
        pair, row = slab // 2, (slab % 2) * tok
        q_all[pair, row : row + tok, :] = first_refs[slab][0:tok, :]
        kl_ref[pair, row : row + tok, :] = first_refs[slab][tok : 2 * tok, :]
        vl_ref[pair, row : row + tok, :] = first_refs[slab][2 * tok : 3 * tok, :]
        g_all[pair, row : row + tok, :] = second_refs[slab][0:tok, :]
        for place in range(far_levels):
            at = tok + 64 * place
            spot = far + place * BLOCK + 32 * slab
            for each in range(pairs):
                kl_ref[each, spot : spot + 32, :] = second_refs[slab][at : at + 32, :]
                vl_ref[each, spot : spot + 32, :] = second_refs[slab][at + 32 : at + 64, :]
    pool = pool_matrix(BLOCK, 1)
    for pair in range(pairs):
        kl_ref[pair ^ 1, near:far, :] = (mm(pool, kl_ref[pair, 0:near, :]) * 0.5).astype(BF16)
        vl_ref[pair ^ 1, near:far, :] = mm(pool, vl_ref[pair, 0:near, :]).astype(BF16)
    for pair in range(pairs):
        for head in range(2):
            lanes = slice(head * HDIM, head * HDIM + HDIM)
            queries, grads = q_all[pair, :, lanes], g_all[pair, :, lanes]
            keys, values = kl_ref[pair, :, lanes], vl_ref[pair, :, lanes]
            scores = mm_cols(queries, keys)
            prob_grad = mm_cols(grads, values)
            top = jnp.max(scores, axis=1, keepdims=True)
            raised = jnp.exp2((scores - top) * to_exp2)
            inverse = 1.0 / jnp.sum(raised, axis=1, keepdims=True)
            prob = raised * inverse
            centre = jnp.sum(prob * prob_grad, axis=1, keepdims=True)
            prob_low = prob.astype(BF16)
            score_grad = (prob * ((prob_grad - centre) * inv_scale)).astype(BF16)
            prob_ref[2 * pair + head] = prob_low
            grad_ref[2 * pair + head] = score_grad
            key_terms = mm_rows(score_grad, queries)
            value_terms = mm_rows(prob_low, grads)
            for terms, local, level1, distant in (
                (key_terms, dk_ref, ck_ref, fk_ref),
                (value_terms, dv_ref, cv_ref, fv_ref),
            ):
                local[pair * near : pair * near + near, lanes] = terms[0:near]
                level1[pair ^ 1, :, lanes] = terms[near:far].astype(BF16)
                if pair == 0:
                    distant[:, lanes] = terms[far:]
                else:
                    distant[:, lanes] += terms[far:]
    for pair in range(pairs):
        rows = slice(pair * near, pair * near + near)
        dk_ref[rows, :] += mm_rows(pool, ck_ref[pair]) * 0.5
        dv_ref[rows, :] += mm_rows(pool, cv_ref[pair])
    for (place, part, count), out_ref in zip(entries, far_refs):
        for kind, total in enumerate((fk_ref, fv_ref)):
            for slab in range(slots):
                start = place * BLOCK + 32 * slab + part * count
                at = (kind * slots + slab) * count
                out_ref[at : at + count, :] = total[start : start + count, :].astype(BF16)


def reduce_kernel(slots, kl_ref, vl_ref, prob_ref, grad_ref, *refs):
    home_refs, query_refs = refs[:slots], refs[slots:]
    tok = BLOCK
    for pair in range(slots // 2):
        for head in range(2):
            lanes = slice(head * HDIM, head * HDIM + HDIM)
            attended = mm(prob_ref[2 * pair + head], vl_ref[pair, :, lanes]).astype(BF16)
            query_grad = mm(grad_ref[2 * pair + head], kl_ref[pair, :, lanes]).astype(BF16)
            for side in range(2):
                rows = slice(side * tok, side * tok + tok)
                home_refs[2 * pair + side][0:tok, lanes] = attended[rows]
                query_refs[2 * pair + side][:, lanes] = query_grad[rows]


def merge_kernel(slots, levels, dk_ref, dv_ref, *refs):
    query_refs, refs = refs[:slots], refs[slots:]
    far_refs, out_refs = refs[: len(levels)], refs[len(levels) :]
    tok = BLOCK
    for slab in range(slots):
        rows = slice(slab * tok, slab * tok + tok)
        key_sum, value_sum = dk_ref[rows, :], dv_ref[rows, :]
        for level, far_ref in zip(levels, far_refs):
            count = piece_rows(level)
            pool = level_pool(count, level)
            mine = far_ref[slab * count : slab * count + count, :]
            key_sum += mm_rows(pool, mine) * (1.0 / (1 << level))
            at = (slots + slab) * count
            value_sum += mm_rows(pool, far_ref[at : at + count, :])
        out_refs[slab][0:tok, :] = query_refs[slab][...]
        out_refs[slab][tok : 2 * tok, :] = key_sum.astype(BF16)
        out_refs[slab][2 * tok :, :] = value_sum.astype(BF16)


def collect_kernel(slots, at_ref, *refs):
    in_refs, att_ref = refs[:slots], refs[slots]
    low = at_ref[0]
    tok, width = BLOCK, in_refs[0].shape[1]
    for mask in range(slots):
        att_ref[:, col_block(low, mask, width)] = in_refs[mask][0:tok, :]


def project_kernel(at_ref, att_ref, w_ref, keep_ref, *send_refs):
    core = at_ref[1]
    half = att_ref.shape[1]
    part = half // 2
    for place in range(2):
        other = pl.multiple_of((1 - core) * half + place * part, part)
        send = mm_cols(att_ref[...], w_ref[pl.ds(other, part), :])
        send_refs[place][...] = send.astype(BF16)
    first = pl.multiple_of(core * half, half)
    keep_ref[...] = mm_cols(att_ref[...], w_ref[pl.ds(first, half), :])


def add_kernel(keep_ref, left_ref, right_ref, out_ref):
    part = left_ref.shape[1]
    for place, got_ref in enumerate((left_ref, right_ref)):
        cols = slice(place * part, place * part + part)
        out_ref[:, cols] = (keep_ref[:, cols] + got_ref[...].astype(F32)).astype(BF16)


def place_kernel(slots, blocks, at_ref, *refs):
    in_refs, out_refs, sems = refs[:slots], refs[slots:-1], refs[-1]
    low = at_ref[0]
    tok, width = BLOCK, in_refs[0].shape[1]
    copies = []
    for place, block in enumerate(blocks):
        for mask in range(slots):
            copy = pltpu.make_async_copy(
                in_refs[mask].at[pl.ds(block * tok, tok), :],
                out_refs[place].at[:, col_block(low, mask, width)],
                sems.at[place * slots + mask],
            )
            copy.start()
            copies.append(copy)
    for copy in copies:
        copy.wait()


def straight(levels, slots):
    return all((slots << place) * 4 <= 32 for place in range(len(levels)))


def far_entries(levels, slots):
    entries, masks = [], []
    for place, level in enumerate(levels):
        if not straight(levels, slots):
            entries.append((place, 0, 32))
            continue
        for part in range(1 << place):
            entries.append((place, part, BLOCK >> level))
            masks.append(1 << level ^ part * slots)
    return entries, masks


def gather_far(pieces, levels, slots):
    columns = pieces[0].shape[1]
    if straight(levels, slots):
        entries, masks = far_entries(levels, slots)
        return [swap_seq(pieces[entry[0]], mask) for entry, mask in zip(entries, masks)]
    held = {}
    for place, level in enumerate(levels):
        block = pieces[place].reshape(2, piece_rows(level), columns)
        held[level] = block[:, None, : BLOCK >> level]
    found = []
    for step in levels:
        sent = [held[level].reshape(-1, columns) for level in levels if level >= step]
        got = swap_seq(jnp.concatenate(sent, axis=0), 1 << step)
        first = 0
        for level in levels:
            if level < step:
                continue
            count = held[level].size // columns
            part = got[first : first + count].reshape(held[level].shape)
            first += count
            if level == step:
                found.append(part.reshape(64, columns))
            else:
                held[level] = jnp.concatenate([held[level], part], axis=1)
    return found


def scatter_far(packed, levels, slots):
    width = packed[0].shape[1]
    if straight(levels, slots):
        entries, masks = far_entries(levels, slots)
        shares = [swap_seq(array, mask) for array, mask in zip(packed, masks)]
        return shares, [levels[entry[0]] for entry in entries]
    blocks = {}
    for place, level in enumerate(levels):
        rows = BLOCK >> level
        blocks[level] = packed[place].reshape(2 * slots, 32 // rows, rows, width)
    ready = {}
    for step in reversed(levels):
        sent, kept = [blocks[step].reshape(-1, width)], {}
        for level in levels:
            if level > step:
                size = ready[level].shape[1] // 2
                kept[level] = ready[level][:, :size]
                sent.append(ready[level][:, size:].astype(BF16).reshape(-1, width))
        got = swap_seq(jnp.concatenate(sent, axis=0), 1 << step)
        first = blocks[step].size // width
        ready[step] = got[0:first].reshape(blocks[step].shape)
        for level in kept:
            count = kept[level].size // width
            part = got[first : first + count].reshape(kept[level].shape)
            first += count
            ready[level] = kept[level].astype(F32) + part.astype(F32)
    shares = []
    for level in levels:
        share = ready[level].astype(BF16).reshape(2 * slots, -1, width)
        pad = piece_rows(level) - share.shape[1]
        if pad:
            share = jnp.pad(share, ((0, 0), (0, pad), (0, 0)))
        shares.append(share.reshape(-1, width))
    return shares, list(levels)


def on_device(queries, key_tokens, value_tokens, out_weight, output_grad):
    tok, columns = queries.shape
    heads = columns // HDIM
    slots = heads // 2
    width = columns // slots
    local_levels = slots.bit_length() - 1
    level_count = lax.axis_size("seq").bit_length() - 1
    far = list(range(local_levels, level_count))
    far_rows = 64 * len(far)
    list_rows = 3 * tok + BLOCK * len(far)
    entries, _ = far_entries(far, slots)
    place = jnp.stack([lax.axis_index("seq") & (slots - 1), lax.axis_index("head")])
    place = place.astype(jnp.int32)

    def shape(dims, dtype=BF16):
        return jax.ShapeDtypeStruct(dims, dtype)

    def over(rows):
        return [shape((rows, width))] * slots

    def exchange(chunks):
        got = {0: chunks[0]}
        for mask in sorted(range(1, slots), key=lambda mask: (mask + 1) % 2):
            got[mask] = swap_seq(chunks[mask], mask)
        return [got[mask] for mask in range(slots)]

    other_grad = swap_head(output_grad)
    pieces = call(
        lambda *refs: coarse_kernel(far, *refs),
        [shape((2 * piece_rows(level), columns)) for level in far],
        (key_tokens, value_tokens),
        scratch=[pltpu.VMEM((tok, columns), BF16)] * 2 + [pltpu.SemaphoreType.DMA((2,))],
        specs=[HBM] * 2,
        vmem=8,
    )
    pieces, later, other_grad = lax.optimization_barrier((pieces, place, other_grad))
    far_got = gather_far(pieces, far, slots)
    chunks = call(
        lambda *refs: split_kernel(slots, *refs),
        over(3 * tok),
        (later, queries, key_tokens, value_tokens),
        scratch=[pltpu.SemaphoreType.DMA((3 * slots,))],
        flops=6 * 10**9,
        specs=[SMEM] + [HBM] * 3,
        vmem=8,
    )
    first = exchange(chunks)
    grads = call(
        grad_kernel,
        shape((tok, columns)),
        [place, output_grad, out_weight, other_grad],
        flops=4 * tok * columns * columns,
        specs=[SMEM] + [VMEM] * 3,
        vmem=16,
    )
    chunks = call(
        lambda *refs: second_kernel(slots, entries, *refs),
        over(tok + far_rows),
        [place, grads] + far_got,
        specs=[SMEM] + [VMEM] * (1 + len(far_got)),
        vmem=8,
    )
    second = exchange(chunks)
    pairs = slots // 2
    lists = [shape((pairs, list_rows, width))] * 2
    made = call(
        lambda *refs: attend_kernel(slots, len(far), entries, *refs),
        [shape((2 * slots * rows, width)) for _, _, rows in entries]
        + [shape((slots * tok, width), F32)] * 2
        + lists
        + [shape((slots, 2 * tok, list_rows))] * 2,
        first + second,
        scratch=[
            pltpu.VMEM((pairs, 2 * tok, width), BF16),
            pltpu.VMEM((pairs, 2 * tok, width), BF16),
            pltpu.VMEM((pairs, BLOCK, width), BF16),
            pltpu.VMEM((pairs, BLOCK, width), BF16),
            pltpu.VMEM((BLOCK * len(far), width), F32),
            pltpu.VMEM((BLOCK * len(far), width), F32),
        ],
        flops=8 * heads * tok * list_rows * HDIM,
    )
    shares, share_levels = scatter_far(made[: len(entries)], far, slots)
    key_sum, value_sum, *made = made[len(entries) :]
    made = call(
        lambda *refs: reduce_kernel(slots, *refs),
        over(tok) + over(tok),
        made,
        flops=6 * 10**9,
        vmem=16,
    )
    home = exchange(made[:slots])
    chunks = call(
        lambda *refs: merge_kernel(slots, share_levels, *refs),
        over(3 * tok),
        [key_sum, value_sum] + list(made[slots:]) + shares,
        vmem=8,
    )
    last = exchange(chunks)
    wide = shape((tok, columns))
    attended = call(
        lambda *refs: collect_kernel(slots, *refs),
        wide,
        [place] + home,
        specs=[SMEM] + [VMEM] * slots,
        vmem=8,
    )
    keep, *send = call(
        project_kernel,
        [shape((tok, columns), F32)] + [shape((tok, columns // 2))] * 2,
        [place, attended, out_weight],
        flops=4 * 10**9,
        specs=[SMEM, VMEM, VMEM],
        vmem=16,
    )
    got = [swap_head(part) for part in send]
    output = call(add_kernel, wide, [keep] + got, vmem=8)

    def put(chunks, blocks):
        return call(
            lambda *refs: place_kernel(slots, blocks, *refs),
            [wide] * len(blocks),
            [place] + chunks,
            scratch=[pltpu.SemaphoreType.DMA((len(blocks) * slots,))],
            specs=[SMEM] + [VMEM] * slots,
            vmem=8,
            free=True,
            outs=HBM,
        )

    query_grad, key_grad, value_grad = put(last, (0, 1, 2))
    return output, query_grad, key_grad, value_grad


def solution(mesh):
    placed = P("seq", "head")
    return jax.shard_map(
        on_device,
        mesh=mesh,
        in_specs=(placed, placed, placed, P(None, "head"), placed),
        out_specs=(placed, placed, placed, placed),
        check_vma=False,
    )
```

```python
import math

import jax
import jax.numpy as jnp
from jax import lax
from jax.experimental import pallas as pl
from jax.experimental.pallas import tpu as pltpu
from jax.sharding import PartitionSpec as P

HDIM = 128
ORDER = (0, 1, 3, 2)
BLOCK = 128
BF16 = jnp.bfloat16
F32 = jnp.float32
VMEM = pl.BlockSpec(memory_space=pltpu.VMEM)
SMEM = pl.BlockSpec(memory_space=pltpu.SMEM)
HBM = pl.BlockSpec(memory_space=pltpu.HBM)


def swap_seq(array, mask):
    return lax.ppermute(array, "seq", [(i, i ^ mask) for i in range(lax.axis_size("seq"))])


def swap_head(array):
    return lax.ppermute(array, "head", [(0, 1), (1, 0)])


def mm(left, right):
    return jnp.dot(left, right, preferred_element_type=F32)


def mm_cols(left, right):
    return lax.dot_general(left, right, (((1,), (1,)), ((), ())), preferred_element_type=F32)


def mm_rows(left, right):
    return lax.dot_general(left, right, (((0,), (0,)), ((), ())), preferred_element_type=F32)


def pool_matrix(rows, shift):
    shape = (rows, rows << shift)
    row = lax.broadcasted_iota(jnp.int32, shape, 0)
    col = lax.broadcasted_iota(jnp.int32, shape, 1)
    return jnp.where(lax.shift_right_logical(col, shift) == row, 1.0, 0.0).astype(BF16)


def call(kernel, out_shape, operands, scratch=(), flops=0, vmem=24, specs=None, free=False, outs=VMEM):
    specs = specs or [VMEM] * len(operands)
    operands = [
        pltpu.with_memory_space_constraint(x, pltpu.HBM) if spec is HBM else x
        for x, spec in zip(operands, specs)
    ]
    moved = 0 if free else sum(x.size * x.dtype.itemsize for x in operands)
    return pl.pallas_call(
        kernel,
        out_shape=out_shape,
        in_specs=specs,
        out_specs=jax.tree.map(lambda _: outs, out_shape),
        scratch_shapes=list(scratch),
        compiler_params=pltpu.CompilerParams(vmem_limit_bytes=vmem << 20),
        cost_estimate=pl.CostEstimate(flops=flops, bytes_accessed=moved, transcendentals=0),
    )(*operands)


def by_mask(refs):
    return [refs[ORDER.index(mask)] for mask in range(len(refs))]


def level_pool(rows, level):
    row = lax.broadcasted_iota(jnp.int32, (rows, BLOCK), 0)
    col = lax.broadcasted_iota(jnp.int32, (rows, BLOCK), 1)
    return jnp.where(lax.shift_right_logical(col, level) == row, 1.0, 0.0).astype(BF16)


def col_block(low, mask, width):
    return pl.ds(pl.multiple_of((low ^ mask) * width, width), width)


def piece_rows(level):
    return max(16, BLOCK >> level)


def split_kernel(slots, levels, at_ref, q_hbm, k_hbm, v_hbm, *refs):
    piece_refs, chunk_refs, sems = refs[: len(levels)], refs[len(levels) : -1], refs[-1]
    low = at_ref[0]
    tok, width = BLOCK, chunk_refs[0].shape[1]
    copies = []
    for place, source in ((1, k_hbm), (2, v_hbm), (0, q_hbm)):
        for mask in range(slots):
            copy = pltpu.make_async_copy(
                source.at[:, col_block(low, mask, width)],
                chunk_refs[mask].at[pl.ds(place * tok, tok), :],
                sems.at[place * slots + mask],
            )
            copy.start()
            copies.append(copy)
    for copy in copies[: 2 * slots]:
        copy.wait()
    for level, piece in zip(levels, piece_refs):
        rows = piece_rows(level)
        pool = level_pool(rows, level)
        for mask in range(slots):
            cols = col_block(low, mask, width)
            keys = mm(pool, chunk_refs[mask][tok : 2 * tok, :]) * (1.0 / (1 << level))
            piece[0:rows, cols] = keys.astype(BF16)
            piece[rows:, cols] = mm(pool, chunk_refs[mask][2 * tok : 3 * tok, :]).astype(BF16)
    for copy in copies[2 * slots :]:
        copy.wait()


def grad_kernel(at_ref, mine_ref, w_ref, other_ref, out_ref):
    core = at_ref[1]
    half = mine_ref.shape[1]
    first = pl.multiple_of(core * half, half)
    second = pl.multiple_of((1 - core) * half, half)
    total = mm(mine_ref[...], w_ref[pl.ds(first, half), :])
    total += mm(other_ref[...], w_ref[pl.ds(second, half), :])
    out_ref[...] = total.astype(BF16)


def second_kernel(slots, entries, at_ref, grad_ref, *refs):
    far_refs, out_refs = refs[: len(entries)], refs[len(entries) :]
    low = at_ref[0]
    tok, width = BLOCK, out_refs[0].shape[1]
    for mask in range(slots):
        cols = col_block(low, mask, width)
        out_refs[mask][0:tok, :] = grad_ref[:, cols]
        for (place, part, rows), far_ref in zip(entries, far_refs):
            for kind in range(2):
                at = tok + 64 * place + 32 * kind + part * rows
                source = far_ref[kind * rows : kind * rows + rows, cols]
                out_refs[mask][at : at + rows, :] = source


def attend_kernel(slots, far_levels, entries, *refs):
    first_refs, second_refs = by_mask(refs[:slots]), by_mask(refs[slots : 2 * slots])
    refs = refs[2 * slots :]
    far_refs, refs = refs[: len(entries)], refs[len(entries) :]
    kl_ref, vl_ref, q_all, g_all, prob_ref, grad_ref, fk_ref, fv_ref = refs
    tok = BLOCK
    pairs = slots // 2
    inv_scale = 1.0 / math.sqrt(HDIM)
    to_exp2 = inv_scale * math.log2(math.e)
    near, far = 2 * tok, 3 * tok
    for slab in range(slots):
        pair, row = slab // 2, (slab % 2) * tok
        q_all[pair, row : row + tok, :] = first_refs[slab][0:tok, :]
        kl_ref[pair, row : row + tok, :] = first_refs[slab][tok : 2 * tok, :]
        vl_ref[pair, row : row + tok, :] = first_refs[slab][2 * tok :, :]
        g_all[pair, row : row + tok, :] = second_refs[slab][0:tok, :]
        for place in range(far_levels):
            at = tok + 64 * place
            spot = far + place * BLOCK + 32 * slab
            for each in range(pairs):
                kl_ref[each, spot : spot + 32, :] = second_refs[slab][at : at + 32, :]
                vl_ref[each, spot : spot + 32, :] = second_refs[slab][at + 32 : at + 64, :]
    pool = pool_matrix(BLOCK, 1)
    for pair in range(pairs):
        kl_ref[pair ^ 1, near:far, :] = (mm(pool, kl_ref[pair, 0:near, :]) * 0.5).astype(BF16)
        vl_ref[pair ^ 1, near:far, :] = mm(pool, vl_ref[pair, 0:near, :]).astype(BF16)
    for pair in range(pairs):
        for head in range(2):
            lanes = slice(head * HDIM, head * HDIM + HDIM)
            queries, grads = q_all[pair, :, lanes], g_all[pair, :, lanes]
            keys, values = kl_ref[pair, :, lanes], vl_ref[pair, :, lanes]
            scores = mm_cols(queries, keys)
            prob_grad = mm_cols(grads, values)
            top = jnp.max(scores, axis=1, keepdims=True)
            raised = jnp.exp2((scores - top) * to_exp2)
            inverse = 1.0 / jnp.sum(raised, axis=1, keepdims=True)
            prob = raised * inverse
            centre = jnp.sum(prob * prob_grad, axis=1, keepdims=True)
            prob_low = prob.astype(BF16)
            score_grad = (prob * ((prob_grad - centre) * inv_scale)).astype(BF16)
            prob_ref[2 * pair + head] = prob_low
            grad_ref[2 * pair + head] = score_grad
            key_terms = mm_rows(score_grad[:, far:], queries)
            value_terms = mm_rows(prob_low[:, far:], grads)
            if pair == 0:
                fk_ref[:, lanes] = key_terms
                fv_ref[:, lanes] = value_terms
            else:
                fk_ref[:, lanes] += key_terms
                fv_ref[:, lanes] += value_terms
    for (place, part, rows), out_ref in zip(entries, far_refs):
        for kind, total in enumerate((fk_ref, fv_ref)):
            for slab in range(slots):
                start = place * BLOCK + 32 * slab + part * rows
                at = (kind * slots + slab) * rows
                out_ref[at : at + rows, :] = total[start : start + rows, :].astype(BF16)


def reduce_kernel(slots, kl_ref, vl_ref, q_all, g_all, prob_ref, grad_ref, *refs):
    home_refs, (dk_ref, dv_ref, ck_ref, cv_ref) = refs[:slots], refs[slots:]
    tok = BLOCK
    pairs = slots // 2
    near, far = 2 * tok, 3 * tok
    for pair in range(pairs):
        for head in range(2):
            lanes = slice(head * HDIM, head * HDIM + HDIM)
            unit = 2 * pair + head
            attended = mm(prob_ref[unit], vl_ref[pair, :, lanes]).astype(BF16)
            query_grad = mm(grad_ref[unit], kl_ref[pair, :, lanes]).astype(BF16)
            for side in range(2):
                rows = slice(side * tok, side * tok + tok)
                home_refs[2 * pair + side][0:tok, lanes] = attended[rows]
                home_refs[2 * pair + side][tok:, lanes] = query_grad[rows]
            key_terms = mm_rows(grad_ref[unit, :, 0:far], q_all[pair, :, lanes])
            value_terms = mm_rows(prob_ref[unit, :, 0:far], g_all[pair, :, lanes])
            for terms, local, level1 in (
                (key_terms, dk_ref, ck_ref),
                (value_terms, dv_ref, cv_ref),
            ):
                local[pair * near : pair * near + near, lanes] = terms[0:near]
                level1[pair ^ 1, :, lanes] = terms[near:].astype(BF16)
    pool = pool_matrix(BLOCK, 1)
    for pair in range(pairs):
        rows = slice(pair * near, pair * near + near)
        dk_ref[rows, :] += mm_rows(pool, ck_ref[pair]) * 0.5
        dv_ref[rows, :] += mm_rows(pool, cv_ref[pair])


def merge_kernel(slots, levels, dk_ref, dv_ref, *refs):
    far_refs, out_refs = refs[: len(levels)], refs[len(levels) :]
    tok = BLOCK
    for slab in range(slots):
        rows = slice(slab * tok, slab * tok + tok)
        key_sum, value_sum = dk_ref[rows, :], dv_ref[rows, :]
        for level, far_ref in zip(levels, far_refs):
            count = piece_rows(level)
            pool = level_pool(count, level)
            mine = far_ref[slab * count : slab * count + count, :]
            key_sum += mm_rows(pool, mine) * (1.0 / (1 << level))
            at = (slots + slab) * count
            value_sum += mm_rows(pool, far_ref[at : at + count, :])
        out_refs[slab][0:tok, :] = key_sum.astype(BF16)
        out_refs[slab][tok:, :] = value_sum.astype(BF16)


def collect_kernel(slots, at_ref, *refs):
    in_refs, att_ref = by_mask(refs[:slots]), refs[slots]
    low = at_ref[0]
    tok, width = BLOCK, in_refs[0].shape[1]
    for mask in range(slots):
        att_ref[:, col_block(low, mask, width)] = in_refs[mask][0:tok, :]


def project_kernel(at_ref, att_ref, w_ref, keep_ref, *send_refs):
    core = at_ref[1]
    half = att_ref.shape[1]
    part = half // len(send_refs)
    for place, send_ref in enumerate(send_refs):
        other = pl.multiple_of((1 - core) * half + place * part, part)
        send_ref[...] = mm_cols(att_ref[...], w_ref[pl.ds(other, part), :]).astype(BF16)
    first = pl.multiple_of(core * half, half)
    keep_ref[...] = mm_cols(att_ref[...], w_ref[pl.ds(first, half), :])


def add_kernel(keep_ref, *refs):
    got_refs, out_ref = refs[:-1], refs[-1]
    part = got_refs[0].shape[1]
    for place, got_ref in enumerate(got_refs):
        cols = slice(place * part, place * part + part)
        out_ref[:, cols] = (keep_ref[:, cols] + got_ref[...].astype(F32)).astype(BF16)


def place_kernel(slots, blocks, at_ref, *refs):
    in_refs, out_refs, sems = by_mask(refs[:slots]), refs[slots:-1], refs[-1]
    low = at_ref[0]
    tok, width = BLOCK, in_refs[0].shape[1]
    copies = []
    for place, block in enumerate(blocks):
        for mask in range(slots):
            copy = pltpu.make_async_copy(
                in_refs[mask].at[pl.ds(block * tok, tok), :],
                out_refs[place].at[:, col_block(low, mask, width)],
                sems.at[place * slots + mask],
            )
            copy.start()
            copies.append(copy)
    for copy in copies:
        copy.wait()


def straight(levels, slots):
    return all((slots << place) * 4 <= 32 for place in range(len(levels)))


def far_entries(levels, slots):
    entries, masks = [], []
    for place, level in enumerate(levels):
        if not straight(levels, slots):
            entries.append((place, 0, 32))
            continue
        for part in range(1 << place):
            entries.append((place, part, BLOCK >> level))
            masks.append(1 << level ^ part * slots)
    return entries, masks


def gather_far(pieces, levels, slots):
    columns = pieces[0].shape[1]
    if straight(levels, slots):
        entries, masks = far_entries(levels, slots)
        return [swap_seq(pieces[entry[0]], mask) for entry, mask in zip(entries, masks)]
    held = {}
    for place, level in enumerate(levels):
        block = pieces[place].reshape(2, piece_rows(level), columns)
        held[level] = block[:, None, : BLOCK >> level]
    found = []
    for step in levels:
        sent = [held[level].reshape(-1, columns) for level in levels if level >= step]
        got = swap_seq(jnp.concatenate(sent, axis=0), 1 << step)
        first = 0
        for level in levels:
            if level < step:
                continue
            count = held[level].size // columns
            part = got[first : first + count].reshape(held[level].shape)
            first += count
            if level == step:
                found.append(part.reshape(64, columns))
            else:
                held[level] = jnp.concatenate([held[level], part], axis=1)
    return found


def scatter_far(packed, levels, slots):
    width = packed[0].shape[1]
    if straight(levels, slots):
        entries, masks = far_entries(levels, slots)
        shares = [swap_seq(array, mask) for array, mask in zip(packed, masks)]
        return shares, [levels[entry[0]] for entry in entries]
    blocks = {}
    for place, level in enumerate(levels):
        rows = BLOCK >> level
        blocks[level] = packed[place].reshape(2 * slots, 32 // rows, rows, width)
    ready = {}
    for step in reversed(levels):
        sent, kept = [blocks[step].reshape(-1, width)], {}
        for level in levels:
            if level > step:
                size = ready[level].shape[1] // 2
                kept[level] = ready[level][:, :size]
                sent.append(ready[level][:, size:].astype(BF16).reshape(-1, width))
        got = swap_seq(jnp.concatenate(sent, axis=0), 1 << step)
        first = blocks[step].size // width
        ready[step] = got[0:first].reshape(blocks[step].shape)
        for level in kept:
            count = kept[level].size // width
            part = got[first : first + count].reshape(kept[level].shape)
            first += count
            ready[level] = kept[level].astype(F32) + part.astype(F32)
    shares = []
    for level in levels:
        share = ready[level].astype(BF16).reshape(2 * slots, -1, width)
        pad = piece_rows(level) - share.shape[1]
        if pad:
            share = jnp.pad(share, ((0, 0), (0, pad), (0, 0)))
        shares.append(share.reshape(-1, width))
    return shares, list(levels)


def on_device(queries, key_tokens, value_tokens, out_weight, output_grad):
    tok, columns = queries.shape
    heads = columns // HDIM
    slots = heads // 2
    width = columns // slots
    local_levels = slots.bit_length() - 1
    level_count = lax.axis_size("seq").bit_length() - 1
    far = list(range(local_levels, level_count))
    far_rows = 64 * len(far)
    list_rows = 3 * tok + BLOCK * len(far)
    entries, _ = far_entries(far, slots)
    place = jnp.stack([lax.axis_index("seq") & (slots - 1), lax.axis_index("head")])
    place = place.astype(jnp.int32)

    def shape(dims, dtype=BF16):
        return jax.ShapeDtypeStruct(dims, dtype)

    def over(rows):
        return [shape((rows, width))] * slots

    def exchange(chunks):
        moved = [chunks[0]] + [swap_seq(chunks[mask], mask) for mask in range(1, slots)]
        return [moved[mask] for mask in ORDER]

    other_grad = swap_head(output_grad)
    made = call(
        lambda *refs: split_kernel(slots, far, *refs),
        [shape((2 * piece_rows(level), columns)) for level in far] + over(3 * tok),
        (place, queries, key_tokens, value_tokens),
        scratch=[pltpu.SemaphoreType.DMA((3 * slots,))],
        flops=6 * 10**9,
        specs=[SMEM] + [HBM] * 3,
        vmem=8,
    )
    pieces, chunks = made[: len(far)], list(made[len(far) :])
    far_got = gather_far(pieces, far, slots)
    grads = call(
        grad_kernel,
        shape((tok, columns)),
        [place, output_grad, out_weight, other_grad],
        flops=4 * tok * columns * columns,
        specs=[SMEM] + [VMEM] * 3,
        vmem=16,
    )
    first = {0: chunks[0]}
    for mask in ORDER[1:]:
        if mask == ORDER[-1]:
            chunks[mask], grads, first[1] = lax.optimization_barrier((chunks[mask], grads, first[1]))
        first[mask] = swap_seq(chunks[mask], mask)
    first = [first[mask] for mask in ORDER]
    chunks = call(
        lambda *refs: second_kernel(slots, entries, *refs),
        over(tok + far_rows),
        [place, grads] + far_got,
        specs=[SMEM] + [VMEM] * (1 + len(far_got)),
        vmem=8,
    )
    second = exchange(chunks)
    pairs = slots // 2
    made = call(
        lambda *refs: attend_kernel(slots, len(far), entries, *refs),
        [shape((2 * slots * rows, width)) for _, _, rows in entries]
        + [shape((pairs, list_rows, width))] * 2
        + [shape((pairs, 2 * tok, width))] * 2
        + [shape((slots, 2 * tok, list_rows))] * 2,
        first + second,
        scratch=[pltpu.VMEM((BLOCK * len(far), width), F32)] * 2,
        flops=6 * heads * tok * list_rows * HDIM,
    )
    shares, share_levels = scatter_far(made[: len(entries)], far, slots)
    *made, key_sum, value_sum = call(
        lambda *refs: reduce_kernel(slots, *refs),
        over(2 * tok) + [shape((slots * tok, width), F32)] * 2,
        made[len(entries) :],
        scratch=[pltpu.VMEM((pairs, BLOCK, width), BF16)] * 2,
        flops=6 * 10**9,
        vmem=16,
    )
    made[2], *shares[1:] = lax.optimization_barrier((made[2], *shares[1:]))
    home = exchange(made)
    chunks = call(
        lambda *refs: merge_kernel(slots, share_levels, *refs),
        over(2 * tok),
        [key_sum, value_sum] + shares,
        vmem=8,
    )
    home, _ = lax.optimization_barrier((home, chunks))
    last = exchange(chunks)
    wide = shape((tok, columns))
    attended = call(
        lambda *refs: collect_kernel(slots, *refs),
        wide,
        [place] + home,
        specs=[SMEM] + [VMEM] * slots,
        vmem=8,
    )
    keep, *send = call(
        project_kernel,
        [shape((tok, columns), F32)] + [shape((tok, columns // 2))] * 2,
        [place, attended, out_weight],
        flops=4 * 10**9,
        specs=[SMEM, VMEM, VMEM],
        vmem=16,
    )
    got = [swap_head(part) for part in send]
    output = call(add_kernel, wide, [keep] + got, vmem=8)

    def put(chunks, blocks, flops):
        return call(
            lambda *refs: place_kernel(slots, blocks, *refs),
            [wide] * len(blocks),
            [place] + chunks,
            scratch=[pltpu.SemaphoreType.DMA((len(blocks) * slots,))],
            specs=[SMEM] + [VMEM] * slots,
            vmem=8,
            free=True,
            flops=flops,
            outs=HBM,
        )

    (query_grad,) = put(home, (1,), 4 * 10**9)
    key_grad, value_grad = put(last, (0, 1), 0)
    return output, query_grad, key_grad, value_grad


def solution(mesh):
    placed = P("seq", "head")
    return jax.shard_map(
        on_device,
        mesh=mesh,
        in_specs=(placed, placed, placed, P(None, "head"), placed),
        out_specs=(placed, placed, placed, placed),
        check_vma=False,
    )
```

```python
import math

import jax
import jax.numpy as jnp
from jax import lax
from jax.experimental import pallas as pl
from jax.experimental.pallas import tpu as pltpu
from jax.sharding import PartitionSpec as P

HDIM = 128
ORDER = (0, 1, 2, 3)
BLOCK = 128
BF16 = jnp.bfloat16
F32 = jnp.float32
VMEM = pl.BlockSpec(memory_space=pltpu.VMEM)
SMEM = pl.BlockSpec(memory_space=pltpu.SMEM)
HBM = pl.BlockSpec(memory_space=pltpu.HBM)


def swap_seq(array, mask):
    return lax.ppermute(array, "seq", [(i, i ^ mask) for i in range(lax.axis_size("seq"))])


def swap_head(array):
    return lax.ppermute(array, "head", [(0, 1), (1, 0)])


def mm(left, right):
    return jnp.dot(left, right, preferred_element_type=F32)


def mm_cols(left, right):
    return lax.dot_general(left, right, (((1,), (1,)), ((), ())), preferred_element_type=F32)


def mm_rows(left, right):
    return lax.dot_general(left, right, (((0,), (0,)), ((), ())), preferred_element_type=F32)


def pool_matrix(rows, shift):
    shape = (rows, rows << shift)
    row = lax.broadcasted_iota(jnp.int32, shape, 0)
    col = lax.broadcasted_iota(jnp.int32, shape, 1)
    return jnp.where(lax.shift_right_logical(col, shift) == row, 1.0, 0.0).astype(BF16)


def call(kernel, out_shape, operands, scratch=(), flops=0, vmem=24, specs=None, outs=VMEM):
    specs = specs or [VMEM] * len(operands)
    operands = [
        pltpu.with_memory_space_constraint(x, pltpu.HBM) if spec is HBM else x
        for x, spec in zip(operands, specs)
    ]
    moved = sum(x.size * x.dtype.itemsize for x in operands)
    return pl.pallas_call(
        kernel,
        out_shape=out_shape,
        in_specs=specs,
        out_specs=outs if isinstance(outs, list) else jax.tree.map(lambda _: outs, out_shape),
        scratch_shapes=list(scratch),
        compiler_params=pltpu.CompilerParams(vmem_limit_bytes=vmem << 20),
        cost_estimate=pl.CostEstimate(flops=flops, bytes_accessed=moved, transcendentals=0),
    )(*operands)


def by_mask(refs):
    return [refs[ORDER.index(mask)] for mask in range(len(refs))]


def level_pool(rows, level):
    row = lax.broadcasted_iota(jnp.int32, (rows, BLOCK), 0)
    col = lax.broadcasted_iota(jnp.int32, (rows, BLOCK), 1)
    return jnp.where(lax.shift_right_logical(col, level) == row, 1.0, 0.0).astype(BF16)


def col_block(low, mask, width):
    return pl.ds(pl.multiple_of((low ^ mask) * width, width), width)


def piece_rows(level):
    return max(16, BLOCK >> level)


def split_kernel(slots, levels, at_ref, q_hbm, k_hbm, v_hbm, *refs):
    piece_refs, refs = refs[: len(levels)], refs[len(levels) :]
    chunk_refs, (q_ref, k_ref, v_ref, sems) = refs[:slots], refs[slots:]
    low = at_ref[0]
    tok, width = BLOCK, chunk_refs[0].shape[1]
    held = (q_ref, k_ref, v_ref)
    copies = [
        pltpu.make_async_copy(source, held[place], sems.at[place])
        for place, source in ((1, k_hbm), (2, v_hbm), (0, q_hbm))
    ]
    for copy in copies:
        copy.start()
    copies[0].wait()
    copies[1].wait()
    for level, piece in zip(levels, piece_refs):
        rows = piece_rows(level)
        pool = level_pool(rows, level)
        piece[0:rows, :] = (mm(pool, k_ref[...]) * (1.0 / (1 << level))).astype(BF16)
        piece[rows:, :] = mm(pool, v_ref[...]).astype(BF16)
    copies[2].wait()
    for mask in range(slots):
        cols = col_block(low, mask, width)
        for place, source in enumerate(held):
            chunk_refs[mask][place * tok : place * tok + tok, :] = source[:, cols]


def grad_kernel(at_ref, mine_ref, w_ref, other_ref, out_ref):
    core = at_ref[1]
    half = mine_ref.shape[1]
    first = pl.multiple_of(core * half, half)
    second = pl.multiple_of((1 - core) * half, half)
    total = mm(mine_ref[...], w_ref[pl.ds(first, half), :])
    total += mm(other_ref[...], w_ref[pl.ds(second, half), :])
    out_ref[...] = total.astype(BF16)


def second_kernel(slots, entries, at_ref, grad_ref, *refs):
    far_refs, out_refs = refs[: len(entries)], refs[len(entries) :]
    low = at_ref[0]
    tok, width = BLOCK, out_refs[0].shape[1]
    for mask in range(slots):
        cols = col_block(low, mask, width)
        out_refs[mask][0:tok, :] = grad_ref[:, cols]
        for (place, part, rows), far_ref in zip(entries, far_refs):
            for kind in range(2):
                at = tok + 64 * place + 32 * kind + part * rows
                source = far_ref[kind * rows : kind * rows + rows, cols]
                out_refs[mask][at : at + rows, :] = source


def attend_kernel(slots, far_levels, entries, *refs):
    first_refs, second_refs = by_mask(refs[:slots]), by_mask(refs[slots : 2 * slots])
    refs = refs[2 * slots :]
    far_refs, refs = refs[: len(entries)], refs[len(entries) :]
    kl_ref, vl_ref, q_all, g_all, prob_ref, grad_ref, sum_ref, fk_ref, fv_ref = refs
    tok = BLOCK
    pairs = slots // 2
    inv_scale = 1.0 / math.sqrt(HDIM)
    to_exp2 = inv_scale * math.log2(math.e)
    near, far = 2 * tok, 3 * tok
    for slab in range(slots):
        pair, row = slab // 2, (slab % 2) * tok
        q_all[pair, row : row + tok, :] = first_refs[slab][0:tok, :]
        kl_ref[pair, row : row + tok, :] = first_refs[slab][tok : 2 * tok, :]
        vl_ref[pair, row : row + tok, :] = first_refs[slab][2 * tok :, :]
        g_all[pair, row : row + tok, :] = second_refs[slab][0:tok, :]
        for place in range(far_levels):
            at = tok + 64 * place
            spot = far + place * BLOCK + 32 * slab
            for each in range(pairs):
                kl_ref[each, spot : spot + 32, :] = second_refs[slab][at : at + 32, :]
                vl_ref[each, spot : spot + 32, :] = second_refs[slab][at + 32 : at + 64, :]
    pool = pool_matrix(BLOCK, 1)
    for pair in range(pairs):
        kl_ref[pair ^ 1, near:far, :] = (mm(pool, kl_ref[pair, 0:near, :]) * 0.5).astype(BF16)
        vl_ref[pair ^ 1, near:far, :] = mm(pool, vl_ref[pair, 0:near, :]).astype(BF16)
    for pair in range(pairs):
        for head in range(2):
            lanes = slice(head * HDIM, head * HDIM + HDIM)
            queries, grads = q_all[pair, :, lanes], g_all[pair, :, lanes]
            keys, values = kl_ref[pair, :, lanes], vl_ref[pair, :, lanes]
            scores = mm_cols(queries, keys)
            prob_grad = mm_cols(grads, values)
            top = jnp.max(scores, axis=1, keepdims=True)
            raised = jnp.exp2((scores - top) * to_exp2)
            inverse = 1.0 / jnp.sum(raised, axis=1, keepdims=True)
            centre = jnp.sum(raised * prob_grad, axis=1, keepdims=True) * inverse
            raised_low = raised.astype(BF16)
            score_grad = (raised * (prob_grad - centre)).astype(BF16)
            queries = (queries.astype(F32) * (inverse * inv_scale)).astype(BF16)
            grads = (grads.astype(F32) * inverse).astype(BF16)
            prob_ref[2 * pair + head] = raised_low
            grad_ref[2 * pair + head] = score_grad
            sum_ref[2 * pair + head] = jnp.broadcast_to(inverse, (near, HDIM))
            q_all[pair, :, lanes] = queries
            g_all[pair, :, lanes] = grads
            key_terms = mm_rows(score_grad[:, far:], queries)
            value_terms = mm_rows(raised_low[:, far:], grads)
            if pair == 0:
                fk_ref[:, lanes] = key_terms
                fv_ref[:, lanes] = value_terms
            else:
                fk_ref[:, lanes] += key_terms
                fv_ref[:, lanes] += value_terms
    for (place, part, rows), out_ref in zip(entries, far_refs):
        for kind, total in enumerate((fk_ref, fv_ref)):
            for slab in range(slots):
                start = place * BLOCK + 32 * slab + part * rows
                at = (kind * slots + slab) * rows
                out_ref[at : at + rows, :] = total[start : start + rows, :].astype(BF16)


def reduce_kernel(slots, kl_ref, vl_ref, prob_ref, grad_ref, sum_ref, *home_refs):
    tok = BLOCK
    inv_scale = 1.0 / math.sqrt(HDIM)
    for pair in range(slots // 2):
        for head in range(2):
            lanes = slice(head * HDIM, head * HDIM + HDIM)
            unit = 2 * pair + head
            inverse = sum_ref[unit]
            attended = (mm(prob_ref[unit], vl_ref[pair, :, lanes]) * inverse).astype(BF16)
            query_grad = mm(grad_ref[unit], kl_ref[pair, :, lanes]) * (inverse * inv_scale)
            query_grad = query_grad.astype(BF16)
            for side in range(2):
                rows = slice(side * tok, side * tok + tok)
                home_refs[2 * pair + side][0:tok, lanes] = attended[rows]
                home_refs[2 * pair + side][tok:, lanes] = query_grad[rows]


def local_kernel(slots, q_all, g_all, prob_ref, grad_ref, dk_ref, dv_ref, ck_ref, cv_ref):
    tok = BLOCK
    pairs = slots // 2
    near, far = 2 * tok, 3 * tok
    for pair in range(pairs):
        for head in range(2):
            lanes = slice(head * HDIM, head * HDIM + HDIM)
            unit = 2 * pair + head
            key_terms = mm_rows(grad_ref[unit, :, 0:far], q_all[pair, :, lanes])
            value_terms = mm_rows(prob_ref[unit, :, 0:far], g_all[pair, :, lanes])
            for terms, local, level1 in (
                (key_terms, dk_ref, ck_ref),
                (value_terms, dv_ref, cv_ref),
            ):
                local[pair * near : pair * near + near, lanes] = terms[0:near]
                level1[pair ^ 1, :, lanes] = terms[near:].astype(BF16)
    pool = pool_matrix(BLOCK, 1)
    for pair in range(pairs):
        rows = slice(pair * near, pair * near + near)
        dk_ref[rows, :] += mm_rows(pool, ck_ref[pair]) * 0.5
        dv_ref[rows, :] += mm_rows(pool, cv_ref[pair])


def merge_kernel(slots, levels, dk_ref, dv_ref, *refs):
    far_refs, out_refs = refs[: len(levels)], refs[len(levels) :]
    tok = BLOCK
    for slab in range(slots):
        rows = slice(slab * tok, slab * tok + tok)
        key_sum, value_sum = dk_ref[rows, :], dv_ref[rows, :]
        for level, far_ref in zip(levels, far_refs):
            count = piece_rows(level)
            pool = level_pool(count, level)
            mine = far_ref[slab * count : slab * count + count, :]
            key_sum += mm_rows(pool, mine) * (1.0 / (1 << level))
            at = (slots + slab) * count
            value_sum += mm_rows(pool, far_ref[at : at + count, :])
        out_refs[slab][0:tok, :] = key_sum.astype(BF16)
        out_refs[slab][tok:, :] = value_sum.astype(BF16)


def send_kernel(slots, at_ref, w_ref, *refs):
    in_refs, att_ref, send_refs = by_mask(refs[:slots]), refs[slots], refs[slots + 1 :]
    low, core = at_ref[0], at_ref[1]
    tok, half = att_ref.shape
    width = in_refs[0].shape[1]
    for mask in range(slots):
        att_ref[:, col_block(low, mask, width)] = in_refs[mask][0:tok, :]
    part = half // len(send_refs)
    for place, send_ref in enumerate(send_refs):
        other = pl.multiple_of((1 - core) * half + place * part, part)
        send_ref[...] = mm_cols(att_ref[...], w_ref[pl.ds(other, part), :]).astype(BF16)


def keep_kernel(slots, at_ref, w_ref, att_ref, *refs):
    in_refs, (keep_ref, dq_hbm, dq_ref, sem) = by_mask(refs[:slots]), refs[slots:]
    low, core = at_ref[0], at_ref[1]
    tok, half = att_ref.shape
    width = in_refs[0].shape[1]
    for mask in range(slots):
        dq_ref[:, col_block(low, mask, width)] = in_refs[mask][tok:, :]
    copy = pltpu.make_async_copy(dq_ref, dq_hbm, sem)
    copy.start()
    first = pl.multiple_of(core * half, half)
    keep_ref[...] = mm_cols(att_ref[...], w_ref[pl.ds(first, half), :])
    copy.wait()


def finish_kernel(slots, at_ref, keep_ref, *refs):
    in_refs, refs = by_mask(refs[:slots]), refs[slots:]
    got_refs, refs = refs[:-7], refs[-7:]
    hbm_refs, held_refs, sems = refs[:3], refs[3:6], refs[6]
    low = at_ref[0]
    tok, width = BLOCK, in_refs[0].shape[1]
    copies = [
        pltpu.make_async_copy(held_refs[place], hbm_refs[place], sems.at[place])
        for place in range(3)
    ]
    for place in range(2):
        for mask in range(slots):
            rows = slice(place * tok, place * tok + tok)
            held_refs[place][:, col_block(low, mask, width)] = in_refs[mask][rows, :]
        copies[place].start()
    part = got_refs[0].shape[1]
    for place, got_ref in enumerate(got_refs):
        cols = slice(place * part, place * part + part)
        held_refs[2][:, cols] = (keep_ref[:, cols] + got_ref[...].astype(F32)).astype(BF16)
    copies[2].start()
    for copy in copies:
        copy.wait()


def straight(levels, slots):
    return all((slots << place) * 4 <= 32 for place in range(len(levels)))


def far_entries(levels, slots):
    entries, masks = [], []
    for place, level in enumerate(levels):
        if not straight(levels, slots):
            entries.append((place, 0, 32))
            continue
        for part in range(1 << place):
            entries.append((place, part, BLOCK >> level))
            masks.append(1 << level ^ part * slots)
    return entries, masks


def gather_far(pieces, levels, slots):
    columns = pieces[0].shape[1]
    if straight(levels, slots):
        entries, masks = far_entries(levels, slots)
        return [swap_seq(pieces[entry[0]], mask) for entry, mask in zip(entries, masks)]
    held = {}
    for place, level in enumerate(levels):
        block = pieces[place].reshape(2, piece_rows(level), columns)
        held[level] = block[:, None, : BLOCK >> level]
    found = []
    for step in levels:
        sent = [held[level].reshape(-1, columns) for level in levels if level >= step]
        got = swap_seq(jnp.concatenate(sent, axis=0), 1 << step)
        first = 0
        for level in levels:
            if level < step:
                continue
            count = held[level].size // columns
            part = got[first : first + count].reshape(held[level].shape)
            first += count
            if level == step:
                found.append(part.reshape(64, columns))
            else:
                held[level] = jnp.concatenate([held[level], part], axis=1)
    return found


def scatter_far(packed, levels, slots):
    width = packed[0].shape[1]
    if straight(levels, slots):
        entries, masks = far_entries(levels, slots)
        shares = [swap_seq(array, mask) for array, mask in zip(packed, masks)]
        return shares, [levels[entry[0]] for entry in entries]
    blocks = {}
    for place, level in enumerate(levels):
        rows = BLOCK >> level
        blocks[level] = packed[place].reshape(2 * slots, 32 // rows, rows, width)
    ready = {}
    for step in reversed(levels):
        sent, kept = [blocks[step].reshape(-1, width)], {}
        for level in levels:
            if level > step:
                size = ready[level].shape[1] // 2
                kept[level] = ready[level][:, :size]
                sent.append(ready[level][:, size:].astype(BF16).reshape(-1, width))
        got = swap_seq(jnp.concatenate(sent, axis=0), 1 << step)
        first = blocks[step].size // width
        ready[step] = got[0:first].reshape(blocks[step].shape)
        for level in kept:
            count = kept[level].size // width
            part = got[first : first + count].reshape(kept[level].shape)
            first += count
            ready[level] = kept[level].astype(F32) + part.astype(F32)
    shares = []
    for level in levels:
        share = ready[level].astype(BF16).reshape(2 * slots, -1, width)
        pad = piece_rows(level) - share.shape[1]
        if pad:
            share = jnp.pad(share, ((0, 0), (0, pad), (0, 0)))
        shares.append(share.reshape(-1, width))
    return shares, list(levels)


def on_device(queries, key_tokens, value_tokens, out_weight, output_grad):
    tok, columns = queries.shape
    heads = columns // HDIM
    slots = heads // 2
    width = columns // slots
    local_levels = slots.bit_length() - 1
    level_count = lax.axis_size("seq").bit_length() - 1
    far = list(range(local_levels, level_count))
    far_rows = 64 * len(far)
    list_rows = 3 * tok + BLOCK * len(far)
    entries, _ = far_entries(far, slots)
    place = jnp.stack([lax.axis_index("seq") & (slots - 1), lax.axis_index("head")])
    place = place.astype(jnp.int32)

    def shape(dims, dtype=BF16):
        return jax.ShapeDtypeStruct(dims, dtype)

    def over(rows):
        return [shape((rows, width))] * slots

    def exchange(chunks):
        moved = [chunks[0]] + [swap_seq(chunks[mask], mask) for mask in range(1, slots)]
        return [moved[mask] for mask in ORDER]

    made = call(
        lambda *refs: split_kernel(slots, far, *refs),
        [shape((2 * piece_rows(level), columns)) for level in far] + over(3 * tok),
        (place, queries, key_tokens, value_tokens),
        scratch=[pltpu.VMEM((tok, columns), BF16)] * 3 + [pltpu.SemaphoreType.DMA((3,))],
        flops=6 * 10**9,
        specs=[SMEM] + [HBM] * 3,
        vmem=8,
    )
    pieces, chunks = made[: len(far)], list(made[len(far) :])
    pieces, output_grad = lax.optimization_barrier((pieces, output_grad))
    other_grad = swap_head(output_grad)
    far_got = gather_far(pieces, far, slots)
    grads = call(
        grad_kernel,
        shape((tok, columns)),
        [place, output_grad, out_weight, other_grad],
        flops=4 * tok * columns * columns,
        specs=[SMEM] + [VMEM] * 3,
        vmem=16,
    )
    first = {0: chunks[0]}
    for mask in ORDER[1:]:
        if mask == ORDER[-1]:
            chunks[mask], grads, first[1] = lax.optimization_barrier((chunks[mask], grads, first[1]))
        first[mask] = swap_seq(chunks[mask], mask)
    first = [first[mask] for mask in ORDER]
    chunks = call(
        lambda *refs: second_kernel(slots, entries, *refs),
        over(tok + far_rows),
        [place, grads] + far_got,
        specs=[SMEM] + [VMEM] * (1 + len(far_got)),
        vmem=8,
    )
    second = exchange(chunks)
    pairs = slots // 2
    made = call(
        lambda *refs: attend_kernel(slots, len(far), entries, *refs),
        [shape((2 * slots * rows, width)) for _, _, rows in entries]
        + [shape((pairs, list_rows, width))] * 2
        + [shape((pairs, 2 * tok, width))] * 2
        + [shape((slots, 2 * tok, list_rows))] * 2
        + [shape((slots, 2 * tok, HDIM), F32)],
        first + second,
        scratch=[pltpu.VMEM((BLOCK * len(far), width), F32)] * 2,
        flops=6 * heads * tok * list_rows * HDIM,
    )
    shares, share_levels = scatter_far(made[: len(entries)], far, slots)
    key_list, value_list, asked, grads, probs, score_grads, sums = made[len(entries) :]
    made = call(
        lambda *refs: reduce_kernel(slots, *refs),
        over(2 * tok),
        [key_list, value_list, probs, score_grads, sums],
        flops=6 * 10**9,
        vmem=16,
    )
    key_sum, value_sum = call(
        lambda *refs: local_kernel(slots, *refs),
        [shape((slots * tok, width), F32)] * 2,
        [asked, grads, probs, score_grads],
        scratch=[pltpu.VMEM((pairs, BLOCK, width), BF16)] * 2,
        flops=4 * heads * tok * list_rows * HDIM,
        vmem=16,
    )
    made = list(made)
    late = ORDER[-1]
    made[late], key_sum, *shares[1:] = lax.optimization_barrier((made[late], key_sum, *shares[1:]))
    home = exchange(made)
    chunks = call(
        lambda *refs: merge_kernel(slots, share_levels, *refs),
        over(2 * tok),
        [key_sum, value_sum] + shares,
        vmem=8,
    )
    home, _ = lax.optimization_barrier((home, chunks))
    chunks = list(chunks)
    chunks[late], home[-1] = lax.optimization_barrier((chunks[late], home[-1]))
    last = exchange(chunks)
    wide = shape((tok, columns))
    attended, *send = call(
        lambda *refs: send_kernel(slots, *refs),
        [wide] + [shape((tok, columns // 2))] * 2,
        [place, out_weight] + home,
        flops=2 * tok * columns * columns,
        specs=[SMEM] + [VMEM] * (1 + slots),
        vmem=16,
    )
    got = [swap_head(part) for part in send]
    keep, query_grad = call(
        lambda *refs: keep_kernel(slots, *refs),
        [shape((tok, columns), F32), wide],
        [place, out_weight, attended] + home,
        scratch=[pltpu.VMEM((tok, columns), BF16), pltpu.SemaphoreType.DMA(())],
        flops=4 * 10**9,
        specs=[SMEM] + [VMEM] * (2 + slots),
        outs=[VMEM, HBM],
        vmem=16,
    )
    key_grad, value_grad, output = call(
        lambda *refs: finish_kernel(slots, *refs),
        [wide] * 3,
        [place, keep] + last + got,
        scratch=[pltpu.VMEM((tok, columns), BF16)] * 3 + [pltpu.SemaphoreType.DMA((3,))],
        specs=[SMEM] + [VMEM] * (1 + slots + len(got)),
        outs=HBM,
        vmem=8,
    )
    return output, query_grad, key_grad, value_grad


def solution(mesh):
    placed = P("seq", "head")
    return jax.shard_map(
        on_device,
        mesh=mesh,
        in_specs=(placed, placed, placed, P(None, "head"), placed),
        out_specs=(placed, placed, placed, placed),
        check_vma=False,
    )
```

```python
import math

import jax
import jax.numpy as jnp
from jax import lax
from jax.experimental import pallas as pl
from jax.experimental.pallas import tpu as pltpu
from jax.sharding import PartitionSpec as P

HDIM = 128
ORDER = (0, 1, 2, 3)
BLOCK = 128
BF16 = jnp.bfloat16
F32 = jnp.float32
VMEM = pl.BlockSpec(memory_space=pltpu.VMEM)
SMEM = pl.BlockSpec(memory_space=pltpu.SMEM)
HBM = pl.BlockSpec(memory_space=pltpu.HBM)


def swap_seq(array, mask):
    return lax.ppermute(array, "seq", [(i, i ^ mask) for i in range(lax.axis_size("seq"))])


def swap_head(array):
    return lax.ppermute(array, "head", [(0, 1), (1, 0)])


def mm(left, right):
    return jnp.dot(left, right, preferred_element_type=F32)


def mm_cols(left, right):
    return lax.dot_general(left, right, (((1,), (1,)), ((), ())), preferred_element_type=F32)


def mm_rows(left, right):
    return lax.dot_general(left, right, (((0,), (0,)), ((), ())), preferred_element_type=F32)


def pool_matrix(rows, shift):
    shape = (rows, rows << shift)
    row = lax.broadcasted_iota(jnp.int32, shape, 0)
    col = lax.broadcasted_iota(jnp.int32, shape, 1)
    return jnp.where(lax.shift_right_logical(col, shift) == row, 1.0, 0.0).astype(BF16)


def call(kernel, out_shape, operands, scratch=(), flops=0, vmem=24, specs=None, outs=VMEM):
    specs = specs or [VMEM] * len(operands)
    operands = [
        pltpu.with_memory_space_constraint(x, pltpu.HBM) if spec is HBM else x
        for x, spec in zip(operands, specs)
    ]
    moved = sum(x.size * x.dtype.itemsize for x in operands)
    return pl.pallas_call(
        kernel,
        out_shape=out_shape,
        in_specs=specs,
        out_specs=jax.tree.map(lambda _: outs, out_shape),
        scratch_shapes=list(scratch),
        compiler_params=pltpu.CompilerParams(vmem_limit_bytes=vmem << 20),
        cost_estimate=pl.CostEstimate(flops=flops, bytes_accessed=moved, transcendentals=0),
    )(*operands)


def by_mask(refs):
    return [refs[ORDER.index(mask)] for mask in range(len(refs))]


def level_pool(rows, level):
    row = lax.broadcasted_iota(jnp.int32, (rows, BLOCK), 0)
    col = lax.broadcasted_iota(jnp.int32, (rows, BLOCK), 1)
    return jnp.where(lax.shift_right_logical(col, level) == row, 1.0, 0.0).astype(BF16)


def col_block(low, mask, width):
    return pl.ds(pl.multiple_of((low ^ mask) * width, width), width)


def piece_rows(level):
    return max(16, BLOCK >> level)


def token_kernel(slots, at_ref, k_hbm, v_hbm, *refs):
    chunk_refs, (k_ref, v_ref, sems) = refs[:slots], refs[slots:]
    low = at_ref[0]
    tok, width = BLOCK, chunk_refs[0].shape[1]
    held = (k_ref, v_ref)
    copies = [
        pltpu.make_async_copy(source, held[place], sems.at[place])
        for place, source in enumerate((k_hbm, v_hbm))
    ]
    for copy in copies:
        copy.start()
    for place, source in enumerate(held):
        copies[place].wait()
        for mask in range(slots):
            rows = slice(place * tok, place * tok + tok)
            chunk_refs[mask][rows, :] = source[:, col_block(low, mask, width)]


def query_kernel(slots, at_ref, q_ref, mine_ref, w_ref, other_ref, *refs):
    chunk_refs, grad_ref = refs[:slots], refs[slots]
    low, core = at_ref[0], at_ref[1]
    tok, half = mine_ref.shape
    width = chunk_refs[0].shape[1]
    first = pl.multiple_of(core * half, half)
    second = pl.multiple_of((1 - core) * half, half)
    total = mm(mine_ref[...], w_ref[pl.ds(first, half), :])
    total += mm(other_ref[...], w_ref[pl.ds(second, half), :])
    grad_ref[...] = total.astype(BF16)
    for mask in range(slots):
        cols = col_block(low, mask, width)
        chunk_refs[mask][0:tok, :] = q_ref[:, cols]
        chunk_refs[mask][tok:, :] = grad_ref[:, cols]


def coarse_kernel(slots, levels, *refs):
    in_refs, piece_refs = by_mask(refs[:slots]), refs[slots:]
    tok = BLOCK
    for level, piece in zip(levels, piece_refs):
        rows = piece_rows(level)
        pool = level_pool(rows, level)
        for slab in range(slots):
            at = slab * rows
            keys = mm(pool, in_refs[slab][0:tok, :]) * (1.0 / (1 << level))
            piece[at : at + rows, :] = keys.astype(BF16)
            at = (slots + slab) * rows
            piece[at : at + rows, :] = mm(pool, in_refs[slab][tok:, :]).astype(BF16)


def attend_kernel(slots, far_levels, entries, *refs):
    key_refs, query_refs = by_mask(refs[:slots]), by_mask(refs[slots : 2 * slots])
    refs = refs[2 * slots :]
    count = len(entries)
    got_refs, far_refs, refs = refs[:count], refs[count : 2 * count], refs[2 * count :]
    kl_ref, vl_ref, q_all, g_all, prob_ref, grad_ref, sum_ref, fk_ref, fv_ref = refs
    tok = BLOCK
    pairs = slots // 2
    inv_scale = 1.0 / math.sqrt(HDIM)
    to_exp2 = inv_scale * math.log2(math.e)
    near, far = 2 * tok, 3 * tok
    for slab in range(slots):
        pair, row = slab // 2, (slab % 2) * tok
        q_all[pair, row : row + tok, :] = query_refs[slab][0:tok, :]
        g_all[pair, row : row + tok, :] = query_refs[slab][tok:, :]
        kl_ref[pair, row : row + tok, :] = key_refs[slab][0:tok, :]
        vl_ref[pair, row : row + tok, :] = key_refs[slab][tok:, :]
    for (place, part, rows), got_ref in zip(entries, got_refs):
        for slab in range(slots):
            spot = far + place * BLOCK + 32 * slab + part * rows
            for kind, list_ref in enumerate((kl_ref, vl_ref)):
                at = (kind * slots + slab) * rows
                for pair in range(pairs):
                    list_ref[pair, spot : spot + rows, :] = got_ref[at : at + rows, :]
    pool = pool_matrix(BLOCK, 1)
    for pair in range(pairs):
        kl_ref[pair ^ 1, near:far, :] = (mm(pool, kl_ref[pair, 0:near, :]) * 0.5).astype(BF16)
        vl_ref[pair ^ 1, near:far, :] = mm(pool, vl_ref[pair, 0:near, :]).astype(BF16)
    for pair in range(pairs):
        for head in range(2):
            lanes = slice(head * HDIM, head * HDIM + HDIM)
            queries, grads = q_all[pair, :, lanes], g_all[pair, :, lanes]
            keys, values = kl_ref[pair, :, lanes], vl_ref[pair, :, lanes]
            scores = mm_cols(queries, keys)
            prob_grad = mm_cols(grads, values)
            top = jnp.max(scores, axis=1, keepdims=True)
            raised = jnp.exp2((scores - top) * to_exp2)
            inverse = 1.0 / jnp.sum(raised, axis=1, keepdims=True)
            centre = jnp.sum(raised * prob_grad, axis=1, keepdims=True) * inverse
            raised_low = raised.astype(BF16)
            score_grad = (raised * (prob_grad - centre)).astype(BF16)
            queries = (queries.astype(F32) * (inverse * inv_scale)).astype(BF16)
            grads = (grads.astype(F32) * inverse).astype(BF16)
            prob_ref[2 * pair + head] = raised_low
            grad_ref[2 * pair + head] = score_grad
            sum_ref[2 * pair + head] = jnp.broadcast_to(inverse, (near, HDIM))
            q_all[pair, :, lanes] = queries
            g_all[pair, :, lanes] = grads
            key_terms = mm_rows(score_grad[:, far:], queries)
            value_terms = mm_rows(raised_low[:, far:], grads)
            if pair == 0:
                fk_ref[:, lanes] = key_terms
                fv_ref[:, lanes] = value_terms
            else:
                fk_ref[:, lanes] += key_terms
                fv_ref[:, lanes] += value_terms
    for (place, part, rows), out_ref in zip(entries, far_refs):
        for kind, total in enumerate((fk_ref, fv_ref)):
            for slab in range(slots):
                start = place * BLOCK + 32 * slab + part * rows
                at = (kind * slots + slab) * rows
                out_ref[at : at + rows, :] = total[start : start + rows, :].astype(BF16)


def reduce_kernel(slots, kl_ref, vl_ref, prob_ref, grad_ref, sum_ref, *home_refs):
    tok = BLOCK
    inv_scale = 1.0 / math.sqrt(HDIM)
    for pair in range(slots // 2):
        for head in range(2):
            lanes = slice(head * HDIM, head * HDIM + HDIM)
            unit = 2 * pair + head
            inverse = sum_ref[unit]
            attended = (mm(prob_ref[unit], vl_ref[pair, :, lanes]) * inverse).astype(BF16)
            query_grad = mm(grad_ref[unit], kl_ref[pair, :, lanes]) * (inverse * inv_scale)
            query_grad = query_grad.astype(BF16)
            for side in range(2):
                rows = slice(side * tok, side * tok + tok)
                home_refs[2 * pair + side][0:tok, lanes] = attended[rows]
                home_refs[2 * pair + side][tok:, lanes] = query_grad[rows]


def local_kernel(slots, q_all, g_all, prob_ref, grad_ref, dk_ref, dv_ref, ck_ref, cv_ref):
    tok = BLOCK
    pairs = slots // 2
    near, far = 2 * tok, 3 * tok
    for pair in range(pairs):
        for head in range(2):
            lanes = slice(head * HDIM, head * HDIM + HDIM)
            unit = 2 * pair + head
            key_terms = mm_rows(grad_ref[unit, :, 0:far], q_all[pair, :, lanes])
            value_terms = mm_rows(prob_ref[unit, :, 0:far], g_all[pair, :, lanes])
            for terms, local, level1 in (
                (key_terms, dk_ref, ck_ref),
                (value_terms, dv_ref, cv_ref),
            ):
                local[pair * near : pair * near + near, lanes] = terms[0:near]
                level1[pair ^ 1, :, lanes] = terms[near:].astype(BF16)
    pool = pool_matrix(BLOCK, 1)
    for pair in range(pairs):
        rows = slice(pair * near, pair * near + near)
        dk_ref[rows, :] += mm_rows(pool, ck_ref[pair]) * 0.5
        dv_ref[rows, :] += mm_rows(pool, cv_ref[pair])


def merge_kernel(slots, levels, dk_ref, dv_ref, *refs):
    far_refs, out_refs = refs[: len(levels)], refs[len(levels) :]
    tok = BLOCK
    for slab in range(slots):
        rows = slice(slab * tok, slab * tok + tok)
        key_sum, value_sum = dk_ref[rows, :], dv_ref[rows, :]
        for level, far_ref in zip(levels, far_refs):
            count = piece_rows(level)
            pool = level_pool(count, level)
            mine = far_ref[slab * count : slab * count + count, :]
            key_sum += mm_rows(pool, mine) * (1.0 / (1 << level))
            at = (slots + slab) * count
            value_sum += mm_rows(pool, far_ref[at : at + count, :])
        out_refs[slab][0:tok, :] = key_sum.astype(BF16)
        out_refs[slab][tok:, :] = value_sum.astype(BF16)


def send_kernel(slots, at_ref, w_ref, *refs):
    in_refs, att_ref, send_refs = by_mask(refs[:slots]), refs[slots], refs[slots + 1 :]
    low, core = at_ref[0], at_ref[1]
    tok, half = att_ref.shape
    width = in_refs[0].shape[1]
    for mask in range(slots):
        att_ref[:, col_block(low, mask, width)] = in_refs[mask][0:tok, :]
    part = half // len(send_refs)
    for place, send_ref in enumerate(send_refs):
        other = pl.multiple_of((1 - core) * half + place * part, part)
        send_ref[...] = mm_cols(att_ref[...], w_ref[pl.ds(other, part), :]).astype(BF16)


def keep_kernel(at_ref, w_ref, att_ref, keep_ref):
    half = att_ref.shape[1]
    first = pl.multiple_of(at_ref[1] * half, half)
    keep_ref[...] = mm_cols(att_ref[...], w_ref[pl.ds(first, half), :])


def finish_kernel(slots, at_ref, keep_ref, *refs):
    home_refs, last_refs = by_mask(refs[:slots]), by_mask(refs[slots : 2 * slots])
    got_refs, refs = refs[2 * slots : -9], refs[-9:]
    hbm_refs, held_refs, sems = refs[:4], refs[4:8], refs[8]
    low = at_ref[0]
    tok, width = BLOCK, home_refs[0].shape[1]
    copies = [
        pltpu.make_async_copy(held_refs[place], hbm_refs[place], sems.at[place])
        for place in range(4)
    ]
    for place, (in_refs, start) in enumerate(((home_refs, tok), (last_refs, 0), (last_refs, tok))):
        for mask in range(slots):
            cols = col_block(low, mask, width)
            held_refs[place][:, cols] = in_refs[mask][start : start + tok, :]
        copies[place].start()
    part = got_refs[0].shape[1]
    for place, got_ref in enumerate(got_refs):
        cols = slice(place * part, place * part + part)
        held_refs[3][:, cols] = (keep_ref[:, cols] + got_ref[...].astype(F32)).astype(BF16)
    copies[3].start()
    for copy in copies:
        copy.wait()


def straight(levels, slots):
    return all((slots << place) * 4 <= 32 for place in range(len(levels)))


def far_entries(levels, slots):
    entries, masks = [], []
    for place, level in enumerate(levels):
        if not straight(levels, slots):
            entries.append((place, 0, 32))
            continue
        for part in range(1 << place):
            entries.append((place, part, BLOCK >> level))
            masks.append(1 << level ^ part * slots)
    return entries, masks


def gather_far(pieces, levels, slots):
    width = pieces[0].shape[1]
    if straight(levels, slots):
        entries, masks = far_entries(levels, slots)
        return [swap_seq(pieces[entry[0]], mask) for entry, mask in zip(entries, masks)]
    held = {}
    for place, level in enumerate(levels):
        block = pieces[place].reshape(2 * slots, piece_rows(level), width)
        held[level] = block[:, None, : BLOCK >> level]
    found = []
    for step in levels:
        sent = [held[level].reshape(-1, width) for level in levels if level >= step]
        got = swap_seq(jnp.concatenate(sent, axis=0), 1 << step)
        first = 0
        for level in levels:
            if level < step:
                continue
            count = held[level].size // width
            part = got[first : first + count].reshape(held[level].shape)
            first += count
            if level == step:
                found.append(part.reshape(-1, width))
            else:
                held[level] = jnp.concatenate([held[level], part], axis=1)
    return found


def scatter_far(packed, levels, slots):
    width = packed[0].shape[1]
    if straight(levels, slots):
        entries, masks = far_entries(levels, slots)
        shares = [swap_seq(array, mask) for array, mask in zip(packed, masks)]
        return shares, [levels[entry[0]] for entry in entries]
    blocks = {}
    for place, level in enumerate(levels):
        rows = BLOCK >> level
        blocks[level] = packed[place].reshape(2 * slots, 32 // rows, rows, width)
    ready = {}
    for step in reversed(levels):
        sent, kept = [blocks[step].reshape(-1, width)], {}
        for level in levels:
            if level > step:
                size = ready[level].shape[1] // 2
                kept[level] = ready[level][:, :size]
                sent.append(ready[level][:, size:].astype(BF16).reshape(-1, width))
        got = swap_seq(jnp.concatenate(sent, axis=0), 1 << step)
        first = blocks[step].size // width
        ready[step] = got[0:first].reshape(blocks[step].shape)
        for level in kept:
            count = kept[level].size // width
            part = got[first : first + count].reshape(kept[level].shape)
            first += count
            ready[level] = kept[level].astype(F32) + part.astype(F32)
    shares = []
    for level in levels:
        share = ready[level].astype(BF16).reshape(2 * slots, -1, width)
        pad = piece_rows(level) - share.shape[1]
        if pad:
            share = jnp.pad(share, ((0, 0), (0, pad), (0, 0)))
        shares.append(share.reshape(-1, width))
    return shares, list(levels)


def on_device(queries, key_tokens, value_tokens, out_weight, output_grad):
    tok, columns = queries.shape
    heads = columns // HDIM
    slots = heads // 2
    width = columns // slots
    local_levels = slots.bit_length() - 1
    level_count = lax.axis_size("seq").bit_length() - 1
    far = list(range(local_levels, level_count))
    list_rows = 3 * tok + BLOCK * len(far)
    entries, _ = far_entries(far, slots)
    place = jnp.stack([lax.axis_index("seq") & (slots - 1), lax.axis_index("head")])
    place = place.astype(jnp.int32)

    def shape(dims, dtype=BF16):
        return jax.ShapeDtypeStruct(dims, dtype)

    def over(rows):
        return [shape((rows, width))] * slots

    def exchange(chunks):
        moved = [chunks[0]] + [swap_seq(chunks[mask], mask) for mask in range(1, slots)]
        return [moved[mask] for mask in ORDER]

    chunks = call(
        lambda *refs: token_kernel(slots, *refs),
        over(2 * tok),
        (place, key_tokens, value_tokens),
        scratch=[pltpu.VMEM((tok, columns), BF16)] * 2 + [pltpu.SemaphoreType.DMA((2,))],
        flops=6 * 10**9,
        specs=[SMEM] + [HBM] * 2,
        vmem=8,
    )
    keys = exchange(chunks)
    later, output_grad, *_ = lax.optimization_barrier((place, output_grad, *chunks))
    other_grad = swap_head(output_grad)
    chunks = call(
        lambda *refs: query_kernel(slots, *refs),
        over(2 * tok),
        [later, queries, output_grad, out_weight, other_grad],
        scratch=[pltpu.VMEM((tok, columns), BF16)],
        flops=6 * 10**9,
        specs=[SMEM] + [VMEM] * 4,
        vmem=16,
    )
    asked = exchange(chunks)
    sources, *_ = lax.optimization_barrier((keys, asked[1]))
    pieces = call(
        lambda *refs: coarse_kernel(slots, far, *refs),
        [shape((2 * slots * piece_rows(level), width)) for level in far],
        sources,
        vmem=8,
    )
    far_got = gather_far(pieces, far, slots)
    pairs = slots // 2
    made = call(
        lambda *refs: attend_kernel(slots, len(far), entries, *refs),
        [shape((2 * slots * rows, width)) for _, _, rows in entries]
        + [shape((pairs, list_rows, width))] * 2
        + [shape((pairs, 2 * tok, width))] * 2
        + [shape((slots, 2 * tok, list_rows))] * 2
        + [shape((slots, 2 * tok, HDIM), F32)],
        keys + asked + far_got,
        scratch=[pltpu.VMEM((BLOCK * len(far), width), F32)] * 2,
        flops=6 * heads * tok * list_rows * HDIM,
    )
    shares, share_levels = scatter_far(made[: len(entries)], far, slots)
    key_list, value_list, asked, grads, probs, score_grads, sums = made[len(entries) :]
    made = call(
        lambda *refs: reduce_kernel(slots, *refs),
        over(2 * tok),
        [key_list, value_list, probs, score_grads, sums],
        flops=6 * 10**9,
        vmem=16,
    )
    key_sum, value_sum = call(
        lambda *refs: local_kernel(slots, *refs),
        [shape((slots * tok, width), F32)] * 2,
        [asked, grads, probs, score_grads],
        scratch=[pltpu.VMEM((pairs, BLOCK, width), BF16)] * 2,
        flops=4 * heads * tok * list_rows * HDIM,
        vmem=16,
    )
    made = list(made)
    late = ORDER[-1]
    made[late], key_sum, *shares = lax.optimization_barrier((made[late], key_sum, *shares))
    home = exchange(made)
    chunks = call(
        lambda *refs: merge_kernel(slots, share_levels, *refs),
        over(2 * tok),
        [key_sum, value_sum] + shares,
        vmem=8,
    )
    home, _ = lax.optimization_barrier((home, chunks))
    chunks = list(chunks)
    last = exchange(chunks)
    wide = shape((tok, columns))
    attended, *send = call(
        lambda *refs: send_kernel(slots, *refs),
        [wide] + [shape((tok, columns // 2))] * 2,
        [place, out_weight] + home,
        flops=2 * tok * columns * columns,
        specs=[SMEM] + [VMEM] * (1 + slots),
        vmem=16,
    )
    got = [swap_head(part) for part in send]
    keep = call(
        keep_kernel,
        shape((tok, columns), F32),
        [place, out_weight, attended],
        flops=4 * 10**9,
        specs=[SMEM, VMEM, VMEM],
        vmem=16,
    )
    query_grad, key_grad, value_grad, output = call(
        lambda *refs: finish_kernel(slots, *refs),
        [wide] * 4,
        [place, keep] + home + last + got,
        scratch=[pltpu.VMEM((tok, columns), BF16)] * 4 + [pltpu.SemaphoreType.DMA((4,))],
        specs=[SMEM] + [VMEM] * (1 + 2 * slots + len(got)),
        outs=HBM,
        vmem=8,
    )
    return output, query_grad, key_grad, value_grad


def solution(mesh):
    placed = P("seq", "head")
    return jax.shard_map(
        on_device,
        mesh=mesh,
        in_specs=(placed, placed, placed, P(None, "head"), placed),
        out_specs=(placed, placed, placed, placed),
        check_vma=False,
    )
```

```python
import math

import jax
import jax.numpy as jnp
from jax import lax
from jax.experimental import pallas as pl
from jax.experimental.pallas import tpu as pltpu
from jax.sharding import PartitionSpec as P

HDIM = 128
ORDER = (0, 1, 2, 3)
BLOCK = 128
BF16 = jnp.bfloat16
F32 = jnp.float32
VMEM = pl.BlockSpec(memory_space=pltpu.VMEM)
SMEM = pl.BlockSpec(memory_space=pltpu.SMEM)
HBM = pl.BlockSpec(memory_space=pltpu.HBM)


def swap_seq(array, mask):
    return lax.ppermute(array, "seq", [(i, i ^ mask) for i in range(lax.axis_size("seq"))])


def swap_head(array):
    return lax.ppermute(array, "head", [(0, 1), (1, 0)])


def mm(left, right):
    return jnp.dot(left, right, preferred_element_type=F32)


def mm_cols(left, right):
    return lax.dot_general(left, right, (((1,), (1,)), ((), ())), preferred_element_type=F32)


def mm_rows(left, right):
    return lax.dot_general(left, right, (((0,), (0,)), ((), ())), preferred_element_type=F32)


def pool_matrix(rows, shift):
    shape = (rows, rows << shift)
    row = lax.broadcasted_iota(jnp.int32, shape, 0)
    col = lax.broadcasted_iota(jnp.int32, shape, 1)
    return jnp.where(lax.shift_right_logical(col, shift) == row, 1.0, 0.0).astype(BF16)


def call(kernel, out_shape, operands, scratch=(), flops=0, vmem=24, specs=None, outs=VMEM, free=False):
    specs = specs or [VMEM] * len(operands)
    operands = [
        pltpu.with_memory_space_constraint(x, pltpu.HBM) if spec is HBM else x
        for x, spec in zip(operands, specs)
    ]
    moved = 0 if free else sum(x.size * x.dtype.itemsize for x in operands)
    return pl.pallas_call(
        kernel,
        out_shape=out_shape,
        in_specs=specs,
        out_specs=jax.tree.map(lambda _: outs, out_shape),
        scratch_shapes=list(scratch),
        compiler_params=pltpu.CompilerParams(vmem_limit_bytes=vmem << 20),
        cost_estimate=pl.CostEstimate(flops=flops, bytes_accessed=moved, transcendentals=0),
    )(*operands)


def by_mask(refs):
    return [refs[ORDER.index(mask)] for mask in range(len(refs))]


def level_pool(rows, level):
    row = lax.broadcasted_iota(jnp.int32, (rows, BLOCK), 0)
    col = lax.broadcasted_iota(jnp.int32, (rows, BLOCK), 1)
    return jnp.where(lax.shift_right_logical(col, level) == row, 1.0, 0.0).astype(BF16)


def col_block(low, mask, width):
    return pl.ds(pl.multiple_of((low ^ mask) * width, width), width)


def piece_rows(level):
    return max(16, BLOCK >> level)


def load_kernel(*refs):
    count = len(refs) // 2
    sems = refs[-1]
    copies = [
        pltpu.make_async_copy(refs[place], refs[count + place], sems.at[place])
        for place in range(count)
    ]
    for copy in copies:
        copy.start()
    for copy in copies:
        copy.wait()


def token_kernel(slots, at_ref, k_ref, v_ref, *chunk_refs):
    low = at_ref[0]
    tok, width = BLOCK, chunk_refs[0].shape[1]
    for mask in range(slots):
        cols = col_block(low, mask, width)
        chunk_refs[mask][0:tok, :] = k_ref[:, cols]
        chunk_refs[mask][tok:, :] = v_ref[:, cols]


def query_kernel(slots, at_ref, q_ref, mine_ref, w_ref, other_ref, *refs):
    chunk_refs, grad_ref = refs[:slots], refs[slots]
    low, core = at_ref[0], at_ref[1]
    tok, half = mine_ref.shape
    width = chunk_refs[0].shape[1]
    first = pl.multiple_of(core * half, half)
    second = pl.multiple_of((1 - core) * half, half)
    total = mm(mine_ref[...], w_ref[pl.ds(first, half), :])
    total += mm(other_ref[...], w_ref[pl.ds(second, half), :])
    grad_ref[...] = total.astype(BF16)
    for mask in range(slots):
        cols = col_block(low, mask, width)
        chunk_refs[mask][0:tok, :] = q_ref[:, cols]
        chunk_refs[mask][tok:, :] = grad_ref[:, cols]


def coarse_kernel(slots, levels, *refs):
    in_refs, piece_refs = by_mask(refs[:slots]), refs[slots:]
    tok = BLOCK
    for level, piece in zip(levels, piece_refs):
        rows = piece_rows(level)
        pool = level_pool(rows, level)
        for slab in range(slots):
            at = slab * rows
            keys = mm(pool, in_refs[slab][0:tok, :]) * (1.0 / (1 << level))
            piece[at : at + rows, :] = keys.astype(BF16)
            at = (slots + slab) * rows
            piece[at : at + rows, :] = mm(pool, in_refs[slab][tok:, :]).astype(BF16)


def attend_kernel(slots, far_levels, entries, *refs):
    key_refs, query_refs = by_mask(refs[:slots]), by_mask(refs[slots : 2 * slots])
    refs = refs[2 * slots :]
    count = len(entries)
    got_refs, far_refs, refs = refs[:count], refs[count : 2 * count], refs[2 * count :]
    kl_ref, vl_ref, q_all, g_all, prob_ref, grad_ref, sum_ref, fk_ref, fv_ref = refs
    tok = BLOCK
    pairs = slots // 2
    inv_scale = 1.0 / math.sqrt(HDIM)
    to_exp2 = inv_scale * math.log2(math.e)
    near, far = 2 * tok, 3 * tok
    for slab in range(slots):
        pair, row = slab // 2, (slab % 2) * tok
        q_all[pair, row : row + tok, :] = query_refs[slab][0:tok, :]
        g_all[pair, row : row + tok, :] = query_refs[slab][tok:, :]
        kl_ref[pair, row : row + tok, :] = key_refs[slab][0:tok, :]
        vl_ref[pair, row : row + tok, :] = key_refs[slab][tok:, :]
    for (place, part, rows), got_ref in zip(entries, got_refs):
        for slab in range(slots):
            spot = far + place * BLOCK + 32 * slab + part * rows
            for kind, list_ref in enumerate((kl_ref, vl_ref)):
                at = (kind * slots + slab) * rows
                for pair in range(pairs):
                    list_ref[pair, spot : spot + rows, :] = got_ref[at : at + rows, :]
    pool = pool_matrix(BLOCK, 1)
    for pair in range(pairs):
        kl_ref[pair ^ 1, near:far, :] = (mm(pool, kl_ref[pair, 0:near, :]) * 0.5).astype(BF16)
        vl_ref[pair ^ 1, near:far, :] = mm(pool, vl_ref[pair, 0:near, :]).astype(BF16)
    for pair in range(pairs):
        for head in range(2):
            lanes = slice(head * HDIM, head * HDIM + HDIM)
            queries, grads = q_all[pair, :, lanes], g_all[pair, :, lanes]
            keys, values = kl_ref[pair, :, lanes], vl_ref[pair, :, lanes]
            scores = mm_cols(queries, keys)
            prob_grad = mm_cols(grads, values)
            top = jnp.max(scores, axis=1, keepdims=True)
            raised = jnp.exp2((scores - top) * to_exp2)
            inverse = 1.0 / jnp.sum(raised, axis=1, keepdims=True)
            centre = jnp.sum(raised * prob_grad, axis=1, keepdims=True) * inverse
            raised_low = raised.astype(BF16)
            score_grad = (raised * (prob_grad - centre)).astype(BF16)
            queries = (queries.astype(F32) * (inverse * inv_scale)).astype(BF16)
            grads = (grads.astype(F32) * inverse).astype(BF16)
            prob_ref[2 * pair + head] = raised_low
            grad_ref[2 * pair + head] = score_grad
            sum_ref[2 * pair + head] = jnp.broadcast_to(inverse, (near, HDIM))
            q_all[pair, :, lanes] = queries
            g_all[pair, :, lanes] = grads
            key_terms = mm_rows(score_grad[:, far:], queries)
            value_terms = mm_rows(raised_low[:, far:], grads)
            if pair == 0:
                fk_ref[:, lanes] = key_terms
                fv_ref[:, lanes] = value_terms
            else:
                fk_ref[:, lanes] += key_terms
                fv_ref[:, lanes] += value_terms
    for (place, part, rows), out_ref in zip(entries, far_refs):
        for kind, total in enumerate((fk_ref, fv_ref)):
            for slab in range(slots):
                start = place * BLOCK + 32 * slab + part * rows
                at = (kind * slots + slab) * rows
                out_ref[at : at + rows, :] = total[start : start + rows, :].astype(BF16)


def reduce_kernel(slots, kl_ref, vl_ref, prob_ref, grad_ref, sum_ref, *home_refs):
    tok = BLOCK
    inv_scale = 1.0 / math.sqrt(HDIM)
    for pair in range(slots // 2):
        for head in range(2):
            lanes = slice(head * HDIM, head * HDIM + HDIM)
            unit = 2 * pair + head
            inverse = sum_ref[unit]
            attended = (mm(prob_ref[unit], vl_ref[pair, :, lanes]) * inverse).astype(BF16)
            query_grad = mm(grad_ref[unit], kl_ref[pair, :, lanes]) * (inverse * inv_scale)
            query_grad = query_grad.astype(BF16)
            for side in range(2):
                rows = slice(side * tok, side * tok + tok)
                home_refs[2 * pair + side][0:tok, lanes] = attended[rows]
                home_refs[2 * pair + side][tok:, lanes] = query_grad[rows]


def local_kernel(slots, q_all, g_all, prob_ref, grad_ref, dk_ref, dv_ref, ck_ref, cv_ref):
    tok = BLOCK
    pairs = slots // 2
    near, far = 2 * tok, 3 * tok
    for pair in range(pairs):
        for head in range(2):
            lanes = slice(head * HDIM, head * HDIM + HDIM)
            unit = 2 * pair + head
            key_terms = mm_rows(grad_ref[unit, :, 0:far], q_all[pair, :, lanes])
            value_terms = mm_rows(prob_ref[unit, :, 0:far], g_all[pair, :, lanes])
            for terms, local, level1 in (
                (key_terms, dk_ref, ck_ref),
                (value_terms, dv_ref, cv_ref),
            ):
                local[pair * near : pair * near + near, lanes] = terms[0:near]
                level1[pair ^ 1, :, lanes] = terms[near:].astype(BF16)
    pool = pool_matrix(BLOCK, 1)
    for pair in range(pairs):
        rows = slice(pair * near, pair * near + near)
        dk_ref[rows, :] += mm_rows(pool, ck_ref[pair]) * 0.5
        dv_ref[rows, :] += mm_rows(pool, cv_ref[pair])


def merge_kernel(slots, levels, dk_ref, dv_ref, *refs):
    far_refs, out_refs = refs[: len(levels)], refs[len(levels) :]
    tok = BLOCK
    for slab in range(slots):
        rows = slice(slab * tok, slab * tok + tok)
        key_sum, value_sum = dk_ref[rows, :], dv_ref[rows, :]
        for level, far_ref in zip(levels, far_refs):
            count = piece_rows(level)
            pool = level_pool(count, level)
            mine = far_ref[slab * count : slab * count + count, :]
            key_sum += mm_rows(pool, mine) * (1.0 / (1 << level))
            at = (slots + slab) * count
            value_sum += mm_rows(pool, far_ref[at : at + count, :])
        out_refs[slab][0:tok, :] = key_sum.astype(BF16)
        out_refs[slab][tok:, :] = value_sum.astype(BF16)


def flip_kernel(w_ref, out_ref):
    half = out_ref.shape[0]
    for place in range(w_ref.shape[0] // half):
        rows = slice(place * half, place * half + half)
        out_ref[:, rows] = w_ref[rows, :].T


def send_kernel(slots, at_ref, w_ref, *refs):
    in_refs, att_ref, send_refs = by_mask(refs[:slots]), refs[slots], refs[slots + 1 :]
    low, core = at_ref[0], at_ref[1]
    tok, half = att_ref.shape
    width = in_refs[0].shape[1]
    for mask in range(slots):
        att_ref[:, col_block(low, mask, width)] = in_refs[mask][0:tok, :]
    part = half // len(send_refs)
    for place, send_ref in enumerate(send_refs):
        other = pl.multiple_of((1 - core) * half + place * part, part)
        send_ref[...] = mm(att_ref[...], w_ref[:, pl.ds(other, part)]).astype(BF16)


def keep_kernel(slots, at_ref, w_ref, att_ref, *refs):
    home_refs, (keep_ref, dq_ref) = by_mask(refs[:slots]), refs[slots:]
    tok, half = att_ref.shape
    width = home_refs[0].shape[1]
    for mask in range(slots):
        dq_ref[:, col_block(at_ref[0], mask, width)] = home_refs[mask][tok:, :]
    first = pl.multiple_of(at_ref[1] * half, half)
    keep_ref[...] = mm(att_ref[...], w_ref[:, pl.ds(first, half)])


def add_kernel(keep_ref, *refs):
    got_refs, out_ref = refs[:-1], refs[-1]
    part = got_refs[0].shape[1]
    for place, got_ref in enumerate(got_refs):
        cols = slice(place * part, place * part + part)
        out_ref[:, cols] = (keep_ref[:, cols] + got_ref[...].astype(F32)).astype(BF16)


def finish_kernel(slots, at_ref, out_ref, dq_ref, *refs):
    last_refs, refs = by_mask(refs[:slots]), refs[slots:]
    hbm_refs, (dk_ref, dv_ref, sems) = refs[:4], refs[4:]
    tok, width = BLOCK, last_refs[0].shape[1]
    copies = [
        pltpu.make_async_copy(source, hbm_refs[place], sems.at[place])
        for place, source in enumerate((out_ref, dq_ref, dk_ref, dv_ref))
    ]
    copies[0].start()
    copies[1].start()
    for place, held_ref in enumerate((dk_ref, dv_ref)):
        rows = slice(place * tok, place * tok + tok)
        for mask in range(slots):
            held_ref[:, col_block(at_ref[0], mask, width)] = last_refs[mask][rows, :]
        copies[2 + place].start()
    for copy in copies:
        copy.wait()


def straight(levels, slots):
    return all((slots << place) * 4 <= 32 for place in range(len(levels)))


def far_entries(levels, slots):
    entries, masks = [], []
    for place, level in enumerate(levels):
        if not straight(levels, slots):
            entries.append((place, 0, 32))
            continue
        for part in range(1 << place):
            entries.append((place, part, BLOCK >> level))
            masks.append(1 << level ^ part * slots)
    return entries, masks


def gather_far(pieces, levels, slots):
    width = pieces[0].shape[1]
    if straight(levels, slots):
        entries, masks = far_entries(levels, slots)
        return [swap_seq(pieces[entry[0]], mask) for entry, mask in zip(entries, masks)]
    held = {}
    for place, level in enumerate(levels):
        block = pieces[place].reshape(2 * slots, piece_rows(level), width)
        held[level] = block[:, None, : BLOCK >> level]
    found = []
    for step in levels:
        sent = [held[level].reshape(-1, width) for level in levels if level >= step]
        got = swap_seq(jnp.concatenate(sent, axis=0), 1 << step)
        first = 0
        for level in levels:
            if level < step:
                continue
            count = held[level].size // width
            part = got[first : first + count].reshape(held[level].shape)
            first += count
            if level == step:
                found.append(part.reshape(-1, width))
            else:
                held[level] = jnp.concatenate([held[level], part], axis=1)
    return found


def scatter_far(packed, levels, slots):
    width = packed[0].shape[1]
    if straight(levels, slots):
        entries, masks = far_entries(levels, slots)
        shares = [swap_seq(array, mask) for array, mask in zip(packed, masks)]
        return shares, [levels[entry[0]] for entry in entries]
    blocks = {}
    for place, level in enumerate(levels):
        rows = BLOCK >> level
        blocks[level] = packed[place].reshape(2 * slots, 32 // rows, rows, width)
    ready = {}
    for step in reversed(levels):
        sent, kept = [blocks[step].reshape(-1, width)], {}
        for level in levels:
            if level > step:
                size = ready[level].shape[1] // 2
                kept[level] = ready[level][:, :size]
                sent.append(ready[level][:, size:].astype(BF16).reshape(-1, width))
        got = swap_seq(jnp.concatenate(sent, axis=0), 1 << step)
        first = blocks[step].size // width
        ready[step] = got[0:first].reshape(blocks[step].shape)
        for level in kept:
            count = kept[level].size // width
            part = got[first : first + count].reshape(kept[level].shape)
            first += count
            ready[level] = kept[level].astype(F32) + part.astype(F32)
    shares = []
    for level in levels:
        share = ready[level].astype(BF16).reshape(2 * slots, -1, width)
        pad = piece_rows(level) - share.shape[1]
        if pad:
            share = jnp.pad(share, ((0, 0), (0, pad), (0, 0)))
        shares.append(share.reshape(-1, width))
    return shares, list(levels)


def on_device(queries, key_tokens, value_tokens, out_weight, output_grad):
    tok, columns = queries.shape
    heads = columns // HDIM
    slots = heads // 2
    width = columns // slots
    local_levels = slots.bit_length() - 1
    level_count = lax.axis_size("seq").bit_length() - 1
    far = list(range(local_levels, level_count))
    list_rows = 3 * tok + BLOCK * len(far)
    entries, _ = far_entries(far, slots)
    place = jnp.stack([lax.axis_index("seq") & (slots - 1), lax.axis_index("head")])
    place = place.astype(jnp.int32)

    def shape(dims, dtype=BF16):
        return jax.ShapeDtypeStruct(dims, dtype)

    def over(rows):
        return [shape((rows, width))] * slots

    def exchange(chunks):
        moved = [chunks[0]] + [swap_seq(chunks[mask], mask) for mask in range(1, slots)]
        return [moved[mask] for mask in ORDER]

    held = call(
        load_kernel,
        [shape((tok, columns))] * 2,
        [key_tokens, value_tokens],
        scratch=[pltpu.SemaphoreType.DMA((2,))],
        specs=[HBM] * 2,
        vmem=8,
    )
    chunks = call(
        lambda *refs: token_kernel(slots, *refs),
        over(2 * tok),
        [place] + list(held),
        flops=6 * 10**9,
        specs=[SMEM] + [VMEM] * 2,
        vmem=8,
    )
    keys = exchange(chunks)
    later, *_ = lax.optimization_barrier((place, *chunks))
    other_grad = swap_head(output_grad)
    chunks = call(
        lambda *refs: query_kernel(slots, *refs),
        over(2 * tok),
        [later, queries, output_grad, out_weight, other_grad],
        scratch=[pltpu.VMEM((tok, columns), BF16)],
        flops=6 * 10**9,
        specs=[SMEM] + [VMEM] * 4,
        vmem=16,
    )
    asked = exchange(chunks)
    flipped = call(
        flip_kernel,
        shape(out_weight.shape[::-1]),
        [out_weight],
        vmem=24,
        free=True,
    )
    sources, flipped, *_ = lax.optimization_barrier((keys, flipped, asked[1]))
    pieces = call(
        lambda *refs: coarse_kernel(slots, far, *refs),
        [shape((2 * slots * piece_rows(level), width)) for level in far],
        sources,
        vmem=8,
    )
    far_got = gather_far(pieces, far, slots)
    pairs = slots // 2
    made = call(
        lambda *refs: attend_kernel(slots, len(far), entries, *refs),
        [shape((2 * slots * rows, width)) for _, _, rows in entries]
        + [shape((pairs, list_rows, width))] * 2
        + [shape((pairs, 2 * tok, width))] * 2
        + [shape((slots, 2 * tok, list_rows))] * 2
        + [shape((slots, 2 * tok, HDIM), F32)],
        keys + asked + far_got,
        scratch=[pltpu.VMEM((BLOCK * len(far), width), F32)] * 2,
        flops=6 * heads * tok * list_rows * HDIM,
    )
    shares, share_levels = scatter_far(made[: len(entries)], far, slots)
    key_list, value_list, asked, grads, probs, score_grads, sums = made[len(entries) :]
    made = call(
        lambda *refs: reduce_kernel(slots, *refs),
        over(2 * tok),
        [key_list, value_list, probs, score_grads, sums],
        flops=6 * 10**9,
        vmem=16,
    )
    key_sum, value_sum = call(
        lambda *refs: local_kernel(slots, *refs),
        [shape((slots * tok, width), F32)] * 2,
        [asked, grads, probs, score_grads],
        scratch=[pltpu.VMEM((pairs, BLOCK, width), BF16)] * 2,
        flops=4 * heads * tok * list_rows * HDIM,
        vmem=16,
    )
    made = list(made)
    late = ORDER[-1]
    made[late], key_sum, *shares = lax.optimization_barrier((made[late], key_sum, *shares))
    home = exchange(made)
    chunks = call(
        lambda *refs: merge_kernel(slots, share_levels, *refs),
        over(2 * tok),
        [key_sum, value_sum] + shares,
        vmem=8,
    )
    home, _ = lax.optimization_barrier((home, chunks))
    chunks = list(chunks)
    last = exchange(chunks)
    wide = shape((tok, columns))
    attended, *send = call(
        lambda *refs: send_kernel(slots, *refs),
        [wide] + [shape((tok, columns // 2))] * 2,
        [place, flipped] + home,
        flops=2 * tok * columns * columns,
        specs=[SMEM] + [VMEM] * (1 + slots),
        vmem=16,
    )
    got = [swap_head(part) for part in send]
    keep, query_grad = call(
        lambda *refs: keep_kernel(slots, *refs),
        [shape((tok, columns), F32), wide],
        [place, flipped, attended] + home,
        flops=4 * 10**9,
        specs=[SMEM] + [VMEM] * (2 + slots),
        vmem=16,
    )
    output = call(add_kernel, wide, [keep] + got, vmem=8)
    output, query_grad, key_grad, value_grad = call(
        lambda *refs: finish_kernel(slots, *refs),
        [wide] * 4,
        [place, output, query_grad] + last,
        scratch=[pltpu.VMEM((tok, columns), BF16)] * 2 + [pltpu.SemaphoreType.DMA((4,))],
        specs=[SMEM] + [VMEM] * (2 + slots),
        outs=HBM,
        vmem=8,
    )
    return output, query_grad, key_grad, value_grad


def solution(mesh):
    placed = P("seq", "head")
    return jax.shard_map(
        on_device,
        mesh=mesh,
        in_specs=(placed, placed, placed, P(None, "head"), placed),
        out_specs=(placed, placed, placed, placed),
        check_vma=False,
    )
```

```python
import math

import jax
import jax.numpy as jnp
from jax import lax
from jax.experimental import pallas as pl
from jax.experimental.pallas import tpu as pltpu
from jax.sharding import PartitionSpec as P

HDIM = 128
ORDER = (0, 1, 2, 3)
BLOCK = 128
BF16 = jnp.bfloat16
F32 = jnp.float32
VMEM = pl.BlockSpec(memory_space=pltpu.VMEM)
SMEM = pl.BlockSpec(memory_space=pltpu.SMEM)
HBM = pl.BlockSpec(memory_space=pltpu.HBM)


def swap_seq(array, mask):
    return lax.ppermute(array, "seq", [(i, i ^ mask) for i in range(lax.axis_size("seq"))])


def swap_head(array):
    return lax.ppermute(array, "head", [(0, 1), (1, 0)])


def mm(left, right):
    return jnp.dot(left, right, preferred_element_type=F32)


def mm_cols(left, right):
    return lax.dot_general(left, right, (((1,), (1,)), ((), ())), preferred_element_type=F32)


def mm_rows(left, right):
    return lax.dot_general(left, right, (((0,), (0,)), ((), ())), preferred_element_type=F32)


def pool_matrix(rows, shift):
    shape = (rows, rows << shift)
    row = lax.broadcasted_iota(jnp.int32, shape, 0)
    col = lax.broadcasted_iota(jnp.int32, shape, 1)
    return jnp.where(lax.shift_right_logical(col, shift) == row, 1.0, 0.0).astype(BF16)


def call(kernel, out_shape, operands, scratch=(), flops=0, vmem=24, specs=None, outs=VMEM, free=False):
    specs = specs or [VMEM] * len(operands)
    operands = [
        pltpu.with_memory_space_constraint(x, pltpu.HBM) if spec is HBM else x
        for x, spec in zip(operands, specs)
    ]
    moved = 0 if free else sum(x.size * x.dtype.itemsize for x in operands)
    return pl.pallas_call(
        kernel,
        out_shape=out_shape,
        in_specs=specs,
        out_specs=jax.tree.map(lambda _: outs, out_shape),
        scratch_shapes=list(scratch),
        compiler_params=pltpu.CompilerParams(vmem_limit_bytes=vmem << 20),
        cost_estimate=pl.CostEstimate(flops=flops, bytes_accessed=moved, transcendentals=0),
    )(*operands)


def by_mask(refs):
    return [refs[ORDER.index(mask)] for mask in range(len(refs))]


def level_pool(rows, level):
    row = lax.broadcasted_iota(jnp.int32, (rows, BLOCK), 0)
    col = lax.broadcasted_iota(jnp.int32, (rows, BLOCK), 1)
    return jnp.where(lax.shift_right_logical(col, level) == row, 1.0, 0.0).astype(BF16)


def col_block(low, mask, width):
    return pl.ds(pl.multiple_of((low ^ mask) * width, width), width)


def piece_rows(level):
    return max(16, BLOCK >> level)


def load_kernel(*refs):
    count = len(refs) // 2
    sems = refs[-1]
    copies = [
        pltpu.make_async_copy(refs[place], refs[count + place], sems.at[place])
        for place in range(count)
    ]
    for copy in copies:
        copy.start()
    for copy in copies:
        copy.wait()


def token_kernel(slots, at_ref, k_ref, v_ref, *chunk_refs):
    low = at_ref[0]
    tok, width = BLOCK, chunk_refs[0].shape[1]
    for mask in range(slots):
        cols = col_block(low, mask, width)
        chunk_refs[mask][0:tok, :] = k_ref[:, cols]
        chunk_refs[mask][tok:, :] = v_ref[:, cols]


def query_kernel(slots, at_ref, q_ref, mine_ref, w_ref, other_ref, *refs):
    chunk_refs, grad_ref = refs[:slots], refs[slots]
    low, core = at_ref[0], at_ref[1]
    tok, half = mine_ref.shape
    width = chunk_refs[0].shape[1]
    first = pl.multiple_of(core * half, half)
    second = pl.multiple_of((1 - core) * half, half)
    total = mm(mine_ref[...], w_ref[pl.ds(first, half), :])
    total += mm(other_ref[...], w_ref[pl.ds(second, half), :])
    grad_ref[...] = total.astype(BF16)
    for mask in range(slots):
        cols = col_block(low, mask, width)
        chunk_refs[mask][0:tok, :] = q_ref[:, cols]
        chunk_refs[mask][tok:, :] = grad_ref[:, cols]


def coarse_kernel(slots, levels, *refs):
    in_refs, piece_refs = by_mask(refs[:slots]), refs[slots:]
    tok = BLOCK
    for level, piece in zip(levels, piece_refs):
        rows = piece_rows(level)
        pool = level_pool(rows, level)
        for slab in range(slots):
            at = slab * rows
            keys = mm(pool, in_refs[slab][0:tok, :]) * (1.0 / (1 << level))
            piece[at : at + rows, :] = keys.astype(BF16)
            at = (slots + slab) * rows
            piece[at : at + rows, :] = mm(pool, in_refs[slab][tok:, :]).astype(BF16)


def attend_kernel(slots, far_levels, entries, *refs):
    key_refs, query_refs = by_mask(refs[:slots]), by_mask(refs[slots : 2 * slots])
    refs = refs[2 * slots :]
    count = len(entries)
    got_refs, far_refs, refs = refs[:count], refs[count : 2 * count], refs[2 * count :]
    kl_ref, vl_ref, q_all, g_all, prob_ref, grad_ref, sum_ref = refs
    tok = BLOCK
    pairs = slots // 2
    inv_scale = 1.0 / math.sqrt(HDIM)
    to_exp2 = inv_scale * math.log2(math.e)
    near, far = 2 * tok, 3 * tok
    for slab in range(slots):
        pair, row = slab // 2, (slab % 2) * tok
        q_all[pair, row : row + tok, :] = query_refs[slab][0:tok, :]
        g_all[pair, row : row + tok, :] = query_refs[slab][tok:, :]
        kl_ref[pair, row : row + tok, :] = key_refs[slab][0:tok, :]
        vl_ref[pair, row : row + tok, :] = key_refs[slab][tok:, :]
    for (place, part, rows), got_ref in zip(entries, got_refs):
        for slab in range(slots):
            spot = far + place * BLOCK + 32 * slab + part * rows
            for kind, list_ref in enumerate((kl_ref, vl_ref)):
                at = (kind * slots + slab) * rows
                for pair in range(pairs):
                    list_ref[pair, spot : spot + rows, :] = got_ref[at : at + rows, :]
    pool = pool_matrix(BLOCK, 1)
    for pair in range(pairs):
        kl_ref[pair ^ 1, near:far, :] = (mm(pool, kl_ref[pair, 0:near, :]) * 0.5).astype(BF16)
        vl_ref[pair ^ 1, near:far, :] = mm(pool, vl_ref[pair, 0:near, :]).astype(BF16)

    def products(unit):
        pair, head = unit // 2, unit % 2
        lanes = slice(head * HDIM, head * HDIM + HDIM)
        scores = mm_cols(q_all[pair, :, lanes], kl_ref[pair, :, lanes])
        return scores, mm_cols(g_all[pair, :, lanes], vl_ref[pair, :, lanes])

    ready = products(0)
    for unit in range(slots):
        pair, head = unit // 2, unit % 2
        lanes = slice(head * HDIM, head * HDIM + HDIM)
        scores, prob_grad = ready
        if unit + 1 < slots:
            ready = products(unit + 1)
        top = jnp.max(scores, axis=1, keepdims=True)
        raised = jnp.exp2((scores - top) * to_exp2)
        inverse = 1.0 / jnp.sum(raised, axis=1, keepdims=True)
        centre = jnp.sum(raised * prob_grad, axis=1, keepdims=True) * inverse
        prob_ref[unit] = raised.astype(BF16)
        grad_ref[unit] = (raised * (prob_grad - centre)).astype(BF16)
        sum_ref[unit] = jnp.broadcast_to(inverse, (near, HDIM))
        queries = q_all[pair, :, lanes].astype(F32) * (inverse * inv_scale)
        q_all[pair, :, lanes] = queries.astype(BF16)
        g_all[pair, :, lanes] = (g_all[pair, :, lanes].astype(F32) * inverse).astype(BF16)
    for head in range(2):
        lanes = slice(head * HDIM, head * HDIM + HDIM)
        units = [2 * pair + head for pair in range(pairs)]
        for kind, (left_ref, right_ref) in enumerate(((grad_ref, q_all), (prob_ref, g_all))):
            left = jnp.concatenate([left_ref[unit, :, far:] for unit in units], axis=0)
            right = jnp.concatenate([right_ref[pair, :, lanes] for pair in range(pairs)], axis=0)
            total = mm_rows(left, right).astype(BF16)
            for (place, part, rows), out_ref in zip(entries, far_refs):
                for slab in range(slots):
                    start = place * BLOCK + 32 * slab + part * rows
                    at = (kind * slots + slab) * rows
                    out_ref[at : at + rows, lanes] = total[start : start + rows, :]


def reduce_kernel(slots, kl_ref, vl_ref, prob_ref, grad_ref, sum_ref, *home_refs):
    tok = BLOCK
    inv_scale = 1.0 / math.sqrt(HDIM)
    for pair in range(slots // 2):
        for head in range(2):
            lanes = slice(head * HDIM, head * HDIM + HDIM)
            unit = 2 * pair + head
            inverse = sum_ref[unit]
            attended = (mm(prob_ref[unit], vl_ref[pair, :, lanes]) * inverse).astype(BF16)
            query_grad = mm(grad_ref[unit], kl_ref[pair, :, lanes]) * (inverse * inv_scale)
            query_grad = query_grad.astype(BF16)
            for side in range(2):
                rows = slice(side * tok, side * tok + tok)
                home_refs[2 * pair + side][0:tok, lanes] = attended[rows]
                home_refs[2 * pair + side][tok:, lanes] = query_grad[rows]


def local_kernel(slots, q_all, g_all, prob_ref, grad_ref, dk_ref, dv_ref, ck_ref, cv_ref):
    tok = BLOCK
    pairs = slots // 2
    near, far = 2 * tok, 3 * tok
    for pair in range(pairs):
        for head in range(2):
            lanes = slice(head * HDIM, head * HDIM + HDIM)
            unit = 2 * pair + head
            key_terms = mm_rows(grad_ref[unit, :, 0:far], q_all[pair, :, lanes])
            value_terms = mm_rows(prob_ref[unit, :, 0:far], g_all[pair, :, lanes])
            for terms, local, level1 in (
                (key_terms, dk_ref, ck_ref),
                (value_terms, dv_ref, cv_ref),
            ):
                local[pair * near : pair * near + near, lanes] = terms[0:near]
                level1[pair ^ 1, :, lanes] = terms[near:].astype(BF16)
    pool = pool_matrix(BLOCK, 1)
    for pair in range(pairs):
        rows = slice(pair * near, pair * near + near)
        dk_ref[rows, :] += mm_rows(pool, ck_ref[pair]) * 0.5
        dv_ref[rows, :] += mm_rows(pool, cv_ref[pair])


def merge_kernel(slots, levels, dk_ref, dv_ref, *refs):
    far_refs, out_refs = refs[: len(levels)], refs[len(levels) :]
    tok = BLOCK
    key_pools, value_pools = [], []
    for level in levels:
        count = piece_rows(level)
        shape = (slots * count, slots * tok)
        row = lax.broadcasted_iota(jnp.int32, shape, 0)
        col = lax.broadcasted_iota(jnp.int32, shape, 1)
        slab = lax.shift_right_logical(col, tok.bit_length() - 1)
        held = slab * count + lax.shift_right_logical(col & (tok - 1), level)
        key_pools.append(jnp.where(held == row, 1.0 / (1 << level), 0.0).astype(BF16))
        value_pools.append(jnp.where(held == row, 1.0, 0.0).astype(BF16))
    halves = [ref.shape[0] // 2 for ref in far_refs]
    keys = jnp.concatenate([ref[:half, :] for ref, half in zip(far_refs, halves)], axis=0)
    values = jnp.concatenate([ref[half:, :] for ref, half in zip(far_refs, halves)], axis=0)
    key_sum = dk_ref[...] + mm_rows(jnp.concatenate(key_pools, axis=0), keys)
    value_sum = dv_ref[...] + mm_rows(jnp.concatenate(value_pools, axis=0), values)
    for slab in range(slots):
        rows = slice(slab * tok, slab * tok + tok)
        out_refs[slab][0:tok, :] = key_sum[rows].astype(BF16)
        out_refs[slab][tok:, :] = value_sum[rows].astype(BF16)


def flip_kernel(w_ref, out_ref):
    half = out_ref.shape[0]
    for place in range(w_ref.shape[0] // half):
        rows = slice(place * half, place * half + half)
        out_ref[:, rows] = w_ref[rows, :].T


def send_kernel(slots, at_ref, w_ref, *refs):
    in_refs, att_ref, send_refs = by_mask(refs[:slots]), refs[slots], refs[slots + 1 :]
    low, core = at_ref[0], at_ref[1]
    tok, half = att_ref.shape
    width = in_refs[0].shape[1]
    for mask in range(slots):
        att_ref[:, col_block(low, mask, width)] = in_refs[mask][0:tok, :]
    part = half // len(send_refs)
    for place, send_ref in enumerate(send_refs):
        other = pl.multiple_of((1 - core) * half + place * part, part)
        send_ref[...] = mm(att_ref[...], w_ref[:, pl.ds(other, part)]).astype(BF16)


def keep_kernel(slots, at_ref, w_ref, att_ref, *refs):
    home_refs, (keep_ref, dq_ref) = by_mask(refs[:slots]), refs[slots:]
    tok, half = att_ref.shape
    width = home_refs[0].shape[1]
    for mask in range(slots):
        dq_ref[:, col_block(at_ref[0], mask, width)] = home_refs[mask][tok:, :]
    first = pl.multiple_of(at_ref[1] * half, half)
    keep_ref[...] = mm(att_ref[...], w_ref[:, pl.ds(first, half)])


def add_kernel(keep_ref, *refs):
    got_refs, out_ref = refs[:-1], refs[-1]
    part = got_refs[0].shape[1]
    for place, got_ref in enumerate(got_refs):
        cols = slice(place * part, place * part + part)
        out_ref[:, cols] = (keep_ref[:, cols] + got_ref[...].astype(F32)).astype(BF16)


def finish_kernel(slots, at_ref, out_ref, dq_ref, *refs):
    last_refs, refs = by_mask(refs[:slots]), refs[slots:]
    hbm_refs, (dk_ref, dv_ref, sems) = refs[:4], refs[4:]
    tok, width = BLOCK, last_refs[0].shape[1]
    copies = [
        pltpu.make_async_copy(source, hbm_refs[place], sems.at[place])
        for place, source in enumerate((out_ref, dq_ref, dk_ref, dv_ref))
    ]
    copies[0].start()
    copies[1].start()
    for place, held_ref in enumerate((dk_ref, dv_ref)):
        rows = slice(place * tok, place * tok + tok)
        for mask in range(slots):
            held_ref[:, col_block(at_ref[0], mask, width)] = last_refs[mask][rows, :]
        copies[2 + place].start()
    for copy in copies:
        copy.wait()


def straight(levels, slots):
    return all((slots << place) * 4 <= 32 for place in range(len(levels)))


def far_entries(levels, slots):
    entries, masks = [], []
    for place, level in enumerate(levels):
        if not straight(levels, slots):
            entries.append((place, 0, 32))
            continue
        for part in range(1 << place):
            entries.append((place, part, BLOCK >> level))
            masks.append(1 << level ^ part * slots)
    return entries, masks


def gather_far(pieces, levels, slots):
    width = pieces[0].shape[1]
    if straight(levels, slots):
        entries, masks = far_entries(levels, slots)
        return [swap_seq(pieces[entry[0]], mask) for entry, mask in zip(entries, masks)]
    held = {}
    for place, level in enumerate(levels):
        block = pieces[place].reshape(2 * slots, piece_rows(level), width)
        held[level] = block[:, None, : BLOCK >> level]
    found = []
    for step in levels:
        sent = [held[level].reshape(-1, width) for level in levels if level >= step]
        got = swap_seq(jnp.concatenate(sent, axis=0), 1 << step)
        first = 0
        for level in levels:
            if level < step:
                continue
            count = held[level].size // width
            part = got[first : first + count].reshape(held[level].shape)
            first += count
            if level == step:
                found.append(part.reshape(-1, width))
            else:
                held[level] = jnp.concatenate([held[level], part], axis=1)
    return found


def scatter_far(packed, levels, slots):
    width = packed[0].shape[1]
    if straight(levels, slots):
        entries, masks = far_entries(levels, slots)
        shares = [swap_seq(array, mask) for array, mask in zip(packed, masks)]
        return shares, [levels[entry[0]] for entry in entries]
    blocks = {}
    for place, level in enumerate(levels):
        rows = BLOCK >> level
        blocks[level] = packed[place].reshape(2 * slots, 32 // rows, rows, width)
    ready = {}
    for step in reversed(levels):
        sent, kept = [blocks[step].reshape(-1, width)], {}
        for level in levels:
            if level > step:
                size = ready[level].shape[1] // 2
                kept[level] = ready[level][:, :size]
                sent.append(ready[level][:, size:].astype(BF16).reshape(-1, width))
        got = swap_seq(jnp.concatenate(sent, axis=0), 1 << step)
        first = blocks[step].size // width
        ready[step] = got[0:first].reshape(blocks[step].shape)
        for level in kept:
            count = kept[level].size // width
            part = got[first : first + count].reshape(kept[level].shape)
            first += count
            ready[level] = kept[level].astype(F32) + part.astype(F32)
    shares = []
    for level in levels:
        share = ready[level].astype(BF16).reshape(2 * slots, -1, width)
        pad = piece_rows(level) - share.shape[1]
        if pad:
            share = jnp.pad(share, ((0, 0), (0, pad), (0, 0)))
        shares.append(share.reshape(-1, width))
    return shares, list(levels)


def on_device(queries, key_tokens, value_tokens, out_weight, output_grad):
    tok, columns = queries.shape
    heads = columns // HDIM
    slots = heads // 2
    width = columns // slots
    local_levels = slots.bit_length() - 1
    level_count = lax.axis_size("seq").bit_length() - 1
    far = list(range(local_levels, level_count))
    list_rows = 3 * tok + BLOCK * len(far)
    entries, _ = far_entries(far, slots)
    place = jnp.stack([lax.axis_index("seq") & (slots - 1), lax.axis_index("head")])
    place = place.astype(jnp.int32)

    def shape(dims, dtype=BF16):
        return jax.ShapeDtypeStruct(dims, dtype)

    def over(rows):
        return [shape((rows, width))] * slots

    def exchange(chunks):
        moved = [chunks[0]] + [swap_seq(chunks[mask], mask) for mask in range(1, slots)]
        return [moved[mask] for mask in ORDER]

    held = call(
        load_kernel,
        [shape((tok, columns))] * 2,
        [key_tokens, value_tokens],
        scratch=[pltpu.SemaphoreType.DMA((2,))],
        specs=[HBM] * 2,
        vmem=8,
    )
    chunks = call(
        lambda *refs: token_kernel(slots, *refs),
        over(2 * tok),
        [place] + list(held),
        flops=6 * 10**9,
        specs=[SMEM] + [VMEM] * 2,
        vmem=8,
    )
    keys = exchange(chunks)
    later, *_ = lax.optimization_barrier((place, *chunks))
    other_grad = swap_head(output_grad)
    chunks = call(
        lambda *refs: query_kernel(slots, *refs),
        over(2 * tok),
        [later, queries, output_grad, out_weight, other_grad],
        scratch=[pltpu.VMEM((tok, columns), BF16)],
        flops=6 * 10**9,
        specs=[SMEM] + [VMEM] * 4,
        vmem=16,
    )
    asked = exchange(chunks)
    flipped = call(
        flip_kernel,
        shape(out_weight.shape[::-1]),
        [out_weight],
        vmem=24,
        free=True,
    )
    sources, flipped, *_ = lax.optimization_barrier((keys, flipped, asked[1]))
    pieces = call(
        lambda *refs: coarse_kernel(slots, far, *refs),
        [shape((2 * slots * piece_rows(level), width)) for level in far],
        sources,
        vmem=8,
    )
    far_got = gather_far(pieces, far, slots)
    pairs = slots // 2
    made = call(
        lambda *refs: attend_kernel(slots, len(far), entries, *refs),
        [shape((2 * slots * rows, width)) for _, _, rows in entries]
        + [shape((pairs, list_rows, width))] * 2
        + [shape((pairs, 2 * tok, width))] * 2
        + [shape((slots, 2 * tok, list_rows))] * 2
        + [shape((slots, 2 * tok, HDIM), F32)],
        keys + asked + far_got,
        flops=6 * heads * tok * list_rows * HDIM,
    )
    shares, share_levels = scatter_far(made[: len(entries)], far, slots)
    key_list, value_list, asked, grads, probs, score_grads, sums = made[len(entries) :]
    made = call(
        lambda *refs: reduce_kernel(slots, *refs),
        over(2 * tok),
        [key_list, value_list, probs, score_grads, sums],
        flops=6 * 10**9,
        vmem=16,
    )
    key_sum, value_sum = call(
        lambda *refs: local_kernel(slots, *refs),
        [shape((slots * tok, width), F32)] * 2,
        [asked, grads, probs, score_grads],
        scratch=[pltpu.VMEM((pairs, BLOCK, width), BF16)] * 2,
        flops=4 * heads * tok * list_rows * HDIM,
        vmem=16,
    )
    made = list(made)
    late = ORDER[-1]
    made[late], key_sum, *shares = lax.optimization_barrier((made[late], key_sum, *shares))
    home = exchange(made)
    chunks = call(
        lambda *refs: merge_kernel(slots, share_levels, *refs),
        over(2 * tok),
        [key_sum, value_sum] + shares,
        vmem=8,
    )
    home, _ = lax.optimization_barrier((home, chunks))
    chunks = list(chunks)
    last = exchange(chunks)
    wide = shape((tok, columns))
    attended, *send = call(
        lambda *refs: send_kernel(slots, *refs),
        [wide] + [shape((tok, columns // 2))] * 2,
        [place, flipped] + home,
        flops=2 * tok * columns * columns,
        specs=[SMEM] + [VMEM] * (1 + slots),
        vmem=16,
    )
    got = [swap_head(part) for part in send]
    keep, query_grad = call(
        lambda *refs: keep_kernel(slots, *refs),
        [shape((tok, columns), F32), wide],
        [place, flipped, attended] + home,
        flops=4 * 10**9,
        specs=[SMEM] + [VMEM] * (2 + slots),
        vmem=16,
    )
    output = call(add_kernel, wide, [keep] + got, vmem=8)
    output, query_grad, key_grad, value_grad = call(
        lambda *refs: finish_kernel(slots, *refs),
        [wide] * 4,
        [place, output, query_grad] + last,
        scratch=[pltpu.VMEM((tok, columns), BF16)] * 2 + [pltpu.SemaphoreType.DMA((4,))],
        specs=[SMEM] + [VMEM] * (2 + slots),
        outs=HBM,
        vmem=8,
    )
    return output, query_grad, key_grad, value_grad


def solution(mesh):
    placed = P("seq", "head")
    return jax.shard_map(
        on_device,
        mesh=mesh,
        in_specs=(placed, placed, placed, P(None, "head"), placed),
        out_specs=(placed, placed, placed, placed),
        check_vma=False,
    )
```

```python
import math

import jax
import jax.numpy as jnp
from jax import lax
from jax.experimental import pallas as pl
from jax.experimental.pallas import tpu as pltpu
from jax.sharding import PartitionSpec as P

HDIM = 128
ORDER = (0, 1, 2, 3)
BLOCK = 128
BF16 = jnp.bfloat16
F32 = jnp.float32
VMEM = pl.BlockSpec(memory_space=pltpu.VMEM)
SMEM = pl.BlockSpec(memory_space=pltpu.SMEM)
HBM = pl.BlockSpec(memory_space=pltpu.HBM)


def swap_seq(array, mask):
    return lax.ppermute(array, "seq", [(i, i ^ mask) for i in range(lax.axis_size("seq"))])


def swap_head(array):
    return lax.ppermute(array, "head", [(0, 1), (1, 0)])


def mm(left, right):
    return jnp.dot(left, right, preferred_element_type=F32)


def mm_cols(left, right):
    return lax.dot_general(left, right, (((1,), (1,)), ((), ())), preferred_element_type=F32)


def mm_rows(left, right):
    return lax.dot_general(left, right, (((0,), (0,)), ((), ())), preferred_element_type=F32)


def pool_matrix(rows, shift):
    shape = (rows, rows << shift)
    row = lax.broadcasted_iota(jnp.int32, shape, 0)
    col = lax.broadcasted_iota(jnp.int32, shape, 1)
    return jnp.where(lax.shift_right_logical(col, shift) == row, 1.0, 0.0).astype(BF16)


def call(kernel, out_shape, operands, scratch=(), flops=0, vmem=24, specs=None, outs=VMEM, free=False):
    specs = specs or [VMEM] * len(operands)
    operands = [
        pltpu.with_memory_space_constraint(x, pltpu.HBM) if spec is HBM else x
        for x, spec in zip(operands, specs)
    ]
    moved = 0 if free else sum(x.size * x.dtype.itemsize for x in operands)
    return pl.pallas_call(
        kernel,
        out_shape=out_shape,
        in_specs=specs,
        out_specs=jax.tree.map(lambda _: outs, out_shape),
        scratch_shapes=list(scratch),
        compiler_params=pltpu.CompilerParams(vmem_limit_bytes=vmem << 20),
        cost_estimate=pl.CostEstimate(flops=flops, bytes_accessed=moved, transcendentals=0),
    )(*operands)


def by_mask(refs):
    return [refs[ORDER.index(mask)] for mask in range(len(refs))]


def level_pool(rows, level):
    row = lax.broadcasted_iota(jnp.int32, (rows, BLOCK), 0)
    col = lax.broadcasted_iota(jnp.int32, (rows, BLOCK), 1)
    return jnp.where(lax.shift_right_logical(col, level) == row, 1.0, 0.0).astype(BF16)


def col_block(low, mask, width):
    return pl.ds(pl.multiple_of((low ^ mask) * width, width), width)


def piece_rows(level):
    return max(16, BLOCK >> level)


def load_kernel(*refs):
    count = len(refs) // 2
    sems = refs[-1]
    copies = [
        pltpu.make_async_copy(refs[place], refs[count + place], sems.at[place])
        for place in range(count)
    ]
    for copy in copies:
        copy.start()
    for copy in copies:
        copy.wait()


def token_kernel(slots, at_ref, k_ref, v_ref, *chunk_refs):
    low = at_ref[0]
    tok, width = BLOCK, chunk_refs[0].shape[1]
    for mask in range(slots):
        cols = col_block(low, mask, width)
        chunk_refs[mask][0:tok, :] = k_ref[:, cols]
        chunk_refs[mask][tok:, :] = v_ref[:, cols]


def query_kernel(slots, at_ref, q_ref, mine_ref, w_ref, other_ref, *refs):
    chunk_refs, grad_ref = refs[:slots], refs[slots]
    low, core = at_ref[0], at_ref[1]
    tok, half = mine_ref.shape
    width = chunk_refs[0].shape[1]
    first = pl.multiple_of(core * half, half)
    second = pl.multiple_of((1 - core) * half, half)
    total = mm(mine_ref[...], w_ref[pl.ds(first, half), :])
    total += mm(other_ref[...], w_ref[pl.ds(second, half), :])
    grad_ref[...] = total.astype(BF16)
    for mask in range(slots):
        cols = col_block(low, mask, width)
        chunk_refs[mask][0:tok, :] = q_ref[:, cols]
        chunk_refs[mask][tok:, :] = grad_ref[:, cols]


def coarse_kernel(slots, levels, *refs):
    in_refs, piece_refs = by_mask(refs[:slots]), refs[slots:]
    tok = BLOCK
    for level, piece in zip(levels, piece_refs):
        rows = piece_rows(level)
        pool = level_pool(rows, level)
        for slab in range(slots):
            at = slab * rows
            keys = mm(pool, in_refs[slab][0:tok, :]) * (1.0 / (1 << level))
            piece[at : at + rows, :] = keys.astype(BF16)
            at = (slots + slab) * rows
            piece[at : at + rows, :] = mm(pool, in_refs[slab][tok:, :]).astype(BF16)


def attend_kernel(slots, far_levels, entries, *refs):
    key_refs, query_refs = by_mask(refs[:slots]), by_mask(refs[slots : 2 * slots])
    refs = refs[2 * slots :]
    count = len(entries)
    got_refs, far_refs, refs = refs[:count], refs[count : 2 * count], refs[2 * count :]
    kl_ref, vl_ref, q_all, g_all, prob_ref, grad_ref, sum_ref = refs
    tok = BLOCK
    pairs = slots // 2
    inv_scale = 1.0 / math.sqrt(HDIM)
    to_exp2 = inv_scale * math.log2(math.e)
    near, far = 2 * tok, 3 * tok
    for slab in range(slots):
        pair, row = slab // 2, (slab % 2) * tok
        q_all[pair, row : row + tok, :] = query_refs[slab][0:tok, :]
        g_all[pair, row : row + tok, :] = query_refs[slab][tok:, :]
        kl_ref[pair, row : row + tok, :] = key_refs[slab][0:tok, :]
        vl_ref[pair, row : row + tok, :] = key_refs[slab][tok:, :]
    for (place, part, rows), got_ref in zip(entries, got_refs):
        for slab in range(slots):
            spot = far + place * BLOCK + 32 * slab + part * rows
            for kind, list_ref in enumerate((kl_ref, vl_ref)):
                at = (kind * slots + slab) * rows
                for pair in range(pairs):
                    list_ref[pair, spot : spot + rows, :] = got_ref[at : at + rows, :]
    pool = pool_matrix(BLOCK, 1)
    for pair in range(pairs):
        kl_ref[pair ^ 1, near:far, :] = (mm(pool, kl_ref[pair, 0:near, :]) * 0.5).astype(BF16)
        vl_ref[pair ^ 1, near:far, :] = mm(pool, vl_ref[pair, 0:near, :]).astype(BF16)

    def products(unit):
        pair, head = unit // 2, unit % 2
        lanes = slice(head * HDIM, head * HDIM + HDIM)
        scores = mm_cols(q_all[pair, :, lanes], kl_ref[pair, :, lanes])
        return scores, mm_cols(g_all[pair, :, lanes], vl_ref[pair, :, lanes])

    ready = products(0)
    for unit in range(slots):
        pair, head = unit // 2, unit % 2
        lanes = slice(head * HDIM, head * HDIM + HDIM)
        scores, prob_grad = ready
        if unit + 1 < slots:
            ready = products(unit + 1)
        top = jnp.max(scores, axis=1, keepdims=True)
        raised = jnp.exp2((scores - top) * to_exp2)
        inverse = 1.0 / jnp.sum(raised, axis=1, keepdims=True)
        centre = jnp.sum(raised * prob_grad, axis=1, keepdims=True) * inverse
        prob_ref[unit] = raised.astype(BF16)
        grad_ref[unit] = (raised * (prob_grad - centre)).astype(BF16)
        sum_ref[unit] = jnp.broadcast_to(inverse, (near, HDIM))
        queries = q_all[pair, :, lanes].astype(F32) * (inverse * inv_scale)
        q_all[pair, :, lanes] = queries.astype(BF16)
        g_all[pair, :, lanes] = (g_all[pair, :, lanes].astype(F32) * inverse).astype(BF16)
    for head in range(2):
        lanes = slice(head * HDIM, head * HDIM + HDIM)
        units = [2 * pair + head for pair in range(pairs)]
        for kind, (left_ref, right_ref) in enumerate(((grad_ref, q_all), (prob_ref, g_all))):
            left = jnp.concatenate([left_ref[unit, :, far:] for unit in units], axis=0)
            right = jnp.concatenate([right_ref[pair, :, lanes] for pair in range(pairs)], axis=0)
            total = mm_rows(left, right).astype(BF16)
            for (place, part, rows), out_ref in zip(entries, far_refs):
                for slab in range(slots):
                    start = place * BLOCK + 32 * slab + part * rows
                    at = (kind * slots + slab) * rows
                    out_ref[at : at + rows, lanes] = total[start : start + rows, :]


def reduce_kernel(slots, kl_ref, vl_ref, prob_ref, grad_ref, sum_ref, *home_refs):
    tok = BLOCK
    inv_scale = 1.0 / math.sqrt(HDIM)
    for pair in range(slots // 2):
        for head in range(2):
            lanes = slice(head * HDIM, head * HDIM + HDIM)
            unit = 2 * pair + head
            inverse = sum_ref[unit]
            attended = (mm(prob_ref[unit], vl_ref[pair, :, lanes]) * inverse).astype(BF16)
            query_grad = mm(grad_ref[unit], kl_ref[pair, :, lanes]) * (inverse * inv_scale)
            query_grad = query_grad.astype(BF16)
            for side in range(2):
                rows = slice(side * tok, side * tok + tok)
                home_refs[2 * pair + side][0:tok, lanes] = attended[rows]
                home_refs[2 * pair + side][tok:, lanes] = query_grad[rows]


def local_kernel(slots, q_all, g_all, prob_ref, grad_ref, dk_ref, dv_ref, ck_ref, cv_ref):
    tok = BLOCK
    pairs = slots // 2
    near, far = 2 * tok, 3 * tok
    for pair in range(pairs):
        for head in range(2):
            lanes = slice(head * HDIM, head * HDIM + HDIM)
            unit = 2 * pair + head
            key_terms = mm_rows(grad_ref[unit, :, 0:far], q_all[pair, :, lanes])
            value_terms = mm_rows(prob_ref[unit, :, 0:far], g_all[pair, :, lanes])
            for terms, local, level1 in (
                (key_terms, dk_ref, ck_ref),
                (value_terms, dv_ref, cv_ref),
            ):
                local[pair * near : pair * near + near, lanes] = terms[0:near]
                level1[pair ^ 1, :, lanes] = terms[near:].astype(BF16)
    pool = pool_matrix(BLOCK, 1)
    for pair in range(pairs):
        rows = slice(pair * near, pair * near + near)
        dk_ref[rows, :] += mm_rows(pool, ck_ref[pair]) * 0.5
        dv_ref[rows, :] += mm_rows(pool, cv_ref[pair])


def merge_kernel(slots, levels, dk_ref, dv_ref, *refs):
    far_refs, out_refs = refs[: len(levels)], refs[len(levels) :]
    tok = BLOCK
    key_pools, value_pools = [], []
    for level in levels:
        count = piece_rows(level)
        shape = (slots * count, slots * tok)
        row = lax.broadcasted_iota(jnp.int32, shape, 0)
        col = lax.broadcasted_iota(jnp.int32, shape, 1)
        slab = lax.shift_right_logical(col, tok.bit_length() - 1)
        held = slab * count + lax.shift_right_logical(col & (tok - 1), level)
        key_pools.append(jnp.where(held == row, 1.0 / (1 << level), 0.0).astype(BF16))
        value_pools.append(jnp.where(held == row, 1.0, 0.0).astype(BF16))
    halves = [ref.shape[0] // 2 for ref in far_refs]
    keys = jnp.concatenate([ref[:half, :] for ref, half in zip(far_refs, halves)], axis=0)
    values = jnp.concatenate([ref[half:, :] for ref, half in zip(far_refs, halves)], axis=0)
    key_sum = dk_ref[...] + mm_rows(jnp.concatenate(key_pools, axis=0), keys)
    value_sum = dv_ref[...] + mm_rows(jnp.concatenate(value_pools, axis=0), values)
    for slab in range(slots):
        rows = slice(slab * tok, slab * tok + tok)
        out_refs[slab][0:tok, :] = key_sum[rows].astype(BF16)
        out_refs[slab][tok:, :] = value_sum[rows].astype(BF16)


def flip_kernel(w_ref, out_ref):
    half = out_ref.shape[0]
    for place in range(w_ref.shape[0] // half):
        rows = slice(place * half, place * half + half)
        out_ref[:, rows] = w_ref[rows, :].T


def send_kernel(slots, at_ref, w_ref, *refs):
    in_refs, att_ref, send_refs = by_mask(refs[:slots]), refs[slots], refs[slots + 1 :]
    low, core = at_ref[0], at_ref[1]
    tok, half = att_ref.shape
    width = in_refs[0].shape[1]
    for mask in range(slots):
        att_ref[:, col_block(low, mask, width)] = in_refs[mask][0:tok, :]
    part = half // len(send_refs)
    for place, send_ref in enumerate(send_refs):
        other = pl.multiple_of((1 - core) * half + place * part, part)
        send_ref[...] = mm(att_ref[...], w_ref[:, pl.ds(other, part)]).astype(BF16)


def keep_kernel(slots, at_ref, w_ref, att_ref, *refs):
    home_refs, (keep_ref, dq_ref) = by_mask(refs[:slots]), refs[slots:]
    tok, half = att_ref.shape
    width = home_refs[0].shape[1]
    for mask in range(slots):
        dq_ref[:, col_block(at_ref[0], mask, width)] = home_refs[mask][tok:, :]
    first = pl.multiple_of(at_ref[1] * half, half)
    keep_ref[...] = mm(att_ref[...], w_ref[:, pl.ds(first, half)])


def add_kernel(keep_ref, *refs):
    got_refs, out_ref = refs[:-1], refs[-1]
    part = got_refs[0].shape[1]
    for place, got_ref in enumerate(got_refs):
        cols = slice(place * part, place * part + part)
        out_ref[:, cols] = (keep_ref[:, cols] + got_ref[...].astype(F32)).astype(BF16)


def finish_kernel(slots, at_ref, out_ref, dq_ref, *refs):
    last_refs, refs = by_mask(refs[:slots]), refs[slots:]
    hbm_refs, (dk_ref, dv_ref, sems) = refs[:4], refs[4:]
    tok, width = BLOCK, last_refs[0].shape[1]
    copies = [
        pltpu.make_async_copy(source, hbm_refs[place], sems.at[place])
        for place, source in enumerate((out_ref, dq_ref, dk_ref, dv_ref))
    ]
    copies[0].start()
    copies[1].start()
    for place, held_ref in enumerate((dk_ref, dv_ref)):
        rows = slice(place * tok, place * tok + tok)
        for mask in range(slots):
            held_ref[:, col_block(at_ref[0], mask, width)] = last_refs[mask][rows, :]
        copies[2 + place].start()
    for copy in copies:
        copy.wait()


def straight(levels, slots):
    return all((slots << place) * 4 <= 32 for place in range(len(levels)))


def far_entries(levels, slots):
    entries, masks = [], []
    for place, level in enumerate(levels):
        if not straight(levels, slots):
            entries.append((place, 0, 32))
            continue
        for part in range(1 << place):
            entries.append((place, part, BLOCK >> level))
            masks.append(1 << level ^ part * slots)
    return entries, masks


def gather_far(pieces, levels, slots):
    width = pieces[0].shape[1]
    if straight(levels, slots):
        entries, masks = far_entries(levels, slots)
        return [swap_seq(pieces[entry[0]], mask) for entry, mask in zip(entries, masks)]
    held = {}
    for place, level in enumerate(levels):
        block = pieces[place].reshape(2 * slots, piece_rows(level), width)
        held[level] = block[:, None, : BLOCK >> level]
    found = []
    for step in levels:
        sent = [held[level].reshape(-1, width) for level in levels if level >= step]
        got = swap_seq(jnp.concatenate(sent, axis=0), 1 << step)
        first = 0
        for level in levels:
            if level < step:
                continue
            count = held[level].size // width
            part = got[first : first + count].reshape(held[level].shape)
            first += count
            if level == step:
                found.append(part.reshape(-1, width))
            else:
                held[level] = jnp.concatenate([held[level], part], axis=1)
    return found


def scatter_far(packed, levels, slots):
    width = packed[0].shape[1]
    if straight(levels, slots):
        entries, masks = far_entries(levels, slots)
        shares = [swap_seq(array, mask) for array, mask in zip(packed, masks)]
        return shares, [levels[entry[0]] for entry in entries]
    blocks = {}
    for place, level in enumerate(levels):
        rows = BLOCK >> level
        blocks[level] = packed[place].reshape(2 * slots, 32 // rows, rows, width)
    ready = {}
    for step in reversed(levels):
        sent, kept = [blocks[step].reshape(-1, width)], {}
        for level in levels:
            if level > step:
                size = ready[level].shape[1] // 2
                kept[level] = ready[level][:, :size]
                sent.append(ready[level][:, size:].astype(BF16).reshape(-1, width))
        got = swap_seq(jnp.concatenate(sent, axis=0), 1 << step)
        first = blocks[step].size // width
        ready[step] = got[0:first].reshape(blocks[step].shape)
        for level in kept:
            count = kept[level].size // width
            part = got[first : first + count].reshape(kept[level].shape)
            first += count
            ready[level] = kept[level].astype(F32) + part.astype(F32)
    shares = []
    for level in levels:
        share = ready[level].astype(BF16).reshape(2 * slots, -1, width)
        pad = piece_rows(level) - share.shape[1]
        if pad:
            share = jnp.pad(share, ((0, 0), (0, pad), (0, 0)))
        shares.append(share.reshape(-1, width))
    return shares, list(levels)


def on_device(queries, key_tokens, value_tokens, out_weight, output_grad):
    tok, columns = queries.shape
    heads = columns // HDIM
    slots = heads // 2
    width = columns // slots
    local_levels = slots.bit_length() - 1
    level_count = lax.axis_size("seq").bit_length() - 1
    far = list(range(local_levels, level_count))
    list_rows = 3 * tok + BLOCK * len(far)
    entries, _ = far_entries(far, slots)
    place = jnp.stack([lax.axis_index("seq") & (slots - 1), lax.axis_index("head")])
    place = place.astype(jnp.int32)

    def shape(dims, dtype=BF16):
        return jax.ShapeDtypeStruct(dims, dtype)

    def over(rows):
        return [shape((rows, width))] * slots

    def exchange(chunks):
        moved = [chunks[0]] + [swap_seq(chunks[mask], mask) for mask in range(1, slots)]
        return [moved[mask] for mask in ORDER]

    held = call(
        load_kernel,
        [shape((tok, columns))] * 2,
        [key_tokens, value_tokens],
        scratch=[pltpu.SemaphoreType.DMA((2,))],
        specs=[HBM] * 2,
        vmem=8,
    )
    chunks = call(
        lambda *refs: token_kernel(slots, *refs),
        over(2 * tok),
        [place] + list(held),
        flops=6 * 10**9,
        specs=[SMEM] + [VMEM] * 2,
        vmem=8,
    )
    keys = exchange(chunks)
    later, *_ = lax.optimization_barrier((place, *chunks))
    other_grad = swap_head(output_grad)
    chunks = call(
        lambda *refs: query_kernel(slots, *refs),
        over(2 * tok),
        [later, queries, output_grad, out_weight, other_grad],
        scratch=[pltpu.VMEM((tok, columns), BF16)],
        flops=6 * 10**9,
        specs=[SMEM] + [VMEM] * 4,
        vmem=16,
    )
    asked = exchange(chunks)
    flipped = call(
        flip_kernel,
        shape(out_weight.shape[::-1]),
        [out_weight],
        vmem=24,
        free=True,
    )
    sources, flipped, *_ = lax.optimization_barrier((keys, flipped, asked[1]))
    pieces = call(
        lambda *refs: coarse_kernel(slots, far, *refs),
        [shape((2 * slots * piece_rows(level), width)) for level in far],
        sources,
        vmem=8,
    )
    far_got = gather_far(pieces, far, slots)
    pairs = slots // 2
    made = call(
        lambda *refs: attend_kernel(slots, len(far), entries, *refs),
        [shape((2 * slots * rows, width)) for _, _, rows in entries]
        + [shape((pairs, list_rows, width))] * 2
        + [shape((pairs, 2 * tok, width))] * 2
        + [shape((slots, 2 * tok, list_rows))] * 2
        + [shape((slots, 2 * tok, HDIM), F32)],
        keys + asked + far_got,
        flops=6 * heads * tok * list_rows * HDIM,
    )
    shares, share_levels = scatter_far(made[: len(entries)], far, slots)
    key_list, value_list, asked, grads, probs, score_grads, sums = made[len(entries) :]
    made = call(
        lambda *refs: reduce_kernel(slots, *refs),
        over(2 * tok),
        [key_list, value_list, probs, score_grads, sums],
        flops=6 * 10**9,
        vmem=16,
    )
    key_sum, value_sum = call(
        lambda *refs: local_kernel(slots, *refs),
        [shape((slots * tok, width), F32)] * 2,
        [asked, grads, probs, score_grads],
        scratch=[pltpu.VMEM((pairs, BLOCK, width), BF16)] * 2,
        flops=4 * heads * tok * list_rows * HDIM,
        vmem=16,
    )
    made = list(made)
    late = ORDER[-1]
    made[late], key_sum, *shares = lax.optimization_barrier((made[late], key_sum, *shares))
    home = exchange(made)
    chunks = call(
        lambda *refs: merge_kernel(slots, share_levels, *refs),
        over(2 * tok),
        [key_sum, value_sum] + shares,
        vmem=8,
    )
    home, _ = lax.optimization_barrier((home, chunks))
    chunks = list(chunks)
    last = exchange(chunks)
    wide = shape((tok, columns))
    attended, *send = call(
        lambda *refs: send_kernel(slots, *refs),
        [wide] + [shape((tok, columns))],
        [place, flipped] + home,
        flops=2 * tok * columns * columns,
        specs=[SMEM] + [VMEM] * (1 + slots),
        vmem=16,
    )
    got = [swap_head(part) for part in send]
    keep, query_grad = call(
        lambda *refs: keep_kernel(slots, *refs),
        [shape((tok, columns), F32), wide],
        [place, flipped, attended] + home,
        flops=4 * 10**9,
        specs=[SMEM] + [VMEM] * (2 + slots),
        vmem=16,
    )
    output = call(add_kernel, wide, [keep] + got, vmem=8)
    output, query_grad, key_grad, value_grad = call(
        lambda *refs: finish_kernel(slots, *refs),
        [wide] * 4,
        [place, output, query_grad] + last,
        scratch=[pltpu.VMEM((tok, columns), BF16)] * 2 + [pltpu.SemaphoreType.DMA((4,))],
        specs=[SMEM] + [VMEM] * (2 + slots),
        outs=HBM,
        vmem=8,
    )
    return output, query_grad, key_grad, value_grad


def solution(mesh):
    placed = P("seq", "head")
    return jax.shard_map(
        on_device,
        mesh=mesh,
        in_specs=(placed, placed, placed, P(None, "head"), placed),
        out_specs=(placed, placed, placed, placed),
        check_vma=False,
    )
```

```python
import math

import jax
import jax.numpy as jnp
from jax import lax
from jax.experimental import pallas as pl
from jax.experimental.pallas import tpu as pltpu
from jax.sharding import PartitionSpec as P

HDIM = 128
ORDER = (0, 1, 2, 3)
BACK = (0, 2, 1, 3)
BLOCK = 128
BF16 = jnp.bfloat16
F32 = jnp.float32
VMEM = pl.BlockSpec(memory_space=pltpu.VMEM)
SMEM = pl.BlockSpec(memory_space=pltpu.SMEM)
HBM = pl.BlockSpec(memory_space=pltpu.HBM)


def swap_seq(array, mask):
    return lax.ppermute(array, "seq", [(i, i ^ mask) for i in range(lax.axis_size("seq"))])


def swap_head(array):
    return lax.ppermute(array, "head", [(0, 1), (1, 0)])


def mm(left, right):
    return jnp.dot(left, right, preferred_element_type=F32)


def mm_cols(left, right):
    return lax.dot_general(left, right, (((1,), (1,)), ((), ())), preferred_element_type=F32)


def mm_rows(left, right):
    return lax.dot_general(left, right, (((0,), (0,)), ((), ())), preferred_element_type=F32)


def pool_matrix(rows, shift):
    shape = (rows, rows << shift)
    row = lax.broadcasted_iota(jnp.int32, shape, 0)
    col = lax.broadcasted_iota(jnp.int32, shape, 1)
    return jnp.where(lax.shift_right_logical(col, shift) == row, 1.0, 0.0).astype(BF16)


def call(kernel, out_shape, operands, scratch=(), flops=0, vmem=24, specs=None, outs=VMEM, free=False):
    specs = specs or [VMEM] * len(operands)
    operands = [
        pltpu.with_memory_space_constraint(x, pltpu.HBM) if spec is HBM else x
        for x, spec in zip(operands, specs)
    ]
    moved = 0 if free else sum(x.size * x.dtype.itemsize for x in operands)
    return pl.pallas_call(
        kernel,
        out_shape=out_shape,
        in_specs=specs,
        out_specs=jax.tree.map(lambda _: outs, out_shape),
        scratch_shapes=list(scratch),
        compiler_params=pltpu.CompilerParams(vmem_limit_bytes=vmem << 20),
        cost_estimate=pl.CostEstimate(flops=flops, bytes_accessed=moved, transcendentals=0),
    )(*operands)


def by_mask(refs, order=ORDER):
    return [refs[order.index(mask)] for mask in range(len(refs))]


def level_pool(rows, level):
    row = lax.broadcasted_iota(jnp.int32, (rows, BLOCK), 0)
    col = lax.broadcasted_iota(jnp.int32, (rows, BLOCK), 1)
    return jnp.where(lax.shift_right_logical(col, level) == row, 1.0, 0.0).astype(BF16)


def col_block(low, mask, width):
    return pl.ds(pl.multiple_of((low ^ mask) * width, width), width)


def piece_rows(level):
    return max(16, BLOCK >> level)


def load_kernel(*refs):
    count = len(refs) // 2
    sems = refs[-1]
    copies = [
        pltpu.make_async_copy(refs[place], refs[count + place], sems.at[place])
        for place in range(count)
    ]
    for copy in copies:
        copy.start()
    for copy in copies:
        copy.wait()


def token_kernel(slots, at_ref, k_ref, v_ref, *chunk_refs):
    low = at_ref[0]
    tok, width = BLOCK, chunk_refs[0].shape[1]
    for mask in range(slots):
        cols = col_block(low, mask, width)
        chunk_refs[mask][0:tok, :] = k_ref[:, cols]
        chunk_refs[mask][tok:, :] = v_ref[:, cols]


def query_kernel(slots, at_ref, q_ref, mine_ref, w_ref, other_ref, *refs):
    chunk_refs, grad_ref = refs[:slots], refs[slots]
    low, core = at_ref[0], at_ref[1]
    tok, half = mine_ref.shape
    width = chunk_refs[0].shape[1]
    first = pl.multiple_of(core * half, half)
    second = pl.multiple_of((1 - core) * half, half)
    total = mm(mine_ref[...], w_ref[pl.ds(first, half), :])
    total += mm(other_ref[...], w_ref[pl.ds(second, half), :])
    grad_ref[...] = total.astype(BF16)
    for mask in range(slots):
        cols = col_block(low, mask, width)
        chunk_refs[mask][0:tok, :] = q_ref[:, cols]
        chunk_refs[mask][tok:, :] = grad_ref[:, cols]


def coarse_kernel(slots, levels, *refs):
    in_refs, piece_refs = by_mask(refs[:slots]), refs[slots:]
    tok = BLOCK
    for level, piece in zip(levels, piece_refs):
        rows = piece_rows(level)
        pool = level_pool(rows, level)
        for slab in range(slots):
            at = slab * rows
            keys = mm(pool, in_refs[slab][0:tok, :]) * (1.0 / (1 << level))
            piece[at : at + rows, :] = keys.astype(BF16)
            at = (slots + slab) * rows
            piece[at : at + rows, :] = mm(pool, in_refs[slab][tok:, :]).astype(BF16)


def attend_kernel(slots, far_levels, entries, *refs):
    key_refs, query_refs = by_mask(refs[:slots]), by_mask(refs[slots : 2 * slots])
    refs = refs[2 * slots :]
    count = len(entries)
    got_refs, far_refs, refs = refs[:count], refs[count : 2 * count], refs[2 * count :]
    kl_ref, vl_ref, q_all, g_all, prob_ref, grad_ref, sum_ref = refs
    tok = BLOCK
    pairs = slots // 2
    inv_scale = 1.0 / math.sqrt(HDIM)
    to_exp2 = inv_scale * math.log2(math.e)
    near, far = 2 * tok, 3 * tok
    for slab in range(slots):
        pair, row = slab // 2, (slab % 2) * tok
        q_all[pair, row : row + tok, :] = query_refs[slab][0:tok, :]
        g_all[pair, row : row + tok, :] = query_refs[slab][tok:, :]
        kl_ref[pair, row : row + tok, :] = key_refs[slab][0:tok, :]
        vl_ref[pair, row : row + tok, :] = key_refs[slab][tok:, :]
    for (place, part, rows), got_ref in zip(entries, got_refs):
        for slab in range(slots):
            spot = far + place * BLOCK + 32 * slab + part * rows
            for kind, list_ref in enumerate((kl_ref, vl_ref)):
                at = (kind * slots + slab) * rows
                for pair in range(pairs):
                    list_ref[pair, spot : spot + rows, :] = got_ref[at : at + rows, :]
    pool = pool_matrix(BLOCK, 1)
    for pair in range(pairs):
        kl_ref[pair ^ 1, near:far, :] = (mm(pool, kl_ref[pair, 0:near, :]) * 0.5).astype(BF16)
        vl_ref[pair ^ 1, near:far, :] = mm(pool, vl_ref[pair, 0:near, :]).astype(BF16)

    def products(unit):
        pair, head = unit // 2, unit % 2
        lanes = slice(head * HDIM, head * HDIM + HDIM)
        scores = mm_cols(q_all[pair, :, lanes], kl_ref[pair, :, lanes])
        return scores, mm_cols(g_all[pair, :, lanes], vl_ref[pair, :, lanes])

    ready = products(0)
    for unit in range(slots):
        pair, head = unit // 2, unit % 2
        lanes = slice(head * HDIM, head * HDIM + HDIM)
        scores, prob_grad = ready
        if unit + 1 < slots:
            ready = products(unit + 1)
        top = jnp.max(scores, axis=1, keepdims=True)
        raised = jnp.exp2((scores - top) * to_exp2)
        inverse = 1.0 / jnp.sum(raised, axis=1, keepdims=True)
        centre = jnp.sum(raised * prob_grad, axis=1, keepdims=True) * inverse
        prob_ref[unit] = raised.astype(BF16)
        grad_ref[unit] = (raised * (prob_grad - centre)).astype(BF16)
        sum_ref[unit] = jnp.broadcast_to(inverse, (near, HDIM))
        queries = q_all[pair, :, lanes].astype(F32) * (inverse * inv_scale)
        q_all[pair, :, lanes] = queries.astype(BF16)
        g_all[pair, :, lanes] = (g_all[pair, :, lanes].astype(F32) * inverse).astype(BF16)
    for head in range(2):
        lanes = slice(head * HDIM, head * HDIM + HDIM)
        units = [2 * pair + head for pair in range(pairs)]
        for kind, (left_ref, right_ref) in enumerate(((grad_ref, q_all), (prob_ref, g_all))):
            left = jnp.concatenate([left_ref[unit, :, far:] for unit in units], axis=0)
            right = jnp.concatenate([right_ref[pair, :, lanes] for pair in range(pairs)], axis=0)
            total = mm_rows(left, right).astype(BF16)
            for (place, part, rows), out_ref in zip(entries, far_refs):
                for slab in range(slots):
                    start = place * BLOCK + 32 * slab + part * rows
                    at = (kind * slots + slab) * rows
                    out_ref[at : at + rows, lanes] = total[start : start + rows, :]


def reduce_kernel(slots, kl_ref, vl_ref, prob_ref, grad_ref, sum_ref, *home_refs):
    tok = BLOCK
    inv_scale = 1.0 / math.sqrt(HDIM)
    for pair in range(slots // 2):
        for head in range(2):
            lanes = slice(head * HDIM, head * HDIM + HDIM)
            unit = 2 * pair + head
            inverse = sum_ref[unit]
            attended = (mm(prob_ref[unit], vl_ref[pair, :, lanes]) * inverse).astype(BF16)
            query_grad = mm(grad_ref[unit], kl_ref[pair, :, lanes]) * (inverse * inv_scale)
            query_grad = query_grad.astype(BF16)
            for side in range(2):
                rows = slice(side * tok, side * tok + tok)
                home_refs[2 * pair + side][0:tok, lanes] = attended[rows]
                home_refs[2 * pair + side][tok:, lanes] = query_grad[rows]


def local_kernel(slots, q_all, g_all, prob_ref, grad_ref, dk_ref, dv_ref, ck_ref, cv_ref):
    tok = BLOCK
    pairs = slots // 2
    near, far = 2 * tok, 3 * tok
    for pair in range(pairs):
        for head in range(2):
            lanes = slice(head * HDIM, head * HDIM + HDIM)
            unit = 2 * pair + head
            key_terms = mm_rows(grad_ref[unit, :, 0:far], q_all[pair, :, lanes])
            value_terms = mm_rows(prob_ref[unit, :, 0:far], g_all[pair, :, lanes])
            for terms, local, level1 in (
                (key_terms, dk_ref, ck_ref),
                (value_terms, dv_ref, cv_ref),
            ):
                local[pair * near : pair * near + near, lanes] = terms[0:near]
                level1[pair ^ 1, :, lanes] = terms[near:].astype(BF16)
    pool = pool_matrix(BLOCK, 1)
    for pair in range(pairs):
        rows = slice(pair * near, pair * near + near)
        dk_ref[rows, :] += mm_rows(pool, ck_ref[pair]) * 0.5
        dv_ref[rows, :] += mm_rows(pool, cv_ref[pair])


def merge_kernel(slots, levels, dk_ref, dv_ref, *refs):
    far_refs, out_refs = refs[: len(levels)], refs[len(levels) :]
    tok = BLOCK
    key_pools, value_pools = [], []
    for level in levels:
        count = piece_rows(level)
        shape = (slots * count, slots * tok)
        row = lax.broadcasted_iota(jnp.int32, shape, 0)
        col = lax.broadcasted_iota(jnp.int32, shape, 1)
        slab = lax.shift_right_logical(col, tok.bit_length() - 1)
        held = slab * count + lax.shift_right_logical(col & (tok - 1), level)
        key_pools.append(jnp.where(held == row, 1.0 / (1 << level), 0.0).astype(BF16))
        value_pools.append(jnp.where(held == row, 1.0, 0.0).astype(BF16))
    halves = [ref.shape[0] // 2 for ref in far_refs]
    keys = jnp.concatenate([ref[:half, :] for ref, half in zip(far_refs, halves)], axis=0)
    values = jnp.concatenate([ref[half:, :] for ref, half in zip(far_refs, halves)], axis=0)
    key_sum = dk_ref[...] + mm_rows(jnp.concatenate(key_pools, axis=0), keys)
    value_sum = dv_ref[...] + mm_rows(jnp.concatenate(value_pools, axis=0), values)
    for slab in range(slots):
        rows = slice(slab * tok, slab * tok + tok)
        out_refs[slab][0:tok, :] = key_sum[rows].astype(BF16)
        out_refs[slab][tok:, :] = value_sum[rows].astype(BF16)


def flip_kernel(w_ref, out_ref):
    half = out_ref.shape[0]
    for place in range(w_ref.shape[0] // half):
        rows = slice(place * half, place * half + half)
        out_ref[:, rows] = w_ref[rows, :].T


def send_kernel(slots, at_ref, w_ref, *refs):
    in_refs, att_ref, send_refs = by_mask(refs[:slots], BACK), refs[slots], refs[slots + 1 :]
    low, core = at_ref[0], at_ref[1]
    tok, half = att_ref.shape
    width = in_refs[0].shape[1]
    for mask in range(slots):
        att_ref[:, col_block(low, mask, width)] = in_refs[mask][0:tok, :]
    part = half // len(send_refs)
    for place, send_ref in enumerate(send_refs):
        other = pl.multiple_of((1 - core) * half + place * part, part)
        send_ref[...] = mm(att_ref[...], w_ref[:, pl.ds(other, part)]).astype(BF16)


def keep_kernel(slots, at_ref, w_ref, att_ref, *refs):
    home_refs, (keep_ref, dq_ref) = by_mask(refs[:slots], BACK), refs[slots:]
    tok, half = att_ref.shape
    width = home_refs[0].shape[1]
    for mask in range(slots):
        dq_ref[:, col_block(at_ref[0], mask, width)] = home_refs[mask][tok:, :]
    first = pl.multiple_of(at_ref[1] * half, half)
    keep_ref[...] = mm(att_ref[...], w_ref[:, pl.ds(first, half)])


def add_kernel(keep_ref, *refs):
    got_refs, out_ref = refs[:-1], refs[-1]
    part = got_refs[0].shape[1]
    for place, got_ref in enumerate(got_refs):
        cols = slice(place * part, place * part + part)
        out_ref[:, cols] = (keep_ref[:, cols] + got_ref[...].astype(F32)).astype(BF16)


def finish_kernel(slots, at_ref, out_ref, dq_ref, *refs):
    last_refs, refs = by_mask(refs[:slots], BACK), refs[slots:]
    hbm_refs, (dk_ref, dv_ref, sems) = refs[:4], refs[4:]
    tok, width = BLOCK, last_refs[0].shape[1]
    copies = [
        pltpu.make_async_copy(source, hbm_refs[place], sems.at[place])
        for place, source in enumerate((out_ref, dq_ref, dk_ref, dv_ref))
    ]
    copies[0].start()
    copies[1].start()
    for place, held_ref in enumerate((dk_ref, dv_ref)):
        rows = slice(place * tok, place * tok + tok)
        for mask in range(slots):
            held_ref[:, col_block(at_ref[0], mask, width)] = last_refs[mask][rows, :]
        copies[2 + place].start()
    for copy in copies:
        copy.wait()


def straight(levels, slots):
    return all((slots << place) * 4 <= 32 for place in range(len(levels)))


def far_entries(levels, slots):
    entries, masks = [], []
    for place, level in enumerate(levels):
        if not straight(levels, slots):
            entries.append((place, 0, 32))
            continue
        for part in range(1 << place):
            entries.append((place, part, BLOCK >> level))
            masks.append(1 << level ^ part * slots)
    return entries, masks


def gather_far(pieces, levels, slots):
    width = pieces[0].shape[1]
    if straight(levels, slots):
        entries, masks = far_entries(levels, slots)
        return [swap_seq(pieces[entry[0]], mask) for entry, mask in zip(entries, masks)]
    held = {}
    for place, level in enumerate(levels):
        block = pieces[place].reshape(2 * slots, piece_rows(level), width)
        held[level] = block[:, None, : BLOCK >> level]
    found = []
    for step in levels:
        sent = [held[level].reshape(-1, width) for level in levels if level >= step]
        got = swap_seq(jnp.concatenate(sent, axis=0), 1 << step)
        first = 0
        for level in levels:
            if level < step:
                continue
            count = held[level].size // width
            part = got[first : first + count].reshape(held[level].shape)
            first += count
            if level == step:
                found.append(part.reshape(-1, width))
            else:
                held[level] = jnp.concatenate([held[level], part], axis=1)
    return found


def scatter_far(packed, levels, slots):
    width = packed[0].shape[1]
    if straight(levels, slots):
        entries, masks = far_entries(levels, slots)
        shares = [swap_seq(array, mask) for array, mask in zip(packed, masks)]
        return shares, [levels[entry[0]] for entry in entries]
    blocks = {}
    for place, level in enumerate(levels):
        rows = BLOCK >> level
        blocks[level] = packed[place].reshape(2 * slots, 32 // rows, rows, width)
    ready = {}
    for step in reversed(levels):
        sent, kept = [blocks[step].reshape(-1, width)], {}
        for level in levels:
            if level > step:
                size = ready[level].shape[1] // 2
                kept[level] = ready[level][:, :size]
                sent.append(ready[level][:, size:].astype(BF16).reshape(-1, width))
        got = swap_seq(jnp.concatenate(sent, axis=0), 1 << step)
        first = blocks[step].size // width
        ready[step] = got[0:first].reshape(blocks[step].shape)
        for level in kept:
            count = kept[level].size // width
            part = got[first : first + count].reshape(kept[level].shape)
            first += count
            ready[level] = kept[level].astype(F32) + part.astype(F32)
    shares = []
    for level in levels:
        share = ready[level].astype(BF16).reshape(2 * slots, -1, width)
        pad = piece_rows(level) - share.shape[1]
        if pad:
            share = jnp.pad(share, ((0, 0), (0, pad), (0, 0)))
        shares.append(share.reshape(-1, width))
    return shares, list(levels)


def on_device(queries, key_tokens, value_tokens, out_weight, output_grad):
    tok, columns = queries.shape
    heads = columns // HDIM
    slots = heads // 2
    width = columns // slots
    local_levels = slots.bit_length() - 1
    level_count = lax.axis_size("seq").bit_length() - 1
    far = list(range(local_levels, level_count))
    list_rows = 3 * tok + BLOCK * len(far)
    entries, _ = far_entries(far, slots)
    place = jnp.stack([lax.axis_index("seq") & (slots - 1), lax.axis_index("head")])
    place = place.astype(jnp.int32)

    def shape(dims, dtype=BF16):
        return jax.ShapeDtypeStruct(dims, dtype)

    def over(rows):
        return [shape((rows, width))] * slots

    def exchange(chunks, order=ORDER):
        moved = [chunks[0]] + [swap_seq(chunks[mask], mask) for mask in range(1, slots)]
        return [moved[mask] for mask in order]

    held = call(
        load_kernel,
        [shape((tok, columns))] * 2,
        [key_tokens, value_tokens],
        scratch=[pltpu.SemaphoreType.DMA((2,))],
        specs=[HBM] * 2,
        vmem=8,
    )
    chunks = call(
        lambda *refs: token_kernel(slots, *refs),
        over(2 * tok),
        [place] + list(held),
        flops=6 * 10**9,
        specs=[SMEM] + [VMEM] * 2,
        vmem=8,
    )
    keys = exchange(chunks)
    later, *_ = lax.optimization_barrier((place, *chunks))
    other_grad = swap_head(output_grad)
    chunks = call(
        lambda *refs: query_kernel(slots, *refs),
        over(2 * tok),
        [later, queries, output_grad, out_weight, other_grad],
        scratch=[pltpu.VMEM((tok, columns), BF16)],
        flops=6 * 10**9,
        specs=[SMEM] + [VMEM] * 4,
        vmem=16,
    )
    asked = exchange(chunks)
    flipped = call(
        flip_kernel,
        shape(out_weight.shape[::-1]),
        [out_weight],
        vmem=24,
        free=True,
    )
    sources, flipped, *_ = lax.optimization_barrier((keys, flipped, asked[1]))
    pieces = call(
        lambda *refs: coarse_kernel(slots, far, *refs),
        [shape((2 * slots * piece_rows(level), width)) for level in far],
        sources,
        vmem=8,
    )
    far_got = gather_far(pieces, far, slots)
    pairs = slots // 2
    made = call(
        lambda *refs: attend_kernel(slots, len(far), entries, *refs),
        [shape((2 * slots * rows, width)) for _, _, rows in entries]
        + [shape((pairs, list_rows, width))] * 2
        + [shape((pairs, 2 * tok, width))] * 2
        + [shape((slots, 2 * tok, list_rows))] * 2
        + [shape((slots, 2 * tok, HDIM), F32)],
        keys + asked + far_got,
        flops=6 * heads * tok * list_rows * HDIM,
    )
    shares, share_levels = scatter_far(made[: len(entries)], far, slots)
    key_list, value_list, asked, grads, probs, score_grads, sums = made[len(entries) :]
    made = call(
        lambda *refs: reduce_kernel(slots, *refs),
        over(2 * tok),
        [key_list, value_list, probs, score_grads, sums],
        flops=6 * 10**9,
        vmem=16,
    )
    key_sum, value_sum = call(
        lambda *refs: local_kernel(slots, *refs),
        [shape((slots * tok, width), F32)] * 2,
        [asked, grads, probs, score_grads],
        scratch=[pltpu.VMEM((pairs, BLOCK, width), BF16)] * 2,
        flops=4 * heads * tok * list_rows * HDIM,
        vmem=16,
    )
    made = list(made)
    late = BACK[-1]
    made[late], key_sum, *shares = lax.optimization_barrier((made[late], key_sum, *shares))
    home = exchange(made, BACK)
    chunks = call(
        lambda *refs: merge_kernel(slots, share_levels, *refs),
        over(2 * tok),
        [key_sum, value_sum] + shares,
        vmem=8,
    )
    home, _ = lax.optimization_barrier((home, chunks))
    chunks = list(chunks)
    last = exchange(chunks, BACK)
    wide = shape((tok, columns))
    attended, *send = call(
        lambda *refs: send_kernel(slots, *refs),
        [wide] + [shape((tok, columns))],
        [place, flipped] + home,
        flops=2 * tok * columns * columns,
        specs=[SMEM] + [VMEM] * (1 + slots),
        vmem=16,
    )
    got = [swap_head(part) for part in send]
    keep, query_grad = call(
        lambda *refs: keep_kernel(slots, *refs),
        [shape((tok, columns), F32), wide],
        [place, flipped, attended] + home,
        flops=4 * 10**9,
        specs=[SMEM] + [VMEM] * (2 + slots),
        vmem=16,
    )
    output = call(add_kernel, wide, [keep] + got, vmem=8)
    output, query_grad, key_grad, value_grad = call(
        lambda *refs: finish_kernel(slots, *refs),
        [wide] * 4,
        [place, output, query_grad] + last,
        scratch=[pltpu.VMEM((tok, columns), BF16)] * 2 + [pltpu.SemaphoreType.DMA((4,))],
        specs=[SMEM] + [VMEM] * (2 + slots),
        outs=HBM,
        vmem=8,
    )
    return output, query_grad, key_grad, value_grad


def solution(mesh):
    placed = P("seq", "head")
    return jax.shard_map(
        on_device,
        mesh=mesh,
        in_specs=(placed, placed, placed, P(None, "head"), placed),
        out_specs=(placed, placed, placed, placed),
        check_vma=False,
    )
```

```python
import math

import jax
import jax.numpy as jnp
from jax import lax
from jax.experimental import pallas as pl
from jax.experimental.pallas import tpu as pltpu
from jax.sharding import PartitionSpec as P

HDIM = 128
ORDER = (0, 1, 2, 3)
BACK = (0, 3, 1, 2)
BLOCK = 128
BF16 = jnp.bfloat16
F32 = jnp.float32
VMEM = pl.BlockSpec(memory_space=pltpu.VMEM)
SMEM = pl.BlockSpec(memory_space=pltpu.SMEM)
HBM = pl.BlockSpec(memory_space=pltpu.HBM)


def swap_seq(array, mask):
    return lax.ppermute(array, "seq", [(i, i ^ mask) for i in range(lax.axis_size("seq"))])


def swap_head(array):
    return lax.ppermute(array, "head", [(0, 1), (1, 0)])


def mm(left, right):
    return jnp.dot(left, right, preferred_element_type=F32)


def mm_cols(left, right):
    return lax.dot_general(left, right, (((1,), (1,)), ((), ())), preferred_element_type=F32)


def mm_rows(left, right):
    return lax.dot_general(left, right, (((0,), (0,)), ((), ())), preferred_element_type=F32)


def pool_matrix(rows, shift):
    shape = (rows, rows << shift)
    row = lax.broadcasted_iota(jnp.int32, shape, 0)
    col = lax.broadcasted_iota(jnp.int32, shape, 1)
    return jnp.where(lax.shift_right_logical(col, shift) == row, 1.0, 0.0).astype(BF16)


def call(kernel, out_shape, operands, scratch=(), flops=0, vmem=24, specs=None, outs=VMEM, free=False):
    specs = specs or [VMEM] * len(operands)
    operands = [
        pltpu.with_memory_space_constraint(x, pltpu.HBM) if spec is HBM else x
        for x, spec in zip(operands, specs)
    ]
    moved = 0 if free else sum(x.size * x.dtype.itemsize for x in operands)
    return pl.pallas_call(
        kernel,
        out_shape=out_shape,
        in_specs=specs,
        out_specs=jax.tree.map(lambda _: outs, out_shape),
        scratch_shapes=list(scratch),
        compiler_params=pltpu.CompilerParams(vmem_limit_bytes=vmem << 20),
        cost_estimate=pl.CostEstimate(flops=flops, bytes_accessed=moved, transcendentals=0),
    )(*operands)


def by_mask(refs, order=ORDER):
    return [refs[order.index(mask)] for mask in range(len(refs))]


def level_pool(rows, level):
    row = lax.broadcasted_iota(jnp.int32, (rows, BLOCK), 0)
    col = lax.broadcasted_iota(jnp.int32, (rows, BLOCK), 1)
    return jnp.where(lax.shift_right_logical(col, level) == row, 1.0, 0.0).astype(BF16)


def col_block(low, mask, width):
    return pl.ds(pl.multiple_of((low ^ mask) * width, width), width)


def piece_rows(level):
    return max(16, BLOCK >> level)


def load_kernel(*refs):
    count = len(refs) // 2
    sems = refs[-1]
    copies = [
        pltpu.make_async_copy(refs[place], refs[count + place], sems.at[place])
        for place in range(count)
    ]
    for copy in copies:
        copy.start()
    for copy in copies:
        copy.wait()


def token_kernel(slots, at_ref, k_ref, v_ref, *chunk_refs):
    low = at_ref[0]
    tok, width = BLOCK, chunk_refs[0].shape[1]
    for mask in range(slots):
        cols = col_block(low, mask, width)
        chunk_refs[mask][0:tok, :] = k_ref[:, cols]
        chunk_refs[mask][tok:, :] = v_ref[:, cols]


def query_kernel(slots, at_ref, q_ref, mine_ref, w_ref, other_ref, *refs):
    chunk_refs, grad_ref = refs[:slots], refs[slots]
    low, core = at_ref[0], at_ref[1]
    tok, half = mine_ref.shape
    width = chunk_refs[0].shape[1]
    first = pl.multiple_of(core * half, half)
    second = pl.multiple_of((1 - core) * half, half)
    total = mm(mine_ref[...], w_ref[pl.ds(first, half), :])
    total += mm(other_ref[...], w_ref[pl.ds(second, half), :])
    grad_ref[...] = total.astype(BF16)
    for mask in range(slots):
        cols = col_block(low, mask, width)
        chunk_refs[mask][0:tok, :] = q_ref[:, cols]
        chunk_refs[mask][tok:, :] = grad_ref[:, cols]


def coarse_kernel(slots, levels, *refs):
    in_refs, piece_refs = by_mask(refs[:slots]), refs[slots:]
    tok = BLOCK
    for level, piece in zip(levels, piece_refs):
        rows = piece_rows(level)
        pool = level_pool(rows, level)
        for slab in range(slots):
            at = slab * rows
            keys = mm(pool, in_refs[slab][0:tok, :]) * (1.0 / (1 << level))
            piece[at : at + rows, :] = keys.astype(BF16)
            at = (slots + slab) * rows
            piece[at : at + rows, :] = mm(pool, in_refs[slab][tok:, :]).astype(BF16)


def attend_kernel(slots, far_levels, entries, *refs):
    key_refs, query_refs = by_mask(refs[:slots]), by_mask(refs[slots : 2 * slots])
    refs = refs[2 * slots :]
    count = len(entries)
    got_refs, far_refs, refs = refs[:count], refs[count : 2 * count], refs[2 * count :]
    kl_ref, vl_ref, q_all, g_all, prob_ref, grad_ref, sum_ref = refs
    tok = BLOCK
    pairs = slots // 2
    inv_scale = 1.0 / math.sqrt(HDIM)
    to_exp2 = inv_scale * math.log2(math.e)
    near, far = 2 * tok, 3 * tok
    for slab in range(slots):
        pair, row = slab // 2, (slab % 2) * tok
        q_all[pair, row : row + tok, :] = query_refs[slab][0:tok, :]
        g_all[pair, row : row + tok, :] = query_refs[slab][tok:, :]
        kl_ref[pair, row : row + tok, :] = key_refs[slab][0:tok, :]
        vl_ref[pair, row : row + tok, :] = key_refs[slab][tok:, :]
    for (place, part, rows), got_ref in zip(entries, got_refs):
        for slab in range(slots):
            spot = far + place * BLOCK + 32 * slab + part * rows
            for kind, list_ref in enumerate((kl_ref, vl_ref)):
                at = (kind * slots + slab) * rows
                for pair in range(pairs):
                    list_ref[pair, spot : spot + rows, :] = got_ref[at : at + rows, :]
    pool = pool_matrix(BLOCK, 1)
    for pair in range(pairs):
        kl_ref[pair ^ 1, near:far, :] = (mm(pool, kl_ref[pair, 0:near, :]) * 0.5).astype(BF16)
        vl_ref[pair ^ 1, near:far, :] = mm(pool, vl_ref[pair, 0:near, :]).astype(BF16)

    def products(unit):
        pair, head = unit // 2, unit % 2
        lanes = slice(head * HDIM, head * HDIM + HDIM)
        scores = mm_cols(q_all[pair, :, lanes], kl_ref[pair, :, lanes])
        return scores, mm_cols(g_all[pair, :, lanes], vl_ref[pair, :, lanes])

    ready = products(0)
    for unit in range(slots):
        pair, head = unit // 2, unit % 2
        lanes = slice(head * HDIM, head * HDIM + HDIM)
        scores, prob_grad = ready
        if unit + 1 < slots:
            ready = products(unit + 1)
        top = jnp.max(scores, axis=1, keepdims=True)
        raised = jnp.exp2((scores - top) * to_exp2)
        inverse = 1.0 / jnp.sum(raised, axis=1, keepdims=True)
        centre = jnp.sum(raised * prob_grad, axis=1, keepdims=True) * inverse
        prob_ref[unit] = raised.astype(BF16)
        grad_ref[unit] = (raised * (prob_grad - centre)).astype(BF16)
        sum_ref[unit] = jnp.broadcast_to(inverse, (near, HDIM))
        queries = q_all[pair, :, lanes].astype(F32) * (inverse * inv_scale)
        q_all[pair, :, lanes] = queries.astype(BF16)
        g_all[pair, :, lanes] = (g_all[pair, :, lanes].astype(F32) * inverse).astype(BF16)
    for head in range(2):
        lanes = slice(head * HDIM, head * HDIM + HDIM)
        units = [2 * pair + head for pair in range(pairs)]
        for kind, (left_ref, right_ref) in enumerate(((grad_ref, q_all), (prob_ref, g_all))):
            left = jnp.concatenate([left_ref[unit, :, far:] for unit in units], axis=0)
            right = jnp.concatenate([right_ref[pair, :, lanes] for pair in range(pairs)], axis=0)
            total = mm_rows(left, right).astype(BF16)
            for (place, part, rows), out_ref in zip(entries, far_refs):
                for slab in range(slots):
                    start = place * BLOCK + 32 * slab + part * rows
                    at = (kind * slots + slab) * rows
                    out_ref[at : at + rows, lanes] = total[start : start + rows, :]


def reduce_kernel(slots, kl_ref, vl_ref, prob_ref, grad_ref, sum_ref, *home_refs):
    tok = BLOCK
    inv_scale = 1.0 / math.sqrt(HDIM)
    for pair in range(slots // 2):
        for head in range(2):
            lanes = slice(head * HDIM, head * HDIM + HDIM)
            unit = 2 * pair + head
            inverse = sum_ref[unit]
            attended = (mm(prob_ref[unit], vl_ref[pair, :, lanes]) * inverse).astype(BF16)
            query_grad = mm(grad_ref[unit], kl_ref[pair, :, lanes]) * (inverse * inv_scale)
            query_grad = query_grad.astype(BF16)
            for side in range(2):
                rows = slice(side * tok, side * tok + tok)
                home_refs[2 * pair + side][0:tok, lanes] = attended[rows]
                home_refs[2 * pair + side][tok:, lanes] = query_grad[rows]


def local_kernel(slots, q_all, g_all, prob_ref, grad_ref, dk_ref, dv_ref, ck_ref, cv_ref):
    tok = BLOCK
    pairs = slots // 2
    near, far = 2 * tok, 3 * tok
    for pair in range(pairs):
        for head in range(2):
            lanes = slice(head * HDIM, head * HDIM + HDIM)
            unit = 2 * pair + head
            key_terms = mm_rows(grad_ref[unit, :, 0:far], q_all[pair, :, lanes])
            value_terms = mm_rows(prob_ref[unit, :, 0:far], g_all[pair, :, lanes])
            for terms, local, level1 in (
                (key_terms, dk_ref, ck_ref),
                (value_terms, dv_ref, cv_ref),
            ):
                local[pair * near : pair * near + near, lanes] = terms[0:near]
                level1[pair ^ 1, :, lanes] = terms[near:].astype(BF16)
    pool = pool_matrix(BLOCK, 1)
    for pair in range(pairs):
        rows = slice(pair * near, pair * near + near)
        dk_ref[rows, :] += mm_rows(pool, ck_ref[pair]) * 0.5
        dv_ref[rows, :] += mm_rows(pool, cv_ref[pair])


def merge_kernel(slots, levels, dk_ref, dv_ref, *refs):
    far_refs, out_refs = refs[: len(levels)], refs[len(levels) :]
    tok = BLOCK
    key_pools, value_pools = [], []
    for level in levels:
        count = piece_rows(level)
        shape = (slots * count, slots * tok)
        row = lax.broadcasted_iota(jnp.int32, shape, 0)
        col = lax.broadcasted_iota(jnp.int32, shape, 1)
        slab = lax.shift_right_logical(col, tok.bit_length() - 1)
        held = slab * count + lax.shift_right_logical(col & (tok - 1), level)
        key_pools.append(jnp.where(held == row, 1.0 / (1 << level), 0.0).astype(BF16))
        value_pools.append(jnp.where(held == row, 1.0, 0.0).astype(BF16))
    halves = [ref.shape[0] // 2 for ref in far_refs]
    keys = jnp.concatenate([ref[:half, :] for ref, half in zip(far_refs, halves)], axis=0)
    values = jnp.concatenate([ref[half:, :] for ref, half in zip(far_refs, halves)], axis=0)
    key_sum = dk_ref[...] + mm_rows(jnp.concatenate(key_pools, axis=0), keys)
    value_sum = dv_ref[...] + mm_rows(jnp.concatenate(value_pools, axis=0), values)
    for slab in range(slots):
        rows = slice(slab * tok, slab * tok + tok)
        out_refs[slab][0:tok, :] = key_sum[rows].astype(BF16)
        out_refs[slab][tok:, :] = value_sum[rows].astype(BF16)


def flip_kernel(w_ref, out_ref):
    half = out_ref.shape[0]
    for place in range(w_ref.shape[0] // half):
        rows = slice(place * half, place * half + half)
        out_ref[:, rows] = w_ref[rows, :].T


def send_kernel(slots, at_ref, w_ref, *refs):
    in_refs, att_ref, send_refs = by_mask(refs[:slots], BACK), refs[slots], refs[slots + 1 :]
    low, core = at_ref[0], at_ref[1]
    tok, half = att_ref.shape
    width = in_refs[0].shape[1]
    for mask in range(slots):
        att_ref[:, col_block(low, mask, width)] = in_refs[mask][0:tok, :]
    part = half // len(send_refs)
    for place, send_ref in enumerate(send_refs):
        other = pl.multiple_of((1 - core) * half + place * part, part)
        send_ref[...] = mm(att_ref[...], w_ref[:, pl.ds(other, part)]).astype(BF16)


def keep_kernel(slots, at_ref, w_ref, att_ref, *refs):
    home_refs, (keep_ref, dq_ref) = by_mask(refs[:slots], BACK), refs[slots:]
    tok, half = att_ref.shape
    width = home_refs[0].shape[1]
    for mask in range(slots):
        dq_ref[:, col_block(at_ref[0], mask, width)] = home_refs[mask][tok:, :]
    first = pl.multiple_of(at_ref[1] * half, half)
    keep_ref[...] = mm(att_ref[...], w_ref[:, pl.ds(first, half)])


def add_kernel(keep_ref, *refs):
    got_refs, out_ref = refs[:-1], refs[-1]
    part = got_refs[0].shape[1]
    for place, got_ref in enumerate(got_refs):
        cols = slice(place * part, place * part + part)
        out_ref[:, cols] = (keep_ref[:, cols] + got_ref[...].astype(F32)).astype(BF16)


def finish_kernel(slots, at_ref, out_ref, dq_ref, *refs):
    last_refs, refs = by_mask(refs[:slots], BACK), refs[slots:]
    hbm_refs, (dk_ref, dv_ref, sems) = refs[:4], refs[4:]
    tok, width = BLOCK, last_refs[0].shape[1]
    copies = [
        pltpu.make_async_copy(source, hbm_refs[place], sems.at[place])
        for place, source in enumerate((out_ref, dq_ref, dk_ref, dv_ref))
    ]
    copies[0].start()
    copies[1].start()
    for place, held_ref in enumerate((dk_ref, dv_ref)):
        rows = slice(place * tok, place * tok + tok)
        for mask in range(slots):
            held_ref[:, col_block(at_ref[0], mask, width)] = last_refs[mask][rows, :]
        copies[2 + place].start()
    for copy in copies:
        copy.wait()


def straight(levels, slots):
    return all((slots << place) * 4 <= 32 for place in range(len(levels)))


def far_entries(levels, slots):
    entries, masks = [], []
    for place, level in enumerate(levels):
        if not straight(levels, slots):
            entries.append((place, 0, 32))
            continue
        for part in range(1 << place):
            entries.append((place, part, BLOCK >> level))
            masks.append(1 << level ^ part * slots)
    return entries, masks


def gather_far(pieces, levels, slots):
    width = pieces[0].shape[1]
    if straight(levels, slots):
        entries, masks = far_entries(levels, slots)
        return [swap_seq(pieces[entry[0]], mask) for entry, mask in zip(entries, masks)]
    held = {}
    for place, level in enumerate(levels):
        block = pieces[place].reshape(2 * slots, piece_rows(level), width)
        held[level] = block[:, None, : BLOCK >> level]
    found = []
    for step in levels:
        sent = [held[level].reshape(-1, width) for level in levels if level >= step]
        got = swap_seq(jnp.concatenate(sent, axis=0), 1 << step)
        first = 0
        for level in levels:
            if level < step:
                continue
            count = held[level].size // width
            part = got[first : first + count].reshape(held[level].shape)
            first += count
            if level == step:
                found.append(part.reshape(-1, width))
            else:
                held[level] = jnp.concatenate([held[level], part], axis=1)
    return found


def scatter_far(packed, levels, slots):
    width = packed[0].shape[1]
    if straight(levels, slots):
        entries, masks = far_entries(levels, slots)
        shares = [swap_seq(array, mask) for array, mask in zip(packed, masks)]
        return shares, [levels[entry[0]] for entry in entries]
    blocks = {}
    for place, level in enumerate(levels):
        rows = BLOCK >> level
        blocks[level] = packed[place].reshape(2 * slots, 32 // rows, rows, width)
    ready = {}
    for step in reversed(levels):
        sent, kept = [blocks[step].reshape(-1, width)], {}
        for level in levels:
            if level > step:
                size = ready[level].shape[1] // 2
                kept[level] = ready[level][:, :size]
                sent.append(ready[level][:, size:].astype(BF16).reshape(-1, width))
        got = swap_seq(jnp.concatenate(sent, axis=0), 1 << step)
        first = blocks[step].size // width
        ready[step] = got[0:first].reshape(blocks[step].shape)
        for level in kept:
            count = kept[level].size // width
            part = got[first : first + count].reshape(kept[level].shape)
            first += count
            ready[level] = kept[level].astype(F32) + part.astype(F32)
    shares = []
    for level in levels:
        share = ready[level].astype(BF16).reshape(2 * slots, -1, width)
        pad = piece_rows(level) - share.shape[1]
        if pad:
            share = jnp.pad(share, ((0, 0), (0, pad), (0, 0)))
        shares.append(share.reshape(-1, width))
    return shares, list(levels)


def on_device(queries, key_tokens, value_tokens, out_weight, output_grad):
    tok, columns = queries.shape
    heads = columns // HDIM
    slots = heads // 2
    width = columns // slots
    local_levels = slots.bit_length() - 1
    level_count = lax.axis_size("seq").bit_length() - 1
    far = list(range(local_levels, level_count))
    list_rows = 3 * tok + BLOCK * len(far)
    entries, _ = far_entries(far, slots)
    place = jnp.stack([lax.axis_index("seq") & (slots - 1), lax.axis_index("head")])
    place = place.astype(jnp.int32)

    def shape(dims, dtype=BF16):
        return jax.ShapeDtypeStruct(dims, dtype)

    def over(rows):
        return [shape((rows, width))] * slots

    def exchange(chunks, order=ORDER):
        moved = [chunks[0]] + [swap_seq(chunks[mask], mask) for mask in range(1, slots)]
        return [moved[mask] for mask in order]

    held = call(
        load_kernel,
        [shape((tok, columns))] * 2,
        [key_tokens, value_tokens],
        scratch=[pltpu.SemaphoreType.DMA((2,))],
        specs=[HBM] * 2,
        vmem=8,
    )
    chunks = call(
        lambda *refs: token_kernel(slots, *refs),
        over(2 * tok),
        [place] + list(held),
        flops=6 * 10**9,
        specs=[SMEM] + [VMEM] * 2,
        vmem=8,
    )
    keys = exchange(chunks)
    later, *_ = lax.optimization_barrier((place, *chunks))
    other_grad = swap_head(output_grad)
    chunks = call(
        lambda *refs: query_kernel(slots, *refs),
        over(2 * tok),
        [later, queries, output_grad, out_weight, other_grad],
        scratch=[pltpu.VMEM((tok, columns), BF16)],
        flops=6 * 10**9,
        specs=[SMEM] + [VMEM] * 4,
        vmem=16,
    )
    asked = exchange(chunks)
    flipped = call(
        flip_kernel,
        shape(out_weight.shape[::-1]),
        [out_weight],
        vmem=24,
        free=True,
    )
    sources, flipped, *_ = lax.optimization_barrier((keys, flipped, asked[1]))
    pieces = call(
        lambda *refs: coarse_kernel(slots, far, *refs),
        [shape((2 * slots * piece_rows(level), width)) for level in far],
        sources,
        vmem=8,
    )
    far_got = gather_far(pieces, far, slots)
    pairs = slots // 2
    made = call(
        lambda *refs: attend_kernel(slots, len(far), entries, *refs),
        [shape((2 * slots * rows, width)) for _, _, rows in entries]
        + [shape((pairs, list_rows, width))] * 2
        + [shape((pairs, 2 * tok, width))] * 2
        + [shape((slots, 2 * tok, list_rows))] * 2
        + [shape((slots, 2 * tok, HDIM), F32)],
        keys + asked + far_got,
        flops=6 * heads * tok * list_rows * HDIM,
    )
    shares, share_levels = scatter_far(made[: len(entries)], far, slots)
    key_list, value_list, asked, grads, probs, score_grads, sums = made[len(entries) :]
    made = call(
        lambda *refs: reduce_kernel(slots, *refs),
        over(2 * tok),
        [key_list, value_list, probs, score_grads, sums],
        flops=6 * 10**9,
        vmem=16,
    )
    key_sum, value_sum = call(
        lambda *refs: local_kernel(slots, *refs),
        [shape((slots * tok, width), F32)] * 2,
        [asked, grads, probs, score_grads],
        scratch=[pltpu.VMEM((pairs, BLOCK, width), BF16)] * 2,
        flops=4 * heads * tok * list_rows * HDIM,
        vmem=16,
    )
    made = list(made)
    late = BACK[-1]
    made[late], key_sum, *shares = lax.optimization_barrier((made[late], key_sum, *shares))
    home = exchange(made, BACK)
    chunks = call(
        lambda *refs: merge_kernel(slots, share_levels, *refs),
        over(2 * tok),
        [key_sum, value_sum] + shares,
        vmem=8,
    )
    home, _ = lax.optimization_barrier((home, chunks))
    chunks = list(chunks)
    last = exchange(chunks, BACK)
    wide = shape((tok, columns))
    attended, *send = call(
        lambda *refs: send_kernel(slots, *refs),
        [wide] + [shape((tok, columns))],
        [place, flipped] + home,
        flops=2 * tok * columns * columns,
        specs=[SMEM] + [VMEM] * (1 + slots),
        vmem=16,
    )
    got = [swap_head(part) for part in send]
    keep, query_grad = call(
        lambda *refs: keep_kernel(slots, *refs),
        [shape((tok, columns), F32), wide],
        [place, flipped, attended] + home,
        flops=4 * 10**9,
        specs=[SMEM] + [VMEM] * (2 + slots),
        vmem=16,
    )
    output = call(add_kernel, wide, [keep] + got, vmem=8)
    output, query_grad, key_grad, value_grad = call(
        lambda *refs: finish_kernel(slots, *refs),
        [wide] * 4,
        [place, output, query_grad] + last,
        scratch=[pltpu.VMEM((tok, columns), BF16)] * 2 + [pltpu.SemaphoreType.DMA((4,))],
        specs=[SMEM] + [VMEM] * (2 + slots),
        outs=HBM,
        vmem=8,
    )
    return output, query_grad, key_grad, value_grad


def solution(mesh):
    placed = P("seq", "head")
    return jax.shard_map(
        on_device,
        mesh=mesh,
        in_specs=(placed, placed, placed, P(None, "head"), placed),
        out_specs=(placed, placed, placed, placed),
        check_vma=False,
    )
```

```python
import math

import jax
import jax.numpy as jnp
from jax import lax
from jax.experimental import pallas as pl
from jax.experimental.pallas import tpu as pltpu
from jax.sharding import PartitionSpec as P

HDIM = 128
ORDER = (0, 1, 2, 3)
BACK = (0, 3, 1, 2)
BLOCK = 128
BF16 = jnp.bfloat16
F32 = jnp.float32
VMEM = pl.BlockSpec(memory_space=pltpu.VMEM)
SMEM = pl.BlockSpec(memory_space=pltpu.SMEM)
HBM = pl.BlockSpec(memory_space=pltpu.HBM)


def swap_seq(array, mask):
    return lax.ppermute(array, "seq", [(i, i ^ mask) for i in range(lax.axis_size("seq"))])


def swap_head(array):
    return lax.ppermute(array, "head", [(0, 1), (1, 0)])


def mm(left, right):
    return jnp.dot(left, right, preferred_element_type=F32)


def mm_cols(left, right):
    return lax.dot_general(left, right, (((1,), (1,)), ((), ())), preferred_element_type=F32)


def mm_rows(left, right):
    return lax.dot_general(left, right, (((0,), (0,)), ((), ())), preferred_element_type=F32)


def pool_matrix(rows, shift):
    shape = (rows, rows << shift)
    row = lax.broadcasted_iota(jnp.int32, shape, 0)
    col = lax.broadcasted_iota(jnp.int32, shape, 1)
    return jnp.where(lax.shift_right_logical(col, shift) == row, 1.0, 0.0).astype(BF16)


def call(kernel, out_shape, operands, scratch=(), flops=0, vmem=24, specs=None, outs=VMEM, free=False):
    specs = specs or [VMEM] * len(operands)
    operands = [
        pltpu.with_memory_space_constraint(x, pltpu.HBM) if spec is HBM else x
        for x, spec in zip(operands, specs)
    ]
    moved = 0 if free else sum(x.size * x.dtype.itemsize for x in operands)
    return pl.pallas_call(
        kernel,
        out_shape=out_shape,
        in_specs=specs,
        out_specs=jax.tree.map(lambda _: outs, out_shape),
        scratch_shapes=list(scratch),
        compiler_params=pltpu.CompilerParams(vmem_limit_bytes=vmem << 20),
        cost_estimate=pl.CostEstimate(flops=flops, bytes_accessed=moved, transcendentals=0),
    )(*operands)


def by_mask(refs, order=ORDER):
    return [refs[order.index(mask)] for mask in range(len(refs))]


def level_pool(rows, level):
    row = lax.broadcasted_iota(jnp.int32, (rows, BLOCK), 0)
    col = lax.broadcasted_iota(jnp.int32, (rows, BLOCK), 1)
    return jnp.where(lax.shift_right_logical(col, level) == row, 1.0, 0.0).astype(BF16)


def col_block(low, mask, width):
    return pl.ds(pl.multiple_of((low ^ mask) * width, width), width)


def piece_rows(level):
    return max(16, BLOCK >> level)


def load_kernel(*refs):
    count = len(refs) // 2
    sems = refs[-1]
    copies = [
        pltpu.make_async_copy(refs[place], refs[count + place], sems.at[place])
        for place in range(count)
    ]
    for copy in copies:
        copy.start()
    for copy in copies:
        copy.wait()


def token_kernel(slots, at_ref, k_ref, v_ref, *chunk_refs):
    low = at_ref[0]
    tok, width = BLOCK, chunk_refs[0].shape[1]
    for mask in range(slots):
        cols = col_block(low, mask, width)
        chunk_refs[mask][0:tok, :] = k_ref[:, cols]
        chunk_refs[mask][tok:, :] = v_ref[:, cols]


def query_kernel(slots, at_ref, q_ref, mine_ref, w_ref, other_ref, *refs):
    chunk_refs, grad_ref = refs[:slots], refs[slots]
    low, core = at_ref[0], at_ref[1]
    tok, half = mine_ref.shape
    width = chunk_refs[0].shape[1]
    first = pl.multiple_of(core * half, half)
    second = pl.multiple_of((1 - core) * half, half)
    total = mm(mine_ref[...], w_ref[pl.ds(first, half), :])
    total += mm(other_ref[...], w_ref[pl.ds(second, half), :])
    grad_ref[...] = total.astype(BF16)
    for mask in range(slots):
        cols = col_block(low, mask, width)
        chunk_refs[mask][0:tok, :] = q_ref[:, cols]
        chunk_refs[mask][tok:, :] = grad_ref[:, cols]


def coarse_kernel(slots, levels, *refs):
    in_refs, piece_refs = by_mask(refs[:slots]), refs[slots:]
    tok = BLOCK
    for level, piece in zip(levels, piece_refs):
        rows = piece_rows(level)
        pool = level_pool(rows, level)
        for slab in range(slots):
            at = slab * rows
            keys = mm(pool, in_refs[slab][0:tok, :]) * (1.0 / (1 << level))
            piece[at : at + rows, :] = keys.astype(BF16)
            at = (slots + slab) * rows
            piece[at : at + rows, :] = mm(pool, in_refs[slab][tok:, :]).astype(BF16)


def attend_kernel(slots, far_levels, entries, *refs):
    key_refs, query_refs = by_mask(refs[:slots]), by_mask(refs[slots : 2 * slots])
    refs = refs[2 * slots :]
    count = len(entries)
    got_refs, far_refs, refs = refs[:count], refs[count : 2 * count], refs[2 * count :]
    kl_ref, vl_ref, q_all, g_all, prob_ref, grad_ref, sum_ref = refs
    tok = BLOCK
    pairs = slots // 2
    inv_scale = 1.0 / math.sqrt(HDIM)
    to_exp2 = inv_scale * math.log2(math.e)
    near, far = 2 * tok, 3 * tok
    for slab in range(slots):
        pair, row = slab // 2, (slab % 2) * tok
        q_all[pair, row : row + tok, :] = query_refs[slab][0:tok, :]
        g_all[pair, row : row + tok, :] = query_refs[slab][tok:, :]
        kl_ref[pair, row : row + tok, :] = key_refs[slab][0:tok, :]
        vl_ref[pair, row : row + tok, :] = key_refs[slab][tok:, :]
    for (place, part, rows), got_ref in zip(entries, got_refs):
        for slab in range(slots):
            spot = far + place * BLOCK + 32 * slab + part * rows
            for kind, list_ref in enumerate((kl_ref, vl_ref)):
                at = (kind * slots + slab) * rows
                for pair in range(pairs):
                    list_ref[pair, spot : spot + rows, :] = got_ref[at : at + rows, :]
    pool = pool_matrix(BLOCK, 1)
    for pair in range(pairs):
        kl_ref[pair ^ 1, near:far, :] = (mm(pool, kl_ref[pair, 0:near, :]) * 0.5).astype(BF16)
        vl_ref[pair ^ 1, near:far, :] = mm(pool, vl_ref[pair, 0:near, :]).astype(BF16)

    def products(unit):
        pair, head = unit // 2, unit % 2
        lanes = slice(head * HDIM, head * HDIM + HDIM)
        scores = mm_cols(q_all[pair, :, lanes], kl_ref[pair, :, lanes])
        return scores, mm_cols(g_all[pair, :, lanes], vl_ref[pair, :, lanes])

    ready = products(0)
    for unit in range(slots):
        pair, head = unit // 2, unit % 2
        lanes = slice(head * HDIM, head * HDIM + HDIM)
        scores, prob_grad = ready
        if unit + 1 < slots:
            ready = products(unit + 1)
        top = jnp.max(scores, axis=1, keepdims=True)
        raised = jnp.exp2((scores - top) * to_exp2)
        inverse = 1.0 / jnp.sum(raised, axis=1, keepdims=True)
        centre = jnp.sum(raised * prob_grad, axis=1, keepdims=True) * inverse
        prob_ref[unit] = raised.astype(BF16)
        grad_ref[unit] = (raised * (prob_grad - centre)).astype(BF16)
        sum_ref[unit] = jnp.broadcast_to(inverse, (near, HDIM))
        queries = q_all[pair, :, lanes].astype(F32) * (inverse * inv_scale)
        q_all[pair, :, lanes] = queries.astype(BF16)
        g_all[pair, :, lanes] = (g_all[pair, :, lanes].astype(F32) * inverse).astype(BF16)
    for head in range(2):
        lanes = slice(head * HDIM, head * HDIM + HDIM)
        units = [2 * pair + head for pair in range(pairs)]
        for kind, (left_ref, right_ref) in enumerate(((grad_ref, q_all), (prob_ref, g_all))):
            left = jnp.concatenate([left_ref[unit, :, far:] for unit in units], axis=0)
            right = jnp.concatenate([right_ref[pair, :, lanes] for pair in range(pairs)], axis=0)
            total = mm_rows(left, right).astype(BF16)
            for (place, part, rows), out_ref in zip(entries, far_refs):
                for slab in range(slots):
                    start = place * BLOCK + 32 * slab + part * rows
                    at = (kind * slots + slab) * rows
                    out_ref[at : at + rows, lanes] = total[start : start + rows, :]


def reduce_kernel(slots, kl_ref, vl_ref, prob_ref, grad_ref, sum_ref, *home_refs):
    tok = BLOCK
    inv_scale = 1.0 / math.sqrt(HDIM)
    for pair in range(slots // 2):
        for head in range(2):
            lanes = slice(head * HDIM, head * HDIM + HDIM)
            unit = 2 * pair + head
            inverse = sum_ref[unit]
            attended = (mm(prob_ref[unit], vl_ref[pair, :, lanes]) * inverse).astype(BF16)
            query_grad = mm(grad_ref[unit], kl_ref[pair, :, lanes]) * (inverse * inv_scale)
            query_grad = query_grad.astype(BF16)
            for side in range(2):
                rows = slice(side * tok, side * tok + tok)
                home_refs[2 * pair + side][0:tok, lanes] = attended[rows]
                home_refs[2 * pair + side][tok:, lanes] = query_grad[rows]


def local_kernel(slots, q_all, g_all, prob_ref, grad_ref, dk_ref, dv_ref, ck_ref, cv_ref):
    tok = BLOCK
    pairs = slots // 2
    near, far = 2 * tok, 3 * tok
    for pair in range(pairs):
        for head in range(2):
            lanes = slice(head * HDIM, head * HDIM + HDIM)
            unit = 2 * pair + head
            key_terms = mm_rows(grad_ref[unit, :, 0:far], q_all[pair, :, lanes])
            value_terms = mm_rows(prob_ref[unit, :, 0:far], g_all[pair, :, lanes])
            for terms, local, level1 in (
                (key_terms, dk_ref, ck_ref),
                (value_terms, dv_ref, cv_ref),
            ):
                local[pair * near : pair * near + near, lanes] = terms[0:near]
                level1[pair ^ 1, :, lanes] = terms[near:].astype(BF16)
    pool = pool_matrix(BLOCK, 1)
    for pair in range(pairs):
        rows = slice(pair * near, pair * near + near)
        dk_ref[rows, :] += mm_rows(pool, ck_ref[pair]) * 0.5
        dv_ref[rows, :] += mm_rows(pool, cv_ref[pair])


def merge_kernel(slots, levels, dk_ref, dv_ref, *refs):
    far_refs, out_refs = refs[: len(levels)], refs[len(levels) :]
    tok = BLOCK
    key_pools, value_pools = [], []
    for level in levels:
        count = piece_rows(level)
        shape = (slots * count, slots * tok)
        row = lax.broadcasted_iota(jnp.int32, shape, 0)
        col = lax.broadcasted_iota(jnp.int32, shape, 1)
        slab = lax.shift_right_logical(col, tok.bit_length() - 1)
        held = slab * count + lax.shift_right_logical(col & (tok - 1), level)
        key_pools.append(jnp.where(held == row, 1.0 / (1 << level), 0.0).astype(BF16))
        value_pools.append(jnp.where(held == row, 1.0, 0.0).astype(BF16))
    halves = [ref.shape[0] // 2 for ref in far_refs]
    keys = jnp.concatenate([ref[:half, :] for ref, half in zip(far_refs, halves)], axis=0)
    values = jnp.concatenate([ref[half:, :] for ref, half in zip(far_refs, halves)], axis=0)
    key_sum = dk_ref[...] + mm_rows(jnp.concatenate(key_pools, axis=0), keys)
    value_sum = dv_ref[...] + mm_rows(jnp.concatenate(value_pools, axis=0), values)
    for slab in range(slots):
        rows = slice(slab * tok, slab * tok + tok)
        out_refs[slab][0:tok, :] = key_sum[rows].astype(BF16)
        out_refs[slab][tok:, :] = value_sum[rows].astype(BF16)


def flip_kernel(w_ref, out_ref):
    half = out_ref.shape[0]
    for place in range(w_ref.shape[0] // half):
        rows = slice(place * half, place * half + half)
        out_ref[:, rows] = w_ref[rows, :].T


def send_kernel(slots, at_ref, w_ref, *refs):
    in_refs, att_ref, send_refs = by_mask(refs[:slots], BACK), refs[slots], refs[slots + 1 :]
    low, core = at_ref[0], at_ref[1]
    tok, half = att_ref.shape
    width = in_refs[0].shape[1]
    for mask in range(slots):
        att_ref[:, col_block(low, mask, width)] = in_refs[mask][0:tok, :]
    part = half // len(send_refs)
    for place, send_ref in enumerate(send_refs):
        other = pl.multiple_of((1 - core) * half + place * part, part)
        send_ref[...] = mm(att_ref[...], w_ref[:, pl.ds(other, part)]).astype(BF16)


def keep_kernel(slots, at_ref, w_ref, att_ref, *refs):
    home_refs, (keep_ref, dq_ref) = by_mask(refs[:slots], BACK), refs[slots:]
    tok, half = att_ref.shape
    width = home_refs[0].shape[1]
    for mask in range(slots):
        dq_ref[:, col_block(at_ref[0], mask, width)] = home_refs[mask][tok:, :]
    first = pl.multiple_of(at_ref[1] * half, half)
    keep_ref[...] = mm(att_ref[...], w_ref[:, pl.ds(first, half)])


def add_kernel(keep_ref, *refs):
    got_refs, out_ref = refs[:-1], refs[-1]
    part = got_refs[0].shape[1]
    for place, got_ref in enumerate(got_refs):
        cols = slice(place * part, place * part + part)
        out_ref[:, cols] = (keep_ref[:, cols] + got_ref[...].astype(F32)).astype(BF16)


def finish_kernel(slots, at_ref, out_ref, dq_ref, *refs):
    last_refs, refs = by_mask(refs[:slots], BACK), refs[slots:]
    hbm_refs, (dk_ref, dv_ref, sems) = refs[:4], refs[4:]
    tok, width = BLOCK, last_refs[0].shape[1]
    copies = [
        pltpu.make_async_copy(source, hbm_refs[place], sems.at[place])
        for place, source in enumerate((out_ref, dq_ref, dk_ref, dv_ref))
    ]
    copies[0].start()
    copies[1].start()
    for place, held_ref in enumerate((dk_ref, dv_ref)):
        rows = slice(place * tok, place * tok + tok)
        for mask in range(slots):
            held_ref[:, col_block(at_ref[0], mask, width)] = last_refs[mask][rows, :]
        copies[2 + place].start()
    for copy in copies:
        copy.wait()


def straight(levels, slots):
    return all((slots << place) * 4 <= 32 for place in range(len(levels)))


def far_entries(levels, slots):
    entries, masks = [], []
    for place, level in enumerate(levels):
        if not straight(levels, slots):
            entries.append((place, 0, 32))
            continue
        for part in range(1 << place):
            entries.append((place, part, BLOCK >> level))
            masks.append(1 << level ^ part * slots)
    return entries, masks


def gather_far(pieces, levels, slots):
    width = pieces[0].shape[1]
    if straight(levels, slots):
        entries, masks = far_entries(levels, slots)
        return [swap_seq(pieces[entry[0]], mask) for entry, mask in zip(entries, masks)]
    held = {}
    for place, level in enumerate(levels):
        block = pieces[place].reshape(2 * slots, piece_rows(level), width)
        held[level] = block[:, None, : BLOCK >> level]
    found = []
    for step in levels:
        sent = [held[level].reshape(-1, width) for level in levels if level >= step]
        got = swap_seq(jnp.concatenate(sent, axis=0), 1 << step)
        first = 0
        for level in levels:
            if level < step:
                continue
            count = held[level].size // width
            part = got[first : first + count].reshape(held[level].shape)
            first += count
            if level == step:
                found.append(part.reshape(-1, width))
            else:
                held[level] = jnp.concatenate([held[level], part], axis=1)
    return found


def scatter_far(packed, levels, slots):
    width = packed[0].shape[1]
    if straight(levels, slots):
        entries, masks = far_entries(levels, slots)
        shares = [swap_seq(array, mask) for array, mask in zip(packed, masks)]
        return shares, [levels[entry[0]] for entry in entries]
    blocks = {}
    for place, level in enumerate(levels):
        rows = BLOCK >> level
        blocks[level] = packed[place].reshape(2 * slots, 32 // rows, rows, width)
    ready = {}
    for step in reversed(levels):
        sent, kept = [blocks[step].reshape(-1, width)], {}
        for level in levels:
            if level > step:
                size = ready[level].shape[1] // 2
                kept[level] = ready[level][:, :size]
                sent.append(ready[level][:, size:].astype(BF16).reshape(-1, width))
        got = swap_seq(jnp.concatenate(sent, axis=0), 1 << step)
        first = blocks[step].size // width
        ready[step] = got[0:first].reshape(blocks[step].shape)
        for level in kept:
            count = kept[level].size // width
            part = got[first : first + count].reshape(kept[level].shape)
            first += count
            ready[level] = kept[level].astype(F32) + part.astype(F32)
    shares = []
    for level in levels:
        share = ready[level].astype(BF16).reshape(2 * slots, -1, width)
        pad = piece_rows(level) - share.shape[1]
        if pad:
            share = jnp.pad(share, ((0, 0), (0, pad), (0, 0)))
        shares.append(share.reshape(-1, width))
    return shares, list(levels)


def on_device(queries, key_tokens, value_tokens, out_weight, output_grad):
    tok, columns = queries.shape
    heads = columns // HDIM
    slots = heads // 2
    width = columns // slots
    local_levels = slots.bit_length() - 1
    level_count = lax.axis_size("seq").bit_length() - 1
    far = list(range(local_levels, level_count))
    list_rows = 3 * tok + BLOCK * len(far)
    entries, _ = far_entries(far, slots)
    place = jnp.stack([lax.axis_index("seq") & (slots - 1), lax.axis_index("head")])
    place = place.astype(jnp.int32)

    def shape(dims, dtype=BF16):
        return jax.ShapeDtypeStruct(dims, dtype)

    def over(rows):
        return [shape((rows, width))] * slots

    def exchange(chunks, order=ORDER):
        moved = [chunks[0]] + [swap_seq(chunks[mask], mask) for mask in range(1, slots)]
        return [moved[mask] for mask in order]

    held = call(
        load_kernel,
        [shape((tok, columns))] * 2,
        [key_tokens, value_tokens],
        scratch=[pltpu.SemaphoreType.DMA((2,))],
        specs=[HBM] * 2,
        vmem=8,
    )
    chunks = call(
        lambda *refs: token_kernel(slots, *refs),
        over(2 * tok),
        [place] + list(held),
        flops=6 * 10**9,
        specs=[SMEM] + [VMEM] * 2,
        vmem=8,
    )
    keys = exchange(chunks)
    later, *_ = lax.optimization_barrier((place, *chunks))
    other_grad = swap_head(output_grad)
    chunks = call(
        lambda *refs: query_kernel(slots, *refs),
        over(2 * tok),
        [later, queries, output_grad, out_weight, other_grad],
        scratch=[pltpu.VMEM((tok, columns), BF16)],
        flops=6 * 10**9,
        specs=[SMEM] + [VMEM] * 4,
        vmem=16,
    )
    asked = exchange(chunks)
    flipped = call(
        flip_kernel,
        shape(out_weight.shape[::-1]),
        [out_weight],
        vmem=24,
        free=True,
    )
    sources, flipped, *_ = lax.optimization_barrier((keys, flipped, asked[1]))
    pieces = call(
        lambda *refs: coarse_kernel(slots, far, *refs),
        [shape((2 * slots * piece_rows(level), width)) for level in far],
        sources,
        vmem=8,
    )
    far_got = gather_far(pieces, far, slots)
    pairs = slots // 2
    made = call(
        lambda *refs: attend_kernel(slots, len(far), entries, *refs),
        [shape((2 * slots * rows, width)) for _, _, rows in entries]
        + [shape((pairs, list_rows, width))] * 2
        + [shape((pairs, 2 * tok, width))] * 2
        + [shape((slots, 2 * tok, list_rows))] * 2
        + [shape((slots, 2 * tok, HDIM), F32)],
        keys + asked + far_got,
        flops=6 * heads * tok * list_rows * HDIM,
    )
    shares, share_levels = scatter_far(made[: len(entries)], far, slots)
    key_list, value_list, asked, grads, probs, score_grads, sums = made[len(entries) :]
    made = call(
        lambda *refs: reduce_kernel(slots, *refs),
        over(2 * tok),
        [key_list, value_list, probs, score_grads, sums],
        flops=6 * 10**9,
        vmem=16,
    )
    key_sum, value_sum = call(
        lambda *refs: local_kernel(slots, *refs),
        [shape((slots * tok, width), F32)] * 2,
        [asked, grads, probs, score_grads],
        scratch=[pltpu.VMEM((pairs, BLOCK, width), BF16)] * 2,
        flops=4 * heads * tok * list_rows * HDIM,
        vmem=16,
    )
    made = list(made)
    late = BACK[-1]
    made[late], *shares = lax.optimization_barrier((made[late], *shares))
    home = exchange(made, BACK)
    chunks = call(
        lambda *refs: merge_kernel(slots, share_levels, *refs),
        over(2 * tok),
        [key_sum, value_sum] + shares,
        vmem=8,
    )
    home, _ = lax.optimization_barrier((home, chunks))
    chunks = list(chunks)
    last = exchange(chunks, BACK)
    wide = shape((tok, columns))
    attended, *send = call(
        lambda *refs: send_kernel(slots, *refs),
        [wide] + [shape((tok, columns))],
        [place, flipped] + home,
        flops=2 * tok * columns * columns,
        specs=[SMEM] + [VMEM] * (1 + slots),
        vmem=16,
    )
    got = [swap_head(part) for part in send]
    keep, query_grad = call(
        lambda *refs: keep_kernel(slots, *refs),
        [shape((tok, columns), F32), wide],
        [place, flipped, attended] + home,
        flops=4 * 10**9,
        specs=[SMEM] + [VMEM] * (2 + slots),
        vmem=16,
    )
    output = call(add_kernel, wide, [keep] + got, vmem=8)
    output, query_grad, key_grad, value_grad = call(
        lambda *refs: finish_kernel(slots, *refs),
        [wide] * 4,
        [place, output, query_grad] + last,
        scratch=[pltpu.VMEM((tok, columns), BF16)] * 2 + [pltpu.SemaphoreType.DMA((4,))],
        specs=[SMEM] + [VMEM] * (2 + slots),
        outs=HBM,
        vmem=8,
    )
    return output, query_grad, key_grad, value_grad


def solution(mesh):
    placed = P("seq", "head")
    return jax.shard_map(
        on_device,
        mesh=mesh,
        in_specs=(placed, placed, placed, P(None, "head"), placed),
        out_specs=(placed, placed, placed, placed),
        check_vma=False,
    )
```

```python
import math

import jax
import jax.numpy as jnp
from jax import lax
from jax.experimental import pallas as pl
from jax.experimental.pallas import tpu as pltpu
from jax.sharding import PartitionSpec as P

HDIM = 128
ORDER = (0, 1, 2, 3)
BACK = (0, 3, 1, 2)
BLOCK = 128
BF16 = jnp.bfloat16
F32 = jnp.float32
VMEM = pl.BlockSpec(memory_space=pltpu.VMEM)
SMEM = pl.BlockSpec(memory_space=pltpu.SMEM)
HBM = pl.BlockSpec(memory_space=pltpu.HBM)


def swap_seq(array, mask):
    return lax.ppermute(array, "seq", [(i, i ^ mask) for i in range(lax.axis_size("seq"))])


def swap_head(array):
    return lax.ppermute(array, "head", [(0, 1), (1, 0)])


def mm(left, right):
    return jnp.dot(left, right, preferred_element_type=F32)


def mm_cols(left, right):
    return lax.dot_general(left, right, (((1,), (1,)), ((), ())), preferred_element_type=F32)


def mm_rows(left, right):
    return lax.dot_general(left, right, (((0,), (0,)), ((), ())), preferred_element_type=F32)


def pool_matrix(rows, shift):
    shape = (rows, rows << shift)
    row = lax.broadcasted_iota(jnp.int32, shape, 0)
    col = lax.broadcasted_iota(jnp.int32, shape, 1)
    return jnp.where(lax.shift_right_logical(col, shift) == row, 1.0, 0.0).astype(BF16)


def call(kernel, out_shape, operands, scratch=(), flops=0, vmem=24, specs=None, outs=VMEM, free=False):
    specs = specs or [VMEM] * len(operands)
    operands = [
        pltpu.with_memory_space_constraint(x, pltpu.HBM) if spec is HBM else x
        for x, spec in zip(operands, specs)
    ]
    moved = 0 if free else sum(x.size * x.dtype.itemsize for x in operands)
    return pl.pallas_call(
        kernel,
        out_shape=out_shape,
        in_specs=specs,
        out_specs=jax.tree.map(lambda _: outs, out_shape),
        scratch_shapes=list(scratch),
        compiler_params=pltpu.CompilerParams(vmem_limit_bytes=vmem << 20),
        cost_estimate=pl.CostEstimate(flops=flops, bytes_accessed=moved, transcendentals=0),
    )(*operands)


def by_mask(refs, order=ORDER):
    return [refs[order.index(mask)] for mask in range(len(refs))]


def level_pool(rows, level):
    row = lax.broadcasted_iota(jnp.int32, (rows, BLOCK), 0)
    col = lax.broadcasted_iota(jnp.int32, (rows, BLOCK), 1)
    return jnp.where(lax.shift_right_logical(col, level) == row, 1.0, 0.0).astype(BF16)


def col_block(low, mask, width):
    return pl.ds(pl.multiple_of((low ^ mask) * width, width), width)


def piece_rows(level):
    return max(16, BLOCK >> level)


def load_kernel(*refs):
    count = len(refs) // 2
    sems = refs[-1]
    copies = [
        pltpu.make_async_copy(refs[place], refs[count + place], sems.at[place])
        for place in range(count)
    ]
    for copy in copies:
        copy.start()
    for copy in copies:
        copy.wait()


def token_kernel(slots, at_ref, k_ref, v_ref, *chunk_refs):
    low = at_ref[0]
    tok, width = BLOCK, chunk_refs[0].shape[1]
    for mask in range(slots):
        cols = col_block(low, mask, width)
        chunk_refs[mask][0:tok, :] = k_ref[:, cols]
        chunk_refs[mask][tok:, :] = v_ref[:, cols]


def query_kernel(slots, at_ref, q_ref, mine_ref, w_ref, other_ref, *refs):
    chunk_refs, grad_ref = refs[:slots], refs[slots]
    low, core = at_ref[0], at_ref[1]
    tok, half = mine_ref.shape
    width = chunk_refs[0].shape[1]
    first = pl.multiple_of(core * half, half)
    second = pl.multiple_of((1 - core) * half, half)
    total = mm(mine_ref[...], w_ref[pl.ds(first, half), :])
    total += mm(other_ref[...], w_ref[pl.ds(second, half), :])
    grad_ref[...] = total.astype(BF16)
    for mask in range(slots):
        cols = col_block(low, mask, width)
        chunk_refs[mask][0:tok, :] = q_ref[:, cols]
        chunk_refs[mask][tok:, :] = grad_ref[:, cols]


def coarse_kernel(slots, levels, *refs):
    in_refs, piece_refs = by_mask(refs[:slots], BACK), refs[slots:]
    tok = BLOCK
    for level, piece in zip(levels, piece_refs):
        rows = piece_rows(level)
        pool = level_pool(rows, level)
        for slab in range(slots):
            at = slab * rows
            keys = mm(pool, in_refs[slab][0:tok, :]) * (1.0 / (1 << level))
            piece[at : at + rows, :] = keys.astype(BF16)
            at = (slots + slab) * rows
            piece[at : at + rows, :] = mm(pool, in_refs[slab][tok:, :]).astype(BF16)


def attend_kernel(slots, far_levels, entries, *refs):
    key_refs = by_mask(refs[:slots], BACK)
    query_refs = by_mask(refs[slots : 2 * slots])
    refs = refs[2 * slots :]
    count = len(entries)
    got_refs, far_refs, refs = refs[:count], refs[count : 2 * count], refs[2 * count :]
    kl_ref, vl_ref, q_all, g_all, prob_ref, grad_ref, sum_ref = refs
    tok = BLOCK
    pairs = slots // 2
    inv_scale = 1.0 / math.sqrt(HDIM)
    to_exp2 = inv_scale * math.log2(math.e)
    near, far = 2 * tok, 3 * tok
    for slab in range(slots):
        pair, row = slab // 2, (slab % 2) * tok
        q_all[pair, row : row + tok, :] = query_refs[slab][0:tok, :]
        g_all[pair, row : row + tok, :] = query_refs[slab][tok:, :]
        kl_ref[pair, row : row + tok, :] = key_refs[slab][0:tok, :]
        vl_ref[pair, row : row + tok, :] = key_refs[slab][tok:, :]
    for (place, part, rows), got_ref in zip(entries, got_refs):
        for slab in range(slots):
            spot = far + place * BLOCK + 32 * slab + part * rows
            for kind, list_ref in enumerate((kl_ref, vl_ref)):
                at = (kind * slots + slab) * rows
                for pair in range(pairs):
                    list_ref[pair, spot : spot + rows, :] = got_ref[at : at + rows, :]
    pool = pool_matrix(BLOCK, 1)
    for pair in range(pairs):
        kl_ref[pair ^ 1, near:far, :] = (mm(pool, kl_ref[pair, 0:near, :]) * 0.5).astype(BF16)
        vl_ref[pair ^ 1, near:far, :] = mm(pool, vl_ref[pair, 0:near, :]).astype(BF16)

    def products(unit):
        pair, head = unit // 2, unit % 2
        lanes = slice(head * HDIM, head * HDIM + HDIM)
        scores = mm_cols(q_all[pair, :, lanes], kl_ref[pair, :, lanes])
        return scores, mm_cols(g_all[pair, :, lanes], vl_ref[pair, :, lanes])

    ready = products(0)
    for unit in range(slots):
        pair, head = unit // 2, unit % 2
        lanes = slice(head * HDIM, head * HDIM + HDIM)
        scores, prob_grad = ready
        if unit + 1 < slots:
            ready = products(unit + 1)
        top = jnp.max(scores, axis=1, keepdims=True)
        raised = jnp.exp2((scores - top) * to_exp2)
        inverse = 1.0 / jnp.sum(raised, axis=1, keepdims=True)
        centre = jnp.sum(raised * prob_grad, axis=1, keepdims=True) * inverse
        prob_ref[unit] = raised.astype(BF16)
        grad_ref[unit] = (raised * (prob_grad - centre)).astype(BF16)
        sum_ref[unit] = jnp.broadcast_to(inverse, (near, HDIM))
        queries = q_all[pair, :, lanes].astype(F32) * (inverse * inv_scale)
        q_all[pair, :, lanes] = queries.astype(BF16)
        g_all[pair, :, lanes] = (g_all[pair, :, lanes].astype(F32) * inverse).astype(BF16)
    for head in range(2):
        lanes = slice(head * HDIM, head * HDIM + HDIM)
        units = [2 * pair + head for pair in range(pairs)]
        for kind, (left_ref, right_ref) in enumerate(((grad_ref, q_all), (prob_ref, g_all))):
            left = jnp.concatenate([left_ref[unit, :, far:] for unit in units], axis=0)
            right = jnp.concatenate([right_ref[pair, :, lanes] for pair in range(pairs)], axis=0)
            total = mm_rows(left, right).astype(BF16)
            for (place, part, rows), out_ref in zip(entries, far_refs):
                for slab in range(slots):
                    start = place * BLOCK + 32 * slab + part * rows
                    at = (kind * slots + slab) * rows
                    out_ref[at : at + rows, lanes] = total[start : start + rows, :]


def reduce_kernel(slots, kl_ref, vl_ref, prob_ref, grad_ref, sum_ref, *home_refs):
    tok = BLOCK
    inv_scale = 1.0 / math.sqrt(HDIM)
    for pair in range(slots // 2):
        for head in range(2):
            lanes = slice(head * HDIM, head * HDIM + HDIM)
            unit = 2 * pair + head
            inverse = sum_ref[unit]
            attended = (mm(prob_ref[unit], vl_ref[pair, :, lanes]) * inverse).astype(BF16)
            query_grad = mm(grad_ref[unit], kl_ref[pair, :, lanes]) * (inverse * inv_scale)
            query_grad = query_grad.astype(BF16)
            for side in range(2):
                rows = slice(side * tok, side * tok + tok)
                home_refs[2 * pair + side][0:tok, lanes] = attended[rows]
                home_refs[2 * pair + side][tok:, lanes] = query_grad[rows]


def local_kernel(slots, q_all, g_all, prob_ref, grad_ref, dk_ref, dv_ref, ck_ref, cv_ref):
    tok = BLOCK
    pairs = slots // 2
    near, far = 2 * tok, 3 * tok
    for pair in range(pairs):
        for head in range(2):
            lanes = slice(head * HDIM, head * HDIM + HDIM)
            unit = 2 * pair + head
            key_terms = mm_rows(grad_ref[unit, :, 0:far], q_all[pair, :, lanes])
            value_terms = mm_rows(prob_ref[unit, :, 0:far], g_all[pair, :, lanes])
            for terms, local, level1 in (
                (key_terms, dk_ref, ck_ref),
                (value_terms, dv_ref, cv_ref),
            ):
                local[pair * near : pair * near + near, lanes] = terms[0:near]
                level1[pair ^ 1, :, lanes] = terms[near:].astype(BF16)
    pool = pool_matrix(BLOCK, 1)
    for pair in range(pairs):
        rows = slice(pair * near, pair * near + near)
        dk_ref[rows, :] += mm_rows(pool, ck_ref[pair]) * 0.5
        dv_ref[rows, :] += mm_rows(pool, cv_ref[pair])


def merge_kernel(slots, levels, dk_ref, dv_ref, *refs):
    far_refs, out_refs = refs[: len(levels)], refs[len(levels) :]
    tok = BLOCK
    key_pools, value_pools = [], []
    for level in levels:
        count = piece_rows(level)
        shape = (slots * count, slots * tok)
        row = lax.broadcasted_iota(jnp.int32, shape, 0)
        col = lax.broadcasted_iota(jnp.int32, shape, 1)
        slab = lax.shift_right_logical(col, tok.bit_length() - 1)
        held = slab * count + lax.shift_right_logical(col & (tok - 1), level)
        key_pools.append(jnp.where(held == row, 1.0 / (1 << level), 0.0).astype(BF16))
        value_pools.append(jnp.where(held == row, 1.0, 0.0).astype(BF16))
    halves = [ref.shape[0] // 2 for ref in far_refs]
    keys = jnp.concatenate([ref[:half, :] for ref, half in zip(far_refs, halves)], axis=0)
    values = jnp.concatenate([ref[half:, :] for ref, half in zip(far_refs, halves)], axis=0)
    key_sum = dk_ref[...] + mm_rows(jnp.concatenate(key_pools, axis=0), keys)
    value_sum = dv_ref[...] + mm_rows(jnp.concatenate(value_pools, axis=0), values)
    for slab in range(slots):
        rows = slice(slab * tok, slab * tok + tok)
        out_refs[slab][0:tok, :] = key_sum[rows].astype(BF16)
        out_refs[slab][tok:, :] = value_sum[rows].astype(BF16)


def flip_kernel(w_ref, out_ref):
    half = out_ref.shape[0]
    for place in range(w_ref.shape[0] // half):
        rows = slice(place * half, place * half + half)
        out_ref[:, rows] = w_ref[rows, :].T


def send_kernel(slots, at_ref, w_ref, *refs):
    in_refs, att_ref, send_refs = by_mask(refs[:slots], BACK), refs[slots], refs[slots + 1 :]
    low, core = at_ref[0], at_ref[1]
    tok, half = att_ref.shape
    width = in_refs[0].shape[1]
    for mask in range(slots):
        att_ref[:, col_block(low, mask, width)] = in_refs[mask][0:tok, :]
    part = half // len(send_refs)
    for place, send_ref in enumerate(send_refs):
        other = pl.multiple_of((1 - core) * half + place * part, part)
        send_ref[...] = mm(att_ref[...], w_ref[:, pl.ds(other, part)]).astype(BF16)


def keep_kernel(slots, at_ref, w_ref, att_ref, *refs):
    home_refs, (keep_ref, dq_ref) = by_mask(refs[:slots], BACK), refs[slots:]
    tok, half = att_ref.shape
    width = home_refs[0].shape[1]
    for mask in range(slots):
        dq_ref[:, col_block(at_ref[0], mask, width)] = home_refs[mask][tok:, :]
    first = pl.multiple_of(at_ref[1] * half, half)
    keep_ref[...] = mm(att_ref[...], w_ref[:, pl.ds(first, half)])


def add_kernel(keep_ref, *refs):
    got_refs, out_ref = refs[:-1], refs[-1]
    part = got_refs[0].shape[1]
    for place, got_ref in enumerate(got_refs):
        cols = slice(place * part, place * part + part)
        out_ref[:, cols] = (keep_ref[:, cols] + got_ref[...].astype(F32)).astype(BF16)


def finish_kernel(slots, at_ref, out_ref, dq_ref, *refs):
    last_refs, refs = by_mask(refs[:slots], BACK), refs[slots:]
    hbm_refs, (dk_ref, dv_ref, sems) = refs[:4], refs[4:]
    tok, width = BLOCK, last_refs[0].shape[1]
    copies = [
        pltpu.make_async_copy(source, hbm_refs[place], sems.at[place])
        for place, source in enumerate((out_ref, dq_ref, dk_ref, dv_ref))
    ]
    copies[0].start()
    copies[1].start()
    for place, held_ref in enumerate((dk_ref, dv_ref)):
        rows = slice(place * tok, place * tok + tok)
        for mask in range(slots):
            held_ref[:, col_block(at_ref[0], mask, width)] = last_refs[mask][rows, :]
        copies[2 + place].start()
    for copy in copies:
        copy.wait()


def straight(levels, slots):
    return all((slots << place) * 4 <= 32 for place in range(len(levels)))


def far_entries(levels, slots):
    entries, masks = [], []
    for place, level in enumerate(levels):
        if not straight(levels, slots):
            entries.append((place, 0, 32))
            continue
        for part in range(1 << place):
            entries.append((place, part, BLOCK >> level))
            masks.append(1 << level ^ part * slots)
    return entries, masks


def gather_far(pieces, levels, slots):
    width = pieces[0].shape[1]
    if straight(levels, slots):
        entries, masks = far_entries(levels, slots)
        return [swap_seq(pieces[entry[0]], mask) for entry, mask in zip(entries, masks)]
    held = {}
    for place, level in enumerate(levels):
        block = pieces[place].reshape(2 * slots, piece_rows(level), width)
        held[level] = block[:, None, : BLOCK >> level]
    found = []
    for step in levels:
        sent = [held[level].reshape(-1, width) for level in levels if level >= step]
        got = swap_seq(jnp.concatenate(sent, axis=0), 1 << step)
        first = 0
        for level in levels:
            if level < step:
                continue
            count = held[level].size // width
            part = got[first : first + count].reshape(held[level].shape)
            first += count
            if level == step:
                found.append(part.reshape(-1, width))
            else:
                held[level] = jnp.concatenate([held[level], part], axis=1)
    return found


def scatter_far(packed, levels, slots):
    width = packed[0].shape[1]
    if straight(levels, slots):
        entries, masks = far_entries(levels, slots)
        shares = [swap_seq(array, mask) for array, mask in zip(packed, masks)]
        return shares, [levels[entry[0]] for entry in entries]
    blocks = {}
    for place, level in enumerate(levels):
        rows = BLOCK >> level
        blocks[level] = packed[place].reshape(2 * slots, 32 // rows, rows, width)
    ready = {}
    for step in reversed(levels):
        sent, kept = [blocks[step].reshape(-1, width)], {}
        for level in levels:
            if level > step:
                size = ready[level].shape[1] // 2
                kept[level] = ready[level][:, :size]
                sent.append(ready[level][:, size:].astype(BF16).reshape(-1, width))
        got = swap_seq(jnp.concatenate(sent, axis=0), 1 << step)
        first = blocks[step].size // width
        ready[step] = got[0:first].reshape(blocks[step].shape)
        for level in kept:
            count = kept[level].size // width
            part = got[first : first + count].reshape(kept[level].shape)
            first += count
            ready[level] = kept[level].astype(F32) + part.astype(F32)
    shares = []
    for level in levels:
        share = ready[level].astype(BF16).reshape(2 * slots, -1, width)
        pad = piece_rows(level) - share.shape[1]
        if pad:
            share = jnp.pad(share, ((0, 0), (0, pad), (0, 0)))
        shares.append(share.reshape(-1, width))
    return shares, list(levels)


def on_device(queries, key_tokens, value_tokens, out_weight, output_grad):
    tok, columns = queries.shape
    heads = columns // HDIM
    slots = heads // 2
    width = columns // slots
    local_levels = slots.bit_length() - 1
    level_count = lax.axis_size("seq").bit_length() - 1
    far = list(range(local_levels, level_count))
    list_rows = 3 * tok + BLOCK * len(far)
    entries, _ = far_entries(far, slots)
    place = jnp.stack([lax.axis_index("seq") & (slots - 1), lax.axis_index("head")])
    place = place.astype(jnp.int32)

    def shape(dims, dtype=BF16):
        return jax.ShapeDtypeStruct(dims, dtype)

    def over(rows):
        return [shape((rows, width))] * slots

    def exchange(chunks, order=ORDER):
        moved = [chunks[0]] + [swap_seq(chunks[mask], mask) for mask in range(1, slots)]
        return [moved[mask] for mask in order]

    held = call(
        load_kernel,
        [shape((tok, columns))] * 2,
        [key_tokens, value_tokens],
        scratch=[pltpu.SemaphoreType.DMA((2,))],
        specs=[HBM] * 2,
        vmem=8,
    )
    chunks = call(
        lambda *refs: token_kernel(slots, *refs),
        over(2 * tok),
        [place] + list(held),
        flops=6 * 10**9,
        specs=[SMEM] + [VMEM] * 2,
        vmem=8,
    )
    keys = exchange(chunks, BACK)
    later, *_ = lax.optimization_barrier((place, *chunks))
    other_grad = swap_head(output_grad)
    chunks = call(
        lambda *refs: query_kernel(slots, *refs),
        over(2 * tok),
        [later, queries, output_grad, out_weight, other_grad],
        scratch=[pltpu.VMEM((tok, columns), BF16)],
        flops=6 * 10**9,
        specs=[SMEM] + [VMEM] * 4,
        vmem=16,
    )
    asked = exchange(chunks)
    flipped = call(
        flip_kernel,
        shape(out_weight.shape[::-1]),
        [out_weight],
        vmem=24,
        free=True,
    )
    sources, flipped, *_ = lax.optimization_barrier((keys, flipped, asked[1]))
    pieces = call(
        lambda *refs: coarse_kernel(slots, far, *refs),
        [shape((2 * slots * piece_rows(level), width)) for level in far],
        sources,
        vmem=8,
    )
    far_got = gather_far(pieces, far, slots)
    pairs = slots // 2
    made = call(
        lambda *refs: attend_kernel(slots, len(far), entries, *refs),
        [shape((2 * slots * rows, width)) for _, _, rows in entries]
        + [shape((pairs, list_rows, width))] * 2
        + [shape((pairs, 2 * tok, width))] * 2
        + [shape((slots, 2 * tok, list_rows))] * 2
        + [shape((slots, 2 * tok, HDIM), F32)],
        keys + asked + far_got,
        flops=6 * heads * tok * list_rows * HDIM,
    )
    shares, share_levels = scatter_far(made[: len(entries)], far, slots)
    key_list, value_list, asked, grads, probs, score_grads, sums = made[len(entries) :]
    made = call(
        lambda *refs: reduce_kernel(slots, *refs),
        over(2 * tok),
        [key_list, value_list, probs, score_grads, sums],
        flops=6 * 10**9,
        vmem=16,
    )
    key_sum, value_sum = call(
        lambda *refs: local_kernel(slots, *refs),
        [shape((slots * tok, width), F32)] * 2,
        [asked, grads, probs, score_grads],
        scratch=[pltpu.VMEM((pairs, BLOCK, width), BF16)] * 2,
        flops=4 * heads * tok * list_rows * HDIM,
        vmem=16,
    )
    made = list(made)
    late = BACK[-1]
    made[late], key_sum, *shares = lax.optimization_barrier((made[late], key_sum, *shares))
    home = exchange(made, BACK)
    chunks = call(
        lambda *refs: merge_kernel(slots, share_levels, *refs),
        over(2 * tok),
        [key_sum, value_sum] + shares,
        vmem=8,
    )
    home, _ = lax.optimization_barrier((home, chunks))
    chunks = list(chunks)
    last = exchange(chunks, BACK)
    wide = shape((tok, columns))
    attended, *send = call(
        lambda *refs: send_kernel(slots, *refs),
        [wide] + [shape((tok, columns))],
        [place, flipped] + home,
        flops=2 * tok * columns * columns,
        specs=[SMEM] + [VMEM] * (1 + slots),
        vmem=16,
    )
    got = [swap_head(part) for part in send]
    keep, query_grad = call(
        lambda *refs: keep_kernel(slots, *refs),
        [shape((tok, columns), F32), wide],
        [place, flipped, attended] + home,
        flops=4 * 10**9,
        specs=[SMEM] + [VMEM] * (2 + slots),
        vmem=16,
    )
    output = call(add_kernel, wide, [keep] + got, vmem=8)
    output, query_grad, key_grad, value_grad = call(
        lambda *refs: finish_kernel(slots, *refs),
        [wide] * 4,
        [place, output, query_grad] + last,
        scratch=[pltpu.VMEM((tok, columns), BF16)] * 2 + [pltpu.SemaphoreType.DMA((4,))],
        specs=[SMEM] + [VMEM] * (2 + slots),
        outs=HBM,
        vmem=8,
    )
    return output, query_grad, key_grad, value_grad


def solution(mesh):
    placed = P("seq", "head")
    return jax.shard_map(
        on_device,
        mesh=mesh,
        in_specs=(placed, placed, placed, P(None, "head"), placed),
        out_specs=(placed, placed, placed, placed),
        check_vma=False,
    )
```
